32 devices in a mesh: rows: 8 (over z, y), tp: 4 (over x, core).
Axes of the slice: x: 2, y: 2, z: 4, core: 2. Of those that a mesh axis runs over, the one named last changes fastest.
Arguments:
- patches: bfloat16 [80, 240, 512], P('rows'), may hold values from -6 to 6
- cotangent: bfloat16 [80, 240, 512], P('rows'), may hold values from -6 to 6
- page_bounds: int32 [8, 2], P('rows'), may hold values from 0 to 7, as said below
- attn_gain: bfloat16 [512], replicated, may hold values from 0.5 to 1.5
- attn_shift: bfloat16 [512], replicated, may hold values from -1.75 to 1.75
- qkv_weight: bfloat16 [3, 512, 512], P(None, None, 'tp'), may hold values from -0.25 to 0.25
- qv_bias: bfloat16 [2, 512], P(None, 'tp'), may hold values from -1.75 to 1.75
- pos_table: bfloat16 [361, 16], P(None, 'tp'), may hold values from -6 to 6
- proj_weight: bfloat16 [512, 512], P('tp'), may hold values from -1 to 1
- proj_bias: bfloat16 [512], replicated, may hold values from -1.75 to 1.75
- mlp_gain: bfloat16 [512], replicated, may hold values from 0.5 to 1.5
- mlp_shift: bfloat16 [512], replicated, may hold values from -1.75 to 1.75
- up_weight: bfloat16 [512, 2048], P(None, 'tp'), may hold values from -0.25 to 0.25
- up_bias: bfloat16 [2048], P('tp'), may hold values from -1.75 to 1.75
- down_weight: bfloat16 [2048, 512], P('tp'), may hold values from -0.1875 to 0.1875
- down_bias: bfloat16 [512], replicated, may hold values from -1.75 to 1.75
Outputs:
- block_out: bfloat16 [80, 240, 512], P('rows')
- grad_patches: bfloat16 [80, 240, 512], P('rows')
- grad_attn_gain: float32 [512], replicated
- grad_attn_shift: float32 [512], replicated
- grad_qkv: float32 [3, 512, 512], P(None, None, 'tp')
- grad_qv_bias: float32 [2, 512], P(None, 'tp')
- grad_pos_table: float32 [361, 16], P(None, 'tp')
- grad_proj: float32 [512, 512], P('tp')
- grad_proj_bias: float32 [512], replicated
- grad_mlp_gain: float32 [512], replicated
- grad_mlp_shift: float32 [512], replicated
- grad_up: float32 [512, 2048], P(None, 'tp')
- grad_up_bias: float32 [2048], P('tp')
- grad_down: float32 [2048, 512], P('tp')
- grad_down_bias: float32 [512], replicated
The draws below stay inside these ranges and needn't reach their ends.
Inputs may be any that keep to these rules, and one draw needn't show every extreme that they name: `page_bounds`: row w holds the first and the last window row of the page that contains w; the 5 pages are consecutive runs of window rows of random lengths covering all 8 rows.
All inputs are finite; a program needn't handle non-finite values.
Results may differ from the reference program's by a relative error of at most 0.012.
The reference program's roundings to bfloat16 on the way count: a program that leaves them out, or rounds other values in their place, can miss the bound.
Values may be sent and summed in bfloat16 or wider, within the bound.
No kernel may reach another device: no remote copies, remote signals or barrier semaphores. Data moves between devices by JAX's collectives and lax.ppermute only.
A program may use at most 128 MiB of HBM per device.

```python
import jax
import jax.numpy as jnp
from jax import lax

D = 512
HEADS = 16
HD = 32
FF = 2048
WIN = 10
NW = 24
NPAGES = 5
HH = 512
SHIFT = 5
PW = 240
TABLE = 361
WROWS = 8
H = 80


def draw_page_bounds(key, part):
    key = jax.random.fold_in(key, 11)
    cut_order = jax.random.permutation(key, WROWS - 1)
    starts = jnp.concatenate([jnp.ones((1,), jnp.int32), (cut_order < NPAGES - 1).astype(jnp.int32)])
    row_ids = jnp.arange(WROWS, dtype=jnp.int32)
    firsts = lax.cummax(jnp.where(starts > 0, row_ids, 0), axis=0)
    page_ends = jnp.concatenate([starts[1:], jnp.ones((1,), jnp.int32)])
    lasts = lax.cummin(jnp.where(page_ends > 0, row_ids, WROWS - 1), axis=0, reverse=True)
    return jnp.stack([firsts, lasts], axis=1).astype(jnp.int32)


def block_scale(rng, shape, cuts, least, largest):
    loudness = 1.0
    for position, shards_of in cuts:
        draws = jax.random.uniform(jax.random.fold_in(jax.random.fold_in(rng, 6), position), (shards_of,), jnp.float32, least / len(cuts), largest / len(cuts))
        loudness = loudness * jnp.repeat(jnp.exp(draws), shape[position] // shards_of).reshape((-1,) + (1,) * (len(shape) - 1 - position))
    return loudness


def scatter_about(stream_key, extent, scale, limit, split=(), kind=jnp.bfloat16):
    level = block_scale(stream_key, extent, split, -0.22, 0.18) if split else 1.0
    values = jax.random.normal(stream_key, extent, jnp.float32) * scale * level
    return jnp.minimum(jnp.maximum(values, -limit), limit).astype(kind)


def setup_inputs(seed: int = 0) -> dict:
    streams_of = jax.random.split(jax.random.key(seed), 17)
    return {
        "patches": scatter_about(streams_of[0], (H, PW, D), 1.0, 6.0, ((0, 8),)),
        "cotangent": scatter_about(streams_of[1], (H, PW, D), 1.0, 6.0, ((0, 8),)),
        "page_bounds": draw_page_bounds(jax.random.fold_in(streams_of[16], 71), 0),
        "attn_gain": jnp.clip(1.0 + 0.1 * jax.random.normal(streams_of[3], (D,), jnp.float32), 0.5, 1.5).astype(jnp.bfloat16),
        "attn_shift": scatter_about(streams_of[4], (D,), 0.3, 1.75),
        "qkv_weight": scatter_about(streams_of[5], (3, D, HH), D ** -0.5, 0.25, ((2, 4),)),
        "qv_bias": scatter_about(streams_of[6], (2, HH), 0.3, 1.75, ((1, 4),)),
        "pos_table": scatter_about(streams_of[7], (TABLE, HEADS), 1.0, 6.0, ((1, 4),)),
        "proj_weight": scatter_about(streams_of[8], (HH, D), (HH // 16) ** -0.5, 1.0, ((0, 4),)),
        "proj_bias": scatter_about(streams_of[9], (D,), 0.3, 1.75),
        "mlp_gain": jnp.clip(1.0 + 0.1 * jax.random.normal(streams_of[10], (D,), jnp.float32), 0.5, 1.5).astype(jnp.bfloat16),
        "mlp_shift": scatter_about(streams_of[11], (D,), 0.3, 1.75),
        "up_weight": scatter_about(streams_of[12], (D, FF), D ** -0.5, 0.25, ((1, 4),)),
        "up_bias": scatter_about(streams_of[13], (FF,), 0.3, 1.75, ((0, 4),)),
        "down_weight": scatter_about(streams_of[14], (FF, D), (FF // 2) ** -0.5, 0.1875, ((0, 4),)),
        "down_bias": scatter_about(streams_of[15], (D,), 0.3, 1.75),
    }


@jax.custom_vjp
def low(v):
    return lax.optimization_barrier(v.astype(jnp.bfloat16)).astype(jnp.float32)

@jax.custom_vjp
def low_back(v):
    return v

def low_keep(v):
    return (low(v), None)

def low_pass(kept, grad):
    return (grad,)

def back_keep(v):
    return (v, None)

def back_low(kept, grad):
    return (low(grad),)
low.defvjp(low_keep, low_pass)
low_back.defvjp(back_keep, back_low)
NORM_EPS = 1e-05
MASKED = -1000000000.0
FINEST = lax.Precision.HIGHEST

def norm_rows(values, gain, offset):
    center = values - lax.optimization_barrier(jnp.mean(values, axis=-1, keepdims=True))
    spread = lax.optimization_barrier(jnp.mean(center * center, axis=-1, keepdims=True))
    return center * lax.rsqrt(spread + NORM_EPS) * gain + offset

def to_windows(field):
    channels = field.shape[-1]
    field = field.reshape(WIN, NW, WIN, channels).transpose(1, 0, 2, 3)
    return field.reshape(NW, WIN * WIN, channels)

def from_windows(field):
    channels = field.shape[-1]
    field = field.reshape(NW, WIN, WIN, channels).transpose(1, 0, 2, 3)
    return field.reshape(WIN, PW, channels)

def split_heads(flat):
    return to_windows(flat.reshape(WIN, PW, HH)).reshape(NW, WIN * WIN, HEADS, HD)

def merge_heads(field):
    return from_windows(field.reshape(NW, WIN * WIN, HH)).reshape(WIN * PW, HH)

def position_index():
    cell_ids = jnp.arange(WIN * WIN, dtype=jnp.int32)
    row_of = cell_ids // WIN
    col_of = cell_ids % WIN
    return (row_of[:, None] - row_of[None, :] + WIN - 1) * (2 * WIN - 1) + (col_of[:, None] - col_of[None, :] + WIN - 1)

def region_ids(end_flag):
    row_ids = jnp.arange(WIN, dtype=jnp.int32)[:, None]
    col_ids = jnp.arange(PW, dtype=jnp.int32)[None, :]
    region = 2 * end_flag * (row_ids >= SHIFT).astype(jnp.int32) + (col_ids >= PW - SHIFT).astype(jnp.int32)
    return to_windows(region[:, :, None])[:, :, 0]

def row_block(strip, end_flag, weights):
    attn_gain, attn_shift, qkv_weight, qv_bias, pos_table, proj_weight, proj_bias, mlp_gain, mlp_shift, up_weight, up_bias, down_weight, down_bias = weights
    tokens = strip.reshape(WIN * PW, D)
    normed = low(norm_rows(tokens, attn_gain, attn_shift))
    queries = low(low_back(jnp.dot(normed, qkv_weight[0], precision=FINEST) + qv_bias[0]) * HD ** (-0.5))
    key_rows = low(low_back(jnp.dot(normed, qkv_weight[1], precision=FINEST)))
    value_rows = low(low_back(jnp.dot(normed, qkv_weight[2], precision=FINEST) + qv_bias[1]))
    q_win = split_heads(queries)
    k_win = split_heads(key_rows)
    v_win = split_heads(value_rows)
    rel_bias = jnp.take(pos_table, position_index(), axis=0).transpose(2, 0, 1)
    region = region_ids(end_flag)
    allowed = region[:, :, None] == region[:, None, :]
    scores = jnp.einsum('wqhd,wkhd->whqk', q_win, k_win, precision=FINEST) + rel_bias[None]
    scores = low_back(jnp.where(allowed[:, None], scores, MASKED))
    probs_soft = low(jax.nn.softmax(scores, axis=-1))
    attended = jnp.einsum('whqk,wkhd->wqhd', probs_soft, v_win, precision=FINEST)
    attended = low(low_back(merge_heads(attended)))
    branch = low_back(jnp.dot(attended, proj_weight, precision=FINEST))
    hidden = tokens + branch + proj_bias
    normed_two = low(norm_rows(hidden, mlp_gain, mlp_shift))
    inner = low_back(jnp.dot(normed_two, up_weight, precision=FINEST) + up_bias)
    activated = low(jax.nn.gelu(inner, approximate=False))
    result = hidden + jnp.dot(activated, down_weight, precision=FINEST) + down_bias
    return result.reshape(WIN, PW, D)

def source_rows(page_bounds):
    row_ids = jnp.arange(H, dtype=jnp.int32)
    window_row = row_ids // WIN
    offset = row_ids % WIN
    firsts = page_bounds[window_row, 0]
    lasts = page_bounds[window_row, 1]
    following = jnp.where(window_row == lasts, firsts, window_row + 1)
    return jnp.where(offset < SHIFT, row_ids + SHIFT, following * WIN + offset - SHIFT).astype(jnp.int32)

def reference(patches, cotangent, page_bounds, attn_gain, attn_shift, qkv_weight, qv_bias, pos_table, proj_weight, proj_bias, mlp_gain, mlp_shift, up_weight, up_bias, down_weight, down_bias):
    source = source_rows(page_bounds)
    page_ends = (page_bounds[:, 1] == jnp.arange(WROWS, dtype=jnp.int32)).astype(jnp.int32)
    params = tuple((item.astype(jnp.float32) for item in (attn_gain, attn_shift, qkv_weight, qv_bias, pos_table, proj_weight, proj_bias, mlp_gain, mlp_shift, up_weight, up_bias, down_weight, down_bias)))

    def forward(field, weights):
        shifted = jnp.roll(jnp.take(field, source, axis=0), -SHIFT, axis=1)
        strips = shifted.reshape(WROWS, WIN, PW, D)
        checked = jax.checkpoint(lambda strip, flag: row_block(strip, flag, weights))
        finished = lax.map(lambda pair_in: checked(pair_in[0], pair_in[1]), (strips, page_ends))
        finished = jnp.roll(finished.reshape(H, PW, D), SHIFT, axis=1)
        return jnp.zeros((H, PW, D), jnp.float32).at[source].set(finished)
    output, pullback = jax.vjp(forward, patches.astype(jnp.float32), params)
    grad_input, grads = pullback(cotangent.astype(jnp.float32))
    g_attn_gain, g_attn_shift, g_qkv, g_qv_bias, g_table, g_proj, g_proj_bias, g_mlp_gain, g_mlp_shift, g_up, g_up_bias, g_down, g_down_bias = grads
    return (output.astype(jnp.bfloat16), grad_input.astype(jnp.bfloat16), g_attn_gain, g_attn_shift, g_qkv, g_qv_bias, g_table, g_proj, g_proj_bias, g_mlp_gain, g_mlp_shift, g_up, g_up_bias, g_down, g_down_bias)
```

```python
import functools

import jax
import jax.numpy as jnp
import numpy as np
from jax import lax
from jax.experimental import pallas as pl
from jax.experimental.pallas import tpu as pltpu
from jax.sharding import PartitionSpec as P

D = 512
HD = 32
WIN = 10
SHIFT = 5
TABLE = 361
TABLE_PAD = 384
NORM_EPS = 1e-05
MASKED = -1000000000.0
HIDDEN_KEY = -1e30

TP = 4
HEADS_HERE = 4
LANES = 128
TOKENS = WIN * WIN
WROW = 112
SEG = 64
STRIP = SHIFT * SEG
COLBLK = 16
NBLK = 5
SLAB = SHIFT * NBLK * COLBLK
STACK = HEADS_HERE * WROW
VEC_ROW = 8
WEIGHT_ROWS = 3 * D + D

F32 = jnp.float32
BF = jnp.bfloat16
VMEM_LIMIT = 56 * 1024 * 1024


def dot(a, b):
    return lax.dot_general(a, b, (((1,), (0,)), ((), ())), preferred_element_type=F32)


def dot_nt(a, b):
    return lax.dot_general(a, b, (((1,), (1,)), ((), ())), preferred_element_type=F32)


def dot_tn(a, b):
    return lax.dot_general(a, b, (((0,), (0,)), ((), ())), preferred_element_type=F32)


def onehot(idx, width):
    lanes = lax.broadcasted_iota(jnp.int32, (idx.shape[0], width), 1)
    return jnp.where(idx == lanes, 1.0, 0.0).astype(BF)


def rows_of(nwl):
    return -(-(nwl * WROW + 16) // 64) * 64


@functools.lru_cache(None)
def index_tables(nwl):
    rows = rows_of(nwl)
    slab_w = NBLK * COLBLK
    strip = np.full((STRIP, 1), -1000, np.int32)
    out_up = np.full((STRIP, 1), -1000, np.int32)
    out_low = np.full((STRIP, 1), -1000, np.int32)
    win_up = np.full((rows, 1), -1000, np.int32)
    win_low = np.full((rows, 1), -1000, np.int32)
    for a in range(SHIFT):
        for cc in range(nwl * WIN):
            j, b = divmod(cc, WIN)
            strip[a * SEG + cc, 0] = a * slab_w + cc
            out_up[a * SEG + cc, 0] = j * WROW + a * WIN + b
            out_low[a * SEG + cc, 0] = j * WROW + (a + SHIFT) * WIN + b
            win_up[j * WROW + a * WIN + b, 0] = a * slab_w + cc
            win_low[j * WROW + (a + SHIFT) * WIN + b, 0] = a * SEG + cc
    return strip, win_up, win_low, out_up, out_low


@functools.lru_cache(None)
def attention_tables():
    pair = np.full((WROW, LANES), -1, np.int32)
    pad = np.zeros((WROW, LANES), np.float32)
    emask = np.zeros((WROW, LANES), np.float32)
    fmask = np.zeros((WROW, LANES), np.float32)
    i = np.arange(TOKENS)
    a, b = i // WIN, i % WIN
    pair[:TOKENS, :TOKENS] = (a[:, None] - a[None] + WIN - 1) * (2 * WIN - 1) + (
        b[:, None] - b[None] + WIN - 1
    )
    emask[:TOKENS, :TOKENS] = (a[:, None] >= SHIFT) != (a[None] >= SHIFT)
    fmask[:TOKENS, :TOKENS] = (b[:, None] >= SHIFT) != (b[None] >= SHIFT)
    pad[:, TOKENS:] = HIDDEN_KEY
    hot = (pair.reshape(1, -1) == np.arange(TABLE_PAD)[:, None]).astype(np.float32)
    return hot, pad, emask * MASKED, fmask * MASKED


def vspec():
    return pl.BlockSpec(memory_space=pltpu.VMEM)


def call(kernel, args, outs, scratch=(), scalars=None, name=None):
    in_specs = [vspec() for _ in args]
    operands = list(args)
    if scalars is not None:
        in_specs = [pl.BlockSpec(memory_space=pltpu.SMEM)] + in_specs
        operands = [scalars] + operands
    return pl.pallas_call(
        kernel,
        out_shape=[jax.ShapeDtypeStruct(s, d) for s, d in outs],
        in_specs=in_specs,
        out_specs=[vspec() for _ in outs],
        scratch_shapes=list(scratch),
        compiler_params=pltpu.CompilerParams(vmem_limit_bytes=VMEM_LIMIT),
        cost_estimate=pl.CostEstimate(flops=1024, bytes_accessed=1024, transcendentals=0),
        name=name,
    )(*operands)


def slab_of(blocks, scratch):
    for i, blk in enumerate(blocks):
        scratch[:, i * COLBLK : (i + 1) * COLBLK, :] = blk[...]
    return scratch[...].reshape(SLAB, D)


def take_kernel(picks, sc, *refs):
    scratch = refs[-1]
    n_out = len(picks)
    outs = refs[-1 - n_out : -1]
    idxs = refs[n_out * NBLK : n_out * NBLK + n_out]
    for k in range(n_out):
        slab = slab_of(refs[k * NBLK : (k + 1) * NBLK], scratch.at[k])
        outs[k][...] = dot(onehot(idxs[k][...] + sc[1], SLAB), slab).astype(BF)


def take_tokens(picks, scalars, name):
    def spec(field, half, i):
        across = field.shape[1] // COLBLK
        return pl.BlockSpec((SHIFT, COLBLK, D), lambda g, sc: (half, lax.rem(sc[0] + i, across), 0))

    sizes = [idx.shape[0] for _, idx, _ in picks]
    return pl.pallas_call(
        functools.partial(take_kernel, picks),
        grid_spec=pltpu.PrefetchScalarGridSpec(
            num_scalar_prefetch=1,
            grid=(1,),
            in_specs=[spec(f, h, i) for f, _, h in picks for i in range(NBLK)]
            + [pl.BlockSpec((n, 1), lambda g, sc: (0, 0)) for n in sizes],
            out_specs=[pl.BlockSpec((n, D), lambda g, sc: (0, 0)) for n in sizes],
            scratch_shapes=[pltpu.VMEM((len(picks), SHIFT, NBLK * COLBLK, D), BF)],
        ),
        out_shape=[jax.ShapeDtypeStruct((n, D), BF) for n in sizes],
        compiler_params=pltpu.CompilerParams(vmem_limit_bytes=VMEM_LIMIT),
        cost_estimate=pl.CostEstimate(flops=1024, bytes_accessed=1024, transcendentals=0),
        name=name,
    )(scalars, *[f for f, _, _ in picks for _ in range(NBLK)], *[idx for _, idx, _ in picks])


def norm_stats(x):
    mean = jnp.mean(x, axis=-1, keepdims=True)
    center = x - mean
    spread = jnp.mean(center * center, axis=-1, keepdims=True)
    inv = lax.rsqrt(spread + NORM_EPS)
    return center * inv, inv


def norm_back(dz, n, inv, gain):
    gz = dz * gain
    m1 = jnp.mean(gz, axis=-1, keepdims=True)
    m2 = jnp.mean(gz * n, axis=-1, keepdims=True)
    return (gz - m1 - n * m2) * inv


def row_chunks(rows, count):
    size = rows // count
    return [(c * size, size) for c in range(count)]


def head_masks():
    lane = lax.broadcasted_iota(jnp.int32, (1, LANES), 1)
    return [(lane >= h * HD) & (lane < (h + 1) * HD) for h in range(HEADS_HERE)]


def stacked(x, masks):
    return jnp.concatenate([jnp.where(m, x, jnp.zeros_like(x)) for m in masks], axis=0)


def unstacked(y, masks):
    total = jnp.where(masks[0], y[:WROW], 0.0)
    for h in range(1, HEADS_HERE):
        total = jnp.where(masks[h], y[h * WROW : (h + 1) * WROW], total)
    return total


def attn_fwd_kernel(nwl, sc, upx, recv, idx_low, norms, qvb, bias, em, fm, bp, *refs):
    wqkv, wproj = refs[:TP], refs[TP : 2 * TP]
    x_out, z1_out, qkv, probs, o_out, hs_out, z2_out, bias_sc = refs[2 * TP :]
    rows = x_out.shape[0]
    is_end = sc[3].astype(F32)
    last = sc[4].astype(F32)
    g1, b1, g2, b2 = (norms[i : i + 1, :] for i in range(4))
    for r0, n in row_chunks(rows, 4):
        x = upx[r0 : r0 + n, :].astype(F32) + dot(onehot(idx_low[r0 : r0 + n, :], STRIP), recv[...])
        x_out[r0 : r0 + n, :] = x.astype(BF)
        z, _ = norm_stats(x)
        z1_out[r0 : r0 + n, :] = (z * g1 + b1).astype(BF)
    scale = HD ** (-0.5)
    for s in range(TP):
        bqv = qvb[s]
        z1 = z1_out[...]
        q = dot(z1, wqkv[s][0])
        qkv[0, s] = ((q + bqv[0:1, :]) * scale).astype(BF)
        qkv[1, s] = dot(z1, wqkv[s][1]).astype(BF)
        v = dot(z1, wqkv[s][2])
        qkv[2, s] = (v + bqv[1:2, :]).astype(BF)
        e = em[...] * is_end
        bias_sc[s] = bias[s] + jnp.concatenate([e] * HEADS_HERE, axis=0)
    o_out[nwl * WROW :, :] = jnp.zeros((rows - nwl * WROW, D), BF)

    def window(j, carry):
        masks = head_masks()
        base = pl.multiple_of(j * WROW, 16)
        flag = jnp.where(j == nwl - 1, last, 0.0)
        fm4 = jnp.concatenate([fm[...] * flag] * HEADS_HERE, axis=0)
        for s in range(TP):
            q = qkv[0, s, pl.ds(base, WROW), :]
            k = qkv[1, s, pl.ds(base, LANES), :]
            v = qkv[2, s, pl.ds(base, LANES), :]
            sco = dot_nt(stacked(q, masks), k) + bias_sc[s] + fm4
            top = jnp.max(sco, axis=-1, keepdims=True)
            e = jnp.exp(sco - top)
            total = jnp.sum(e, axis=-1, keepdims=True)
            p = (e / total).astype(BF)
            probs[j * TP + s] = p
            o = unstacked(dot(p, v), masks)
            o_out[pl.ds(base, WROW), s * LANES : (s + 1) * LANES] = o.astype(BF)
        return carry

    lax.fori_loop(0, nwl, window, 0)
    for r0, n in row_chunks(rows, 2):
        acc = x_out[r0 : r0 + n, :].astype(F32) + bp[...]
        for s in range(TP):
            acc += dot(o_out[r0 : r0 + n, s * LANES : (s + 1) * LANES], wproj[s][...])
        hs_out[r0 : r0 + n, :] = acc
        z, _ = norm_stats(acc)
        z2_out[r0 : r0 + n, :] = (z * g2 + b2).astype(BF)


def mlp_kernel(shards, first, last, sc, *refs):
    refs = list(refs)
    ns = len(shards)
    ups, downs = refs[:ns], refs[ns : 2 * ns]
    z2, hs, ub, idx_low, idx_up_out, idx_low_out, norms, bd = refs[2 * ns : 2 * ns + 8]
    refs = refs[2 * ns + 8 :]
    if first:
        gup, grecv = refs[:2]
        refs = refs[2:]
    else:
        gs, acc_y_in, acc_z_in = refs[:3]
        refs = refs[3:]
    grads, dub = refs[:ns], refs[ns]
    refs = refs[ns + 1 :]
    if first:
        gs = refs[0]
        refs = refs[1:]
    if last:
        out_ul, dh_out, dhb_out, vec_out = refs[:4]
        refs = refs[4:]
    else:
        acc_y_out, acc_z_out = refs[:2]
        refs = refs[2:]
    acc_y, acc_z, act_sc, du_sc = refs
    rows = z2.shape[0]
    if first:
        for r0, n in row_chunks(rows, 4):
            gs[r0 : r0 + n, :] = (
                gup[r0 : r0 + n, :].astype(F32)
                + dot(onehot(idx_low[r0 : r0 + n, :], STRIP), grecv[...])
            ).astype(BF)
    for k, s in enumerate(shards):
        bu = ub[s]
        start = k == 0
        dub_total = jnp.zeros((1, D), F32)
        for r0, n in row_chunks(rows, 4):
            sl = slice(r0, r0 + n)
            u = dot(z2[sl, :], ups[k][...]) + bu
            phi = 0.5 * (1.0 + lax.erf(u * np.float32(np.sqrt(0.5))))
            act = (u * phi).astype(BF)
            slope = phi + u * (jnp.exp(-0.5 * u * u) * np.float32(1 / np.sqrt(2 * np.pi)))
            act_sc[sl, :] = act
            ga = dot_nt(gs[sl, :], downs[k][...])
            du = (slope * ga).astype(BF)
            du_sc[sl, :] = du
            dub_total += jnp.sum(du.astype(F32), axis=0, keepdims=True)
            y = dot(act, downs[k][...])
            z = dot_nt(du, ups[k][...])
            if start and first:
                acc_y[sl, :] = y
                acc_z[sl, :] = z
            elif start:
                acc_y[sl, :] = y + acc_y_in[sl, :]
                acc_z[sl, :] = z + acc_z_in[sl, :]
            else:
                acc_y[sl, :] += y
                acc_z[sl, :] += z
        dub[k : k + 1, :] = dub_total
        grads[k][:D, :] = dot_tn(act_sc[...], gs[...]).astype(BF)
        grads[k][D:, :] = dot_tn(z2[...], du_sc[...]).astype(BF)
    if not last:
        acc_y_out[...] = acc_y[...]
        acc_z_out[...] = acc_z[...]
        return
    g2 = norms[2:3, :]
    sums = [jnp.zeros((1, D), F32) for _ in range(4)]
    for r0, n in row_chunks(rows, 4):
        sl = slice(r0, r0 + n)
        h = hs[sl, :]
        dz = acc_z[sl, :]
        g = gs[sl, :].astype(F32)
        nrm, inv = norm_stats(h)
        dh = g + norm_back(dz, nrm, inv, g2)
        dh_out[sl, :] = dh
        dhb_out[sl, :] = dh.astype(BF)
        for i, term in enumerate((dz * nrm, dz, g, dh)):
            sums[i] = sums[i] + jnp.sum(term, axis=0, keepdims=True)
        act_sc[sl, :] = (h + acc_y[sl, :] + bd[...]).astype(BF)
    vec_out[...] = jnp.concatenate(sums, axis=0)
    y = act_sc[...]
    out_ul[:STRIP, :] = dot(onehot(idx_up_out[...], rows), y).astype(BF)
    out_ul[STRIP:, :] = dot(onehot(idx_low_out[...], rows), y).astype(BF)


def attn_bwd_kernel(shards, first, nwl, dhb, o, qkv, probs, z1, dub, vec, *refs):
    ns = len(shards)
    wproj, wqkv = refs[:ns], refs[ns : 2 * ns]
    refs = list(refs[2 * ns :])
    dz_in = None
    if not first:
        dz_in = refs.pop(0)
    packs = refs[:ns]
    dz, dsum, do_sc, dx_sc = refs[ns:]
    rows = dhb.shape[0]
    scale = HD ** (-0.5)
    for k, s in enumerate(shards):
        do_sc[k] = dot_nt(dhb[...], wproj[k][...]).astype(BF)
        gp = dot_tn(o[:, s * LANES : (s + 1) * LANES], dhb[...]).astype(BF)
        for c in range(D // LANES):
            packs[k][(3 * D + c * LANES) : (3 * D + (c + 1) * LANES), :] = gp[
                :, c * LANES : (c + 1) * LANES
            ]
        for m in range(3):
            dx_sc[k, m, nwl * WROW :, :] = jnp.zeros((rows - nwl * WROW, LANES), BF)
    dsum[...] = jnp.zeros(dsum.shape, F32)

    def window(j, carry):
        masks = head_masks()
        base = pl.multiple_of(j * WROW, 16)
        for k, s in enumerate(shards):
            q = stacked(qkv[0, s, pl.ds(base, WROW), :], masks)
            key = qkv[1, s, pl.ds(base, LANES), :]
            v = qkv[2, s, pl.ds(base, LANES), :]
            do = stacked(do_sc[k, pl.ds(base, WROW), :], masks)
            p = probs[j * TP + s]
            p32 = p.astype(F32)
            dp = dot_nt(do, v)
            pdp = p32 * dp
            ds = (pdp - p32 * jnp.sum(pdp, axis=-1, keepdims=True)).astype(BF)
            dsum[k] += ds.astype(F32)
            dv = dot_tn(p, do)
            dk = dot_tn(ds, q)
            dq = unstacked(dot(ds, key), masks) * scale
            dx_sc[k, 0, pl.ds(base, WROW), :] = dq.astype(BF)
            dx_sc[k, 1, pl.ds(base, WROW), :] = dk[:WROW].astype(BF)
            dx_sc[k, 2, pl.ds(base, WROW), :] = dv[:WROW].astype(BF)
        return carry

    lax.fori_loop(0, nwl, window, 0)
    for k, s in enumerate(shards):
        for m in range(3):
            packs[k][m * D : (m + 1) * D, :] = dot_tn(z1[...], dx_sc[k, m]).astype(BF)
        lines = [dub[s : s + 1, c * LANES : (c + 1) * LANES] for c in range(D // LANES)]
        lines += [jnp.sum(dx_sc[k, m].astype(F32), axis=0, keepdims=True) for m in (0, 2)]
        lines += [jnp.zeros((VEC_ROW - len(lines), LANES), F32)]
        lines += [
            vec[i : i + 1, c * LANES : (c + 1) * LANES]
            for i in range(vec.shape[0])
            for c in range(D // LANES)
        ]
        used = VEC_ROW + vec.shape[0] * (D // LANES)
        lines += [jnp.zeros((packs[k].shape[0] - WEIGHT_ROWS - used, LANES), F32)]
        packs[k][WEIGHT_ROWS:, :] = jnp.concatenate(lines, axis=0).astype(BF)
    for r0, n in row_chunks(rows, 2):
        total = None if first else dz_in[r0 : r0 + n, :]
        for k, s in enumerate(shards):
            for m in range(3):
                term = dot_nt(dx_sc[k, m, r0 : r0 + n, :], wqkv[k][m])
                total = term if total is None else total + term
        dz[r0 : r0 + n, :] = total


def final_kernel(x_ref, dz, dh, norms, idx_up_out, idx_low_out, out_ul, vec_out, sc_g):
    rows = x_ref.shape[0]
    sums = [jnp.zeros((1, D), F32) for _ in range(2)]
    for r0, n in row_chunks(rows, 4):
        sl = slice(r0, r0 + n)
        nrm, inv = norm_stats(x_ref[sl, :].astype(F32))
        d = dz[sl, :]
        sc_g[sl, :] = (dh[sl, :] + norm_back(d, nrm, inv, norms[0:1, :])).astype(BF)
        sums[0] = sums[0] + jnp.sum(d * nrm, axis=0, keepdims=True)
        sums[1] = sums[1] + jnp.sum(d, axis=0, keepdims=True)
    vec_out[...] = jnp.concatenate(sums, axis=0)
    out_ul[:STRIP, :] = dot(onehot(idx_up_out[...], rows), sc_g[...]).astype(BF)
    out_ul[STRIP:, :] = dot(onehot(idx_low_out[...], rows), sc_g[...]).astype(BF)


def page_kernel(sc, *refs):
    out = refs[TP]
    pw = out.shape[1]
    t = sc[2]
    width = pw // TP
    col = lax.broadcasted_iota(jnp.int32, (pw, 1), 0)
    hots = []
    for s in range(TP):
        v = col - width * jnp.bitwise_xor(t, s) - SHIFT
        v = jnp.where(v < 0, v + pw, v)
        v = jnp.where(v < width, v, -1000)
        hots.append(onehot(v, SEG))
    hot = jnp.concatenate(hots, axis=1)
    for r in range(WIN):
        off = STRIP + r * SEG if r < SHIFT else (r - SHIFT) * SEG
        parts = [ul[off : off + SEG, :] for ul in refs[:TP]]
        out[r] = dot(hot, jnp.concatenate(parts, axis=0)).astype(BF)


def swap_tp(x, bit):
    return lax.ppermute(x, "tp", [(i, i ^ bit) for i in range(TP)])


def shift_rows(x, distance):
    n = lax.axis_size("rows")
    return lax.ppermute(x, "rows", [(i, (i + distance) % n) for i in range(n)])


def stages_of(n):
    found, stride = [], 1
    sizes = [2] if n % 2 == 0 else []
    rest = n // 2 if sizes else n
    while rest > 1:
        size = 4 if rest % 4 == 0 else 2 if rest % 2 == 0 else rest
        sizes.append(size)
        rest //= size
    for size in sizes:
        found.append((stride, size))
        stride *= size
    return found


def digit_shift(x, stride, size, d):
    n = lax.axis_size("rows")
    route = []
    for i in range(n):
        digit = (i // stride) % size
        route.append((i, i + ((digit + d) % size - digit) * stride))
    return lax.ppermute(x, "rows", route)


def split_kernel(size, n_in, sc, *refs):
    ins, outs = refs[:n_in], refs[n_in:]
    part = outs[0].shape[0]
    for d in range(size):
        digit = lax.rem(sc[0] + d, size)
        sl = pl.ds(pl.multiple_of(digit * part, part), part)
        total = ins[0][sl, :].astype(F32)
        for r in ins[1:]:
            total += r[sl, :].astype(F32)
        outs[d][...] = total.astype(BF)


def add_and_split(arrays, digit, size, name):
    rows, cols = arrays[0].shape
    return call(
        functools.partial(split_kernel, size, len(arrays)),
        arrays,
        [((rows // size, cols), BF)] * size,
        scalars=jnp.reshape(digit, (1,)).astype(jnp.int32),
        name=name,
    )


def join_kernel(size, cuts, sc, *refs):
    ins, outs, whole = refs[:size], refs[size:-1], refs[-1]
    part = ins[0].shape[0]
    for d in range(size):
        digit = lax.rem(sc[0] + size - d, size)
        whole[pl.ds(pl.multiple_of(digit * part, part), part), :] = ins[d][...]
    if cuts is None:
        outs[0][...] = whole[...]
        return
    for out, pieces in zip(outs, cuts):
        for r0, n, c0, width in pieces:
            out[:, c0 : c0 + width] = whole[r0 : r0 + n, :].astype(F32)


def join(pieces, digit, cuts, name):
    rows, cols = pieces[0].shape
    size = len(pieces)
    if cuts is None:
        outs = [((rows * size, cols), BF)]
    else:
        outs = [((c[0][1], sum(p[3] for p in c)), F32) for c in cuts]
    return call(
        functools.partial(join_kernel, size, cuts),
        pieces,
        outs,
        scratch=[pltpu.VMEM((rows * size, cols), BF)],
        scalars=jnp.reshape(digit, (1,)).astype(jnp.int32),
        name=name,
    )


def sum_over_rows(arrays, cuts, name):
    n = lax.axis_size("rows")
    me = lax.axis_index("rows")
    stages = stages_of(n)
    for stride, size in stages:
        digit = (me // stride) % size
        pieces = add_and_split(arrays, digit, size, name + "_split")
        arrays = [pieces[0]] + [digit_shift(pieces[d], stride, size, d) for d in range(1, size)]
    total = arrays[0].astype(F32)
    for extra in arrays[1:]:
        total = total + extra.astype(F32)
    total = total.astype(BF)
    for i, (stride, size) in enumerate(reversed(stages)):
        digit = (me // stride) % size
        pieces = [total] + [digit_shift(total, stride, size, d) for d in range(1, size)]
        final = i == len(stages) - 1
        total = join(pieces, digit, cuts if final else None, name + "_join")
        if not final:
            total = total[0]
    return total


def sum_over_all(x):
    for bit in (1, 2):
        x = x + swap_tp(x, bit)
    for stride, size in stages_of(lax.axis_size("rows")):
        parts = [digit_shift(x, stride, size, d) for d in range(1, size)]
        for part in parts:
            x = x + part
    return x


def spread_output(out_ul, scalars, page_shape, name):
    lower = shift_rows(out_ul[STRIP:], 1)
    own = jnp.concatenate([out_ul[:STRIP], lower], axis=0)
    from_x = swap_tp(own, 2)
    from_c = swap_tp(own, 1)
    from_cx = swap_tp(from_x, 1)
    return call(
        page_kernel,
        [own, from_c, from_x, from_cx],
        [(page_shape, BF)],
        scalars=scalars,
        name=name,
    )[0]


def per_device(
    patches,
    cotangent,
    page_bounds,
    attn_gain,
    attn_shift,
    qkv_weight,
    qv_bias,
    pos_table,
    proj_weight,
    proj_bias,
    mlp_gain,
    mlp_shift,
    up_weight,
    up_bias,
    down_weight,
    down_bias,
):
    t = lax.axis_index("tp")
    w = lax.axis_index("rows")
    pw = patches.shape[1]
    nwl = pw // WIN // TP
    rows = rows_of(nwl)
    start = nwl * WIN * t + SHIFT
    is_end = (page_bounds[0, 1] == w).astype(jnp.int32)
    scalars = jnp.stack(
        [start // COLBLK, start % COLBLK, t, is_end, (t == TP - 1).astype(jnp.int32)]
    ).astype(jnp.int32)
    idx_strip, idx_win_up, idx_win_low, idx_out_up, idx_out_low = index_tables(nwl)
    hot_np, pad_np, em_np, fm_np = attention_tables()

    small = jnp.concatenate(
        [
            jnp.pad(pos_table.T, ((0, 0), (0, TABLE_PAD - TABLE))).reshape(-1, LANES),
            qv_bias,
            up_bias.reshape(-1, LANES),
        ]
    )
    pair = jnp.stack([small, swap_tp(small, 2)])
    smalls = jnp.concatenate([pair, swap_tp(pair, 1)])

    (strip_x,) = take_tokens([(patches, idx_strip, 0)], scalars, "strip_x")
    recv_x = shift_rows(strip_x, -1)

    def from_tp(x):
        over_x = swap_tp(x, 2)
        return [x, swap_tp(x, 1), over_x, swap_tp(over_x, 1)]

    wqkv = from_tp(qkv_weight)
    n_pos = HEADS_HERE * TABLE_PAD // LANES
    by_shard = jnp.array([0, 2, 1, 3])
    smalls = smalls[by_shard]
    pos_all = smalls[:, :n_pos].reshape(TP * HEADS_HERE, TABLE_PAD)
    qvb_all = smalls[:, n_pos : n_pos + 2]
    ub_all = smalls[:, n_pos + 2 :].reshape(TP, 1, -1)
    hot = jnp.asarray(hot_np, BF)
    bias = jnp.dot(pos_all, hot, preferred_element_type=F32)
    bias = bias.reshape(TP, HEADS_HERE, WROW, LANES) + pad_np
    bias = bias.reshape(TP, STACK, LANES)

    strip_g, up_x, up_g = take_tokens(
        [(cotangent, idx_strip, 0), (patches, idx_win_up, 1), (cotangent, idx_win_up, 1)],
        scalars,
        "take_rest",
    )
    recv_g = shift_rows(strip_g, -1)
    wproj = from_tp(proj_weight)
    wup = from_tp(up_weight)
    wdown = from_tp(down_weight)

    norms = jnp.stack([attn_gain, attn_shift, mlp_gain, mlp_shift]).astype(F32)
    bp = proj_bias.astype(F32)[None]
    bd = down_bias.astype(F32)[None]
    qvb_f = qvb_all.astype(F32)
    ub_f = ub_all.astype(F32)

    x_win, z1, qkv, probs, o, hs, z2 = call(
        functools.partial(attn_fwd_kernel, nwl),
        [up_x, recv_x, idx_win_low, norms, qvb_f, bias, em_np, fm_np, bp] + wqkv + wproj,
        [
            ((rows, D), BF),
            ((rows, D), BF),
            ((3, TP, rows, LANES), BF),
            ((nwl * TP, STACK, LANES), BF),
            ((rows, D), BF),
            ((rows, D), F32),
            ((rows, D), BF),
        ],
        scratch=[pltpu.VMEM((TP, STACK, LANES), F32)],
        scalars=scalars,
        name="attn_fwd",
    )

    def mlp(shards, first, last, extra):
        ns = len(shards)
        outs = [((2 * D, D), BF)] * ns + [((ns, D), F32)]
        if first:
            outs += [((rows, D), BF)]
        if last:
            outs += [((2 * STRIP, D), BF), ((rows, D), F32), ((rows, D), BF), ((4, D), F32)]
        else:
            outs += [((rows, D), F32)] * 2
        return call(
            functools.partial(mlp_kernel, shards, first, last),
            [wup[s] for s in shards]
            + [wdown[s] for s in shards]
            + [z2, hs, ub_f, idx_win_low, idx_out_up, idx_out_low, norms, bd]
            + extra,
            outs,
            scratch=[pltpu.VMEM((rows, D), F32)] * 2 + [pltpu.VMEM((rows, D), BF)] * 2,
            scalars=scalars,
                name="mlp_a" if first else "mlp_b",
        )

    g2, g3, dub_a, gs, acc_y, acc_z = mlp((2, 3), True, False, [up_g, recv_g])
    g0, g1, dub_b, out_ul, dh, dhb, vec_mlp = mlp((0, 1), False, True, [gs, acc_y, acc_z])

    got3 = swap_tp(g3, 1)
    across = (g2.astype(F32) + got3.astype(F32)).astype(BF)
    got_x = swap_tp(across, 2)
    got1 = swap_tp(g1, 1)
    grad_down, grad_up = sum_over_rows(
        [g0, got1, got_x], [[(0, D, 0, D)], [(D, D, 0, D)]], "mlp"
    )

    block_out = spread_output(out_ul, scalars, patches.shape, "page_y")
    dub = jnp.concatenate([dub_b, dub_a], axis=0)

    unit = 16 * lax.axis_size("rows")
    packed_rows = -(-(WEIGHT_ROWS + VEC_ROW + 4 * D // LANES) // unit) * unit

    def attn_bwd(shards, first, extra):
        ns = len(shards)
        outs = [((packed_rows, LANES), BF)] * ns
        outs += [((rows, D), F32), ((ns, STACK, LANES), F32)]
        return call(
            functools.partial(attn_bwd_kernel, shards, first, nwl),
            [dhb, o, qkv, probs, z1, dub, vec_mlp]
            + [wproj[s] for s in shards]
            + [wqkv[s] for s in shards]
            + extra,
            outs,
            scratch=[
                pltpu.VMEM((ns, rows, LANES), BF),
                pltpu.VMEM((ns, 3, rows, LANES), BF),
            ],
            name="attn_bwd_a" if first else "attn_bwd_b",
        )

    a2, a3, dz_a, dsum_a = attn_bwd((2, 3), True, [])
    a0, a1, dz, dsum_b = attn_bwd((0, 1), False, [dz_a])
    gota3 = swap_tp(a3, 1)
    across_a = (a2.astype(F32) + gota3.astype(F32)).astype(BF)
    gota_x = swap_tp(across_a, 2)
    gota1 = swap_tp(a1, 1)
    blocks = [(3 * D + c * LANES, LANES, c * LANES, LANES) for c in range(D // LANES)]
    grad_qkv, grad_proj, rest = sum_over_rows(
        [a0, gota1, gota_x],
        [[(0, 3 * D, 0, LANES)], blocks, [(WEIGHT_ROWS, packed_rows - WEIGHT_ROWS, 0, LANES)]],
        "attn",
    )

    out_g, vec_attn = call(
        final_kernel,
        [x_win, dz, dh, norms, idx_out_up, idx_out_low],
        [((2 * STRIP, D), BF), ((2, D), F32)],
        scratch=[pltpu.VMEM((rows, D), BF)],
        name="final",
    )
    grad_patches = spread_output(out_g, scalars, patches.shape, "page_g")

    flat = jnp.concatenate([dsum_b, dsum_a]).reshape(TP * HEADS_HERE, WROW * LANES)
    high = flat.astype(BF)
    low = (flat - high.astype(F32)).astype(BF)
    dpos = lax.dot_general(
        jnp.concatenate([high, low], axis=0),
        hot,
        (((1,), (1,)), ((), ())),
        preferred_element_type=F32,
    )
    dpos = dpos[: TP * HEADS_HERE] + dpos[TP * HEADS_HERE :]
    order = jnp.bitwise_xor(t, jnp.arange(TP))
    dpos = dpos.reshape(TP, -1, LANES)[order].reshape(-1, LANES)
    packed = sum_over_all(jnp.concatenate([vec_attn.reshape(-1, LANES), dpos]))
    n_vec = 2 * D // LANES
    vec_attn = packed[:n_vec].reshape(2, D)
    mine = lax.dynamic_index_in_dim(packed[n_vec:].reshape(TP, -1), t, 0, keepdims=False)
    grad_pos_table = mine.reshape(HEADS_HERE, TABLE_PAD)[:, :TABLE].T
    grad_up_bias = rest[: D // LANES].reshape(D)
    grad_qv_bias = rest[D // LANES : D // LANES + 2]
    vecs = rest[VEC_ROW : VEC_ROW + 4 * D // LANES].reshape(4, D)

    return (
        block_out,
        grad_patches,
        vec_attn[0],
        vec_attn[1],
        grad_qkv.reshape(3, D, LANES),
        grad_qv_bias,
        grad_pos_table,
        grad_proj,
        vecs[3],
        vecs[0],
        vecs[1],
        grad_up,
        grad_up_bias,
        grad_down,
        vecs[2],
    )


def solution(mesh):
    placed = (
        P("rows", None, None),
        P("rows", None, None),
        P("rows", None),
        P(),
        P(),
        P(None, None, "tp"),
        P(None, "tp"),
        P(None, "tp"),
        P("tp", None),
        P(),
        P(),
        P(),
        P(None, "tp"),
        P("tp"),
        P("tp", None),
        P(),
    )
    return jax.shard_map(
        per_device,
        mesh=mesh,
        in_specs=placed,
        out_specs=(
            P("rows", None, None),
            P("rows", None, None),
            P(),
            P(),
            P(None, None, "tp"),
            P(None, "tp"),
            P(None, "tp"),
            P("tp", None),
            P(),
            P(),
            P(),
            P(None, "tp"),
            P("tp"),
            P("tp", None),
            P(),
        ),
        check_vma=False,
    )
```

```python
import functools

import jax
import jax.numpy as jnp
import numpy as np
from jax import lax
from jax.experimental import pallas as pl
from jax.experimental.pallas import tpu as pltpu
from jax.sharding import PartitionSpec as P

D = 512
HD = 32
WIN = 10
SHIFT = 5
TABLE = 361
TABLE_PAD = 384
NORM_EPS = 1e-05
MASKED = -1000000000.0
HIDDEN_KEY = -1e30

TP = 4
HEADS_HERE = 4
LANES = 128
TOKENS = WIN * WIN
WROW = 112
SEG = 64
STRIP = SHIFT * SEG
COLBLK = 16
NBLK = 5
SLAB = SHIFT * NBLK * COLBLK
STACK = HEADS_HERE * WROW
SPAN = 2 * WIN - 1
REACH = SPAN * (WIN - 1) + WIN - 1
PACK1 = 4 * D + 32
SMALL_VECS = 6 * (D // LANES)
SMALL_SHARD = 24
PACK2 = 2 * D + 16

F32 = jnp.float32
BF = jnp.bfloat16
VMEM_LIMIT = 56 * 1024 * 1024
COST_RATE = 2e8


def dot(a, b):
    return lax.dot_general(a, b, (((1,), (0,)), ((), ())), preferred_element_type=F32)


def dot_nt(a, b):
    return lax.dot_general(a, b, (((1,), (1,)), ((), ())), preferred_element_type=F32)


def dot_tn(a, b):
    return lax.dot_general(a, b, (((0,), (0,)), ((), ())), preferred_element_type=F32)


def onehot(idx, width):
    lanes = lax.broadcasted_iota(jnp.int32, (idx.shape[0], width), 1)
    return jnp.where(idx == lanes, 1.0, 0.0).astype(BF)


def rows_of(nwl):
    return -(-(nwl * WROW + 16) // 64) * 64


@functools.lru_cache(None)
def index_tables(nwl):
    rows = rows_of(nwl)
    slab_w = NBLK * COLBLK
    strip = np.full((STRIP, 1), -1000, np.int32)
    out_up = np.full((STRIP, 1), -1000, np.int32)
    out_low = np.full((STRIP, 1), -1000, np.int32)
    win_up = np.full((rows, 1), -1000, np.int32)
    win_low = np.full((rows, 1), -1000, np.int32)
    for a in range(SHIFT):
        for cc in range(nwl * WIN):
            j, b = divmod(cc, WIN)
            strip[a * SEG + cc, 0] = a * slab_w + cc
            out_up[a * SEG + cc, 0] = j * WROW + a * WIN + b
            out_low[a * SEG + cc, 0] = j * WROW + (a + SHIFT) * WIN + b
            win_up[j * WROW + a * WIN + b, 0] = a * slab_w + cc
            win_low[j * WROW + (a + SHIFT) * WIN + b, 0] = a * SEG + cc
    return strip, win_up, win_low, out_up, out_low


@functools.lru_cache(None)
def attention_tables():
    emask = np.zeros((WROW, LANES), np.float32)
    fmask = np.zeros((WROW, LANES), np.float32)
    i = np.arange(TOKENS)
    a, b = i // WIN, i % WIN
    emask[:TOKENS, :TOKENS] = (a[:, None] >= SHIFT) != (a[None] >= SHIFT)
    fmask[:TOKENS, :TOKENS] = (b[:, None] >= SHIFT) != (b[None] >= SHIFT)
    spread = np.zeros((2 * LANES, LANES), np.float32)
    spread[SPAN * a + b, i] = 1.0
    back = np.zeros((LANES, TABLE_PAD), np.float32)
    back[i, REACH - (SPAN * a + b)] = 1.0
    groups = np.zeros((WIN * 8, STACK), np.float32)
    for h in range(HEADS_HERE):
        groups[a * 8 + h, h * WROW + i] = 1.0
    return emask * MASKED, fmask * MASKED, spread, back, groups


KERNEL_US = {
    "head": 3.0,
    "rest": 5.0,
    "attn_fwd": 14.0,
    "mlp_fwd_a": 8.0,
    "mlp_fwd_b": 8.0,
    "mlp_bwd_a": 8.0,
    "mlp_bwd_b": 9.0,
    "attn_bwd_13": 13.0,
    "attn_bwd_2": 9.0,
    "attn_bwd_0": 11.0,
    "page_y": 4.0,
    "page_g": 4.0,
}


def cost(name):
    return pl.CostEstimate(
        flops=int(KERNEL_US.get(name, 2.0) * COST_RATE), bytes_accessed=1024, transcendentals=0
    )


def vspec():
    return pl.BlockSpec(memory_space=pltpu.VMEM)


def after(x, *others):
    return lax.optimization_barrier((x, *others))[0]


def call(kernel, args, outs, scratch=(), scalars=(), name=None):
    return pl.pallas_call(
        kernel,
        out_shape=[jax.ShapeDtypeStruct(s, d) for s, d in outs],
        in_specs=[pl.BlockSpec(memory_space=pltpu.SMEM) for _ in scalars] + [vspec() for _ in args],
        out_specs=[vspec() for _ in outs],
        scratch_shapes=list(scratch),
        compiler_params=pltpu.CompilerParams(vmem_limit_bytes=VMEM_LIMIT),
        cost_estimate=cost(name),
        name=name,
    )(*scalars, *args)


def column_block(ref, start):
    main = (NBLK - 1) * COLBLK
    last = lax.rem(start + main, ref.shape[1])
    parts = [
        ref[:, pl.ds(pl.multiple_of(start, COLBLK), main), :],
        ref[:, pl.ds(pl.multiple_of(last, COLBLK), COLBLK), :],
    ]
    return jnp.concatenate(parts, axis=1).reshape(SLAB, D)


def first_column(width):
    c = lax.axis_index("tp") * width + SHIFT
    off = lax.rem(c, COLBLK)
    return c - off, off


def head_kernel(width, x_up, idx, wqkv, wproj, table, bias, strip, pack):
    start, off = first_column(width)
    strip[...] = dot(onehot(idx[...] + off, SLAB), column_block(x_up, start)).astype(BF)
    for m in range(3):
        pack[m * D : (m + 1) * D, :] = wqkv[m]
    for c in range(D // LANES):
        pack[3 * D + c * LANES : 3 * D + (c + 1) * LANES, :] = wproj[:, c * LANES : (c + 1) * LANES]
    row = lax.broadcasted_iota(jnp.int32, (TABLE, TABLE_PAD), 0)
    lane = lax.broadcasted_iota(jnp.int32, (TABLE, TABLE_PAD), 1)
    flip = jnp.where(row + lane == TABLE - 1, 1.0, 0.0).astype(BF)
    rev = dot(table[...], flip)
    lines = [rev[:, c * LANES : (c + 1) * LANES] for c in range(TABLE_PAD // LANES)]
    lines += [bias[...].astype(F32), jnp.zeros((PACK1 - 4 * D - 14, LANES), F32)]
    pack[4 * D :, :] = jnp.concatenate(lines, axis=0).astype(BF)


def half_spec(field, half):
    return pl.BlockSpec((SHIFT,) + field.shape[1:], lambda g: (half, 0, 0))


def whole_spec(a):
    return pl.BlockSpec(a.shape, lambda g: (0,) * a.ndim)


def windowed_call(kernel, args, specs, outs, name):
    return pl.pallas_call(
        kernel,
        grid=(1,),
        in_specs=specs,
        out_specs=[pl.BlockSpec(s, lambda g, n=len(s): (0,) * n) for s, _ in outs],
        out_shape=[jax.ShapeDtypeStruct(s, d) for s, d in outs],
        compiler_params=pltpu.CompilerParams(vmem_limit_bytes=VMEM_LIMIT),
        cost_estimate=cost(name),
        name=name,
    )(*args)


def rest_kernel(width, g_up, x_low, g_low, idx_strip, idx_win, up, down, ubias, strip_g, win_x, win_g, pack):
    start, off = first_column(width)
    strip_g[...] = dot(onehot(idx_strip[...] + off, SLAB), column_block(g_up, start)).astype(BF)
    hot = onehot(idx_win[...] + off, SLAB)
    win_x[...] = dot(hot, column_block(x_low, start)).astype(BF)
    win_g[...] = dot(hot, column_block(g_low, start)).astype(BF)
    pack[:D, :] = up[...]
    pack[D : 2 * D, :] = down[...]
    pack[2 * D :, :] = jnp.broadcast_to(ubias[...], (PACK2 - 2 * D, D))


def norm_stats(x):
    mean = jnp.mean(x, axis=-1, keepdims=True)
    center = x - mean
    spread = jnp.mean(center * center, axis=-1, keepdims=True)
    inv = lax.rsqrt(spread + NORM_EPS)
    return center * inv, inv


def norm_back(dz, n, inv, gain):
    gz = dz * gain
    m1 = jnp.mean(gz, axis=-1, keepdims=True)
    m2 = jnp.mean(gz * n, axis=-1, keepdims=True)
    return (gz - m1 - n * m2) * inv


def row_chunks(rows, count):
    size = rows // count
    return [(c * size, size) for c in range(count)]


def head_masks():
    lane = lax.broadcasted_iota(jnp.int32, (1, LANES), 1)
    return [(lane >= h * HD) & (lane < (h + 1) * HD) for h in range(HEADS_HERE)]


def stacked(x, masks):
    return jnp.concatenate([jnp.where(m, x, jnp.zeros_like(x)) for m in masks], axis=0)


def unstacked(y, masks):
    total = jnp.where(masks[0], y[:WROW], 0.0)
    for h in range(1, HEADS_HERE):
        total = jnp.where(masks[h], y[h * WROW : (h + 1) * WROW], total)
    return total


def attn_fwd_kernel(nwl, bounds, upx, recv, idx_low, vecs, em, fm, spread, *refs):
    packs = refs[:TP]
    refs = refs[TP:]
    qkv, probs, o_out = refs[:TP], refs[TP : 2 * TP], refs[2 * TP : 3 * TP]
    x_out, z1_out, hs_out, z2_out, bias_sc, roll_sc, row_sc, w_sc = refs[3 * TP :]
    rows = x_out.shape[0]
    is_end = jnp.where(bounds[0, 1] == lax.axis_index("rows"), 1.0, 0.0)
    last = jnp.where(lax.axis_index("tp") == TP - 1, 1.0, 0.0)
    g1, b1, g2, b2, bp = (vecs[i : i + 1, :] for i in range(5))

    table = jnp.concatenate(
        [
            jnp.concatenate(
                [packs[s][4 * D + 4 * c : 4 * D + 4 * c + 4, :].astype(F32) for c in range(TABLE_PAD // LANES)],
                axis=1,
            )
            for s in range(TP)
        ],
        axis=0,
    )
    for i in range(TOKENS):
        shift = TABLE_PAD - REACH + SPAN * (i // WIN) + i % WIN
        rolled = pltpu.roll(table, shift, 1)
        roll_sc[i * TP * HEADS_HERE : (i + 1) * TP * HEADS_HERE, :] = rolled[:, : 2 * LANES].astype(BF)
    n16 = TOKENS * TP * HEADS_HERE
    row_sc[:n16, :] = dot(roll_sc[...], spread[...])
    row_sc[n16:, :] = jnp.zeros((WROW * TP * HEADS_HERE - n16, LANES), F32)
    lane = lax.broadcasted_iota(jnp.int32, (WROW, LANES), 1)
    extra = em[...] * is_end + jnp.where(lane < TOKENS, 0.0, HIDDEN_KEY)
    for s in range(TP):
        for h in range(HEADS_HERE):
            rows_h = row_sc[pl.ds(s * HEADS_HERE + h, WROW, TP * HEADS_HERE), :]
            bias_sc[s, h * WROW : (h + 1) * WROW, :] = rows_h + extra

    for r0, n in row_chunks(rows, 4):
        x = upx[r0 : r0 + n, :].astype(F32) + dot(onehot(idx_low[r0 : r0 + n, :], STRIP), recv[...])
        x_out[r0 : r0 + n, :] = x.astype(BF)
        z, _ = norm_stats(x)
        z1_out[r0 : r0 + n, :] = (z * g1 + b1).astype(BF)
    scale = HD ** (-0.5)
    for m in range(3):
        for s in range(TP):
            w_sc[:, s * LANES : (s + 1) * LANES] = packs[s][m * D : (m + 1) * D, :]
        for r0, n in row_chunks(rows, 2):
            y = dot(z1_out[r0 : r0 + n, :], w_sc[...])
            for s in range(TP):
                part = y[:, s * LANES : (s + 1) * LANES]
                bq = packs[s][4 * D + 12 : 4 * D + 14, :].astype(F32)
                if m == 0:
                    part = (part + bq[0:1, :]) * scale
                if m == 2:
                    part = part + bq[1:2, :]
                qkv[s][m, r0 : r0 + n, :] = part.astype(BF)
    for s in range(TP):
        o_out[s][nwl * WROW :, :] = jnp.zeros((rows - nwl * WROW, LANES), BF)
        for c in range(D // LANES):
            w_sc[s * LANES : (s + 1) * LANES, c * LANES : (c + 1) * LANES] = packs[s][
                3 * D + c * LANES : 3 * D + (c + 1) * LANES, :
            ]

    def window(j, carry):
        masks = head_masks()
        base = pl.multiple_of(j * WROW, 16)
        flag = jnp.where(j == nwl - 1, last, 0.0)
        fm4 = jnp.concatenate([fm[...] * flag] * HEADS_HERE, axis=0)
        for s in range(TP):
            q = qkv[s][0, pl.ds(base, WROW), :]
            k = qkv[s][1, pl.ds(base, LANES), :]
            v = qkv[s][2, pl.ds(base, LANES), :]
            sco = dot_nt(stacked(q, masks), k) + bias_sc[s] + fm4
            top = jnp.max(sco, axis=-1, keepdims=True)
            e = jnp.exp(sco - top)
            total = jnp.sum(e, axis=-1, keepdims=True)
            p = (e / total).astype(BF)
            probs[s][j] = p
            o = unstacked(dot(p, v), masks)
            o_out[s][pl.ds(base, WROW), :] = o.astype(BF)
        return carry

    lax.fori_loop(0, nwl, window, 0)
    for r0, n in row_chunks(rows, 2):
        o = jnp.concatenate([o_out[s][r0 : r0 + n, :] for s in range(TP)], axis=1)
        acc = x_out[r0 : r0 + n, :].astype(F32) + bp + dot(o, w_sc[...])
        hs_out[r0 : r0 + n, :] = acc
        z, _ = norm_stats(acc)
        z2_out[r0 : r0 + n, :] = (z * g2 + b2).astype(BF)


def my_block(blocks):
    w = lax.axis_index("rows")
    mine = 0
    size = blocks
    while size > 1:
        size //= 2
        mine = mine * 2 + lax.rem(w, 2)
        w = lax.div(w, 2)
    return mine


def store_blocks(out, r0, value, blocks, cols=None):
    size = value.shape[0] // blocks
    mine = my_block(blocks)
    for b in range(blocks):
        at = pl.multiple_of(r0 + jnp.bitwise_xor(mine, b) * size, size)
        part = value[b * size : (b + 1) * size, :]
        if cols is None:
            out[pl.ds(at, size), :] = part
        else:
            out[pl.ds(at, size), cols[0] : cols[1]] = part


def mlp_fwd_kernel(shards, first, blocks, *refs):
    ns = len(shards)
    refs = list(refs)
    packs = refs[:ns]
    z2 = refs[ns]
    refs = refs[ns + 1 :]
    if first:
        gup, grecv, idx_low = refs[:3]
        refs = refs[3:]
    else:
        gs, acc_in, hs, idx_up_out, idx_low_out, vecs = refs[:6]
        refs = refs[6:]
    grads, slopes = refs[:ns], refs[ns : 2 * ns]
    refs = refs[2 * ns :]
    if first:
        gs, acc, act_sc = refs
    else:
        out_ul, acc, act_sc = refs
    rows = z2.shape[0]
    if first:
        for r0, n in row_chunks(rows, 4):
            gs[r0 : r0 + n, :] = (
                gup[r0 : r0 + n, :].astype(F32)
                + dot(onehot(idx_low[r0 : r0 + n, :], STRIP), grecv[...])
            ).astype(BF)
    for k in range(ns):
        ub = packs[k][2 * D : 2 * D + 1, :].astype(F32)
        for r0, n in row_chunks(rows, 4):
            sl = slice(r0, r0 + n)
            u = dot(z2[sl, :], packs[k][:D, :]) + ub
            phi = 0.5 * (1.0 + lax.erf(u * np.float32(np.sqrt(0.5))))
            act = (u * phi).astype(BF)
            slope = phi + u * (jnp.exp(-0.5 * u * u) * np.float32(1 / np.sqrt(2 * np.pi)))
            slopes[k][sl, :] = slope.astype(BF)
            act_sc[sl, :] = act
            y = dot(act, packs[k][D : 2 * D, :])
            if k > 0:
                acc[sl, :] += y
            elif first:
                acc[sl, :] = y
            else:
                acc[sl, :] = y + acc_in[sl, :]
        store_blocks(grads[k], 0, dot_tn(act_sc[...], gs[...]).astype(BF), blocks)
    if first:
        return
    bd = vecs[5:6, :]
    for r0, n in row_chunks(rows, 4):
        sl = slice(r0, r0 + n)
        act_sc[sl, :] = (hs[sl, :] + acc[sl, :] + bd).astype(BF)
    y = act_sc[...]
    out_ul[:STRIP, :] = dot(onehot(idx_up_out[...], rows), y).astype(BF)
    out_ul[STRIP:, :] = dot(onehot(idx_low_out[...], rows), y).astype(BF)


def mlp_bwd_kernel(order, first, blocks, *refs):
    refs = list(refs)
    packs = refs[:2]
    z2, gs, slopes = refs[2], refs[3], refs[4:6]
    refs = refs[6:]
    if not first:
        acc_in, hs, vecs = refs[:3]
        refs = refs[3:]
    grads, dub = refs[:2]
    refs = refs[2:]
    if first:
        acc, du_sc = refs
    else:
        dh_out, dhb_out, vec_out, acc, du_sc = refs
    rows = z2.shape[0]
    for k in range(2):
        dub_total = jnp.zeros((1, D), F32)
        for r0, n in row_chunks(rows, 4):
            sl = slice(r0, r0 + n)
            ga = dot_nt(gs[sl, :], packs[k][D : 2 * D, :])
            du = (slopes[k][sl, :].astype(F32) * ga).astype(BF)
            du_sc[sl, :] = du
            dub_total += jnp.sum(du.astype(F32), axis=0, keepdims=True)
            z = dot_nt(du, packs[k][:D, :])
            if k > 0:
                acc[sl, :] += z
            elif first:
                acc[sl, :] = z
            else:
                acc[sl, :] = z + acc_in[sl, :]
        for c in range(D // LANES):
            line = k * (D // LANES) + c
            dub[line : line + 1, :] = dub_total[:, c * LANES : (c + 1) * LANES]
        store_blocks(grads, k * D, dot_tn(z2[...], du_sc[...]).astype(BF), blocks)
    if first:
        return
    g2 = vecs[2:3, :]
    sums = [jnp.zeros((1, D), F32) for _ in range(4)]
    for r0, n in row_chunks(rows, 4):
        sl = slice(r0, r0 + n)
        dz = acc[sl, :]
        g = gs[sl, :].astype(F32)
        nrm, inv = norm_stats(hs[sl, :])
        dh = g + norm_back(dz, nrm, inv, g2)
        dh_out[sl, :] = dh
        dhb_out[sl, :] = dh.astype(BF)
        for i, term in enumerate((dz * nrm, dz, g, dh)):
            sums[i] = sums[i] + jnp.sum(term, axis=0, keepdims=True)
    for i in range(4):
        for c in range(D // LANES):
            line = i * (D // LANES) + c
            vec_out[line : line + 1, :] = sums[i][:, c * LANES : (c + 1) * LANES]


def attn_bwd_kernel(ns, first, last, nwl, blocks, dhb, z1, *refs):
    refs = list(refs)
    o, qkv, probs, packs = (refs[i * ns : (i + 1) * ns] for i in range(4))
    refs = refs[4 * ns :]
    back, groups = refs[:2]
    refs = refs[2:]
    dz_in = None if first else refs.pop(0)
    if last:
        x_ref, dh, vecs, idx_up_out, idx_low_out, vec_mlp, small13, small2, dub13, dub02 = refs[:10]
        refs = refs[10:]
    if last:
        grads, out_ul, small_out, dpos = refs[:4]
        refs = refs[4:]
    else:
        grads, dpos = refs[:2]
        refs = refs[2:]
    dz, dsum, do_sc, dx_sc = refs
    rows = dhb.shape[0]
    scale = HD ** (-0.5)
    for k in range(ns):
        total = None
        for c in range(D // LANES):
            w = packs[k][3 * D + c * LANES : 3 * D + (c + 1) * LANES, :]
            term = dot_nt(dhb[:, c * LANES : (c + 1) * LANES], w)
            total = term if total is None else total + term
        do_sc[k] = total.astype(BF)
        gp = dot_tn(o[k][...], dhb[...]).astype(BF)
        gp = jnp.concatenate([gp[:, c * LANES : (c + 1) * LANES] for c in range(D // LANES)], axis=0)
        store_blocks(grads, k * D, gp, blocks, (3 * LANES, 4 * LANES))
        dx_sc[k, nwl * WROW :, :] = jnp.zeros((rows - nwl * WROW, 3 * LANES), BF)
    dsum[...] = jnp.zeros(dsum.shape, F32)

    def window(j, carry):
        masks = head_masks()
        base = pl.multiple_of(j * WROW, 16)
        for k in range(ns):
            q = stacked(qkv[k][0, pl.ds(base, WROW), :], masks)
            key = qkv[k][1, pl.ds(base, LANES), :]
            v = qkv[k][2, pl.ds(base, LANES), :]
            do = stacked(do_sc[k, pl.ds(base, WROW), :], masks)
            p = probs[k][j]
            p32 = p.astype(F32)
            pdp = p32 * dot_nt(do, v)
            ds = (pdp - p32 * jnp.sum(pdp, axis=-1, keepdims=True)).astype(BF)
            dsum[k] += ds.astype(F32)
            dv = dot_tn(p, do)
            dk = dot_tn(ds, q)
            dq = unstacked(dot(ds, key), masks) * scale
            dx_sc[k, pl.ds(base, WROW), :LANES] = dq.astype(BF)
            dx_sc[k, pl.ds(base, WROW), LANES : 2 * LANES] = dk[:WROW].astype(BF)
            dx_sc[k, pl.ds(base, WROW), 2 * LANES :] = dv[:WROW].astype(BF)
        return carry

    lax.fori_loop(0, nwl, window, 0)
    for k in range(ns):
        store_blocks(grads, k * D, dot_tn(z1[...], dx_sc[k]).astype(BF), blocks, (0, 3 * LANES))
        high = dsum[k].astype(BF)
        low = (dsum[k] - high.astype(F32)).astype(BF)
        lanes = dot(high, back[...]) + dot(low, back[...])
        turned = jnp.concatenate(
            [
                pltpu.roll(lanes[h * WROW : (h + 1) * WROW, :], 0, 1, stride=1, stride_axis=0)
                for h in range(HEADS_HERE)
            ],
            axis=0,
        )
        high = turned.astype(BF)
        low = (turned - high.astype(F32)).astype(BF)
        summed = dot(groups[...], high) + dot(groups[...], low)
        total = summed[:8, :]
        for a in range(1, WIN):
            total = total + pltpu.roll(summed[a * 8 : (a + 1) * 8, :], (SPAN - WIN) * a, 1)
        per = 16
        for h in range(HEADS_HERE):
            for c in range(TABLE_PAD // LANES):
                line = k * per + h * (TABLE_PAD // LANES) + c
                dpos[line : line + 1, :] = total[h : h + 1, c * LANES : (c + 1) * LANES]
        for i, m in enumerate((0, 2)):
            part = dx_sc[k, :, m * LANES : (m + 1) * LANES].astype(F32)
            line = k * per + 12 + i
            dpos[line : line + 1, :] = jnp.sum(part, axis=0, keepdims=True)
        dpos[k * per + 14 : (k + 1) * per, :] = jnp.zeros((2, LANES), F32)
    sums = [jnp.zeros((1, D), F32) for _ in range(2)]
    for r0, n in row_chunks(rows, 4):
        sl = slice(r0, r0 + n)
        total = None if first else dz_in[sl, :]
        for k in range(ns):
            for m in range(3):
                term = dot_nt(
                    dx_sc[k, sl, m * LANES : (m + 1) * LANES], packs[k][m * D : (m + 1) * D, :]
                )
                total = term if total is None else total + term
        if not last:
            dz[sl, :] = total
            continue
        nrm, inv = norm_stats(x_ref[sl, :].astype(F32))
        dz[sl, :] = (dh[sl, :] + norm_back(total, nrm, inv, vecs[0:1, :])).astype(BF)
        sums[0] = sums[0] + jnp.sum(total * nrm, axis=0, keepdims=True)
        sums[1] = sums[1] + jnp.sum(total, axis=0, keepdims=True)
    if not last:
        return
    n_mlp = vec_mlp.shape[0]
    small_out[:n_mlp, :] = vec_mlp[...]
    for i in range(2):
        for c in range(D // LANES):
            line = n_mlp + i * (D // LANES) + c
            small_out[line : line + 1, :] = sums[i][:, c * LANES : (c + 1) * LANES]
    t = lax.axis_index("tp")
    pieces = [
        (dpos[...], dub02[:4, :]),
        (small13[:16, :], dub13[:4, :]),
        (small2[...], dub02[4:, :]),
        (small13[16:, :], dub13[4:, :]),
    ]
    for s, (lines, dub) in enumerate(pieces):
        at = pl.multiple_of(SMALL_VECS + jnp.bitwise_xor(t, s) * SMALL_SHARD, 8)
        both = jnp.concatenate([lines, dub, jnp.zeros((4, LANES), F32)], axis=0)
        small_out[pl.ds(at, SMALL_SHARD), :] = both
    out_ul[:STRIP, :] = dot(onehot(idx_up_out[...], rows), dz[...]).astype(BF)
    out_ul[STRIP:, :] = dot(onehot(idx_low_out[...], rows), dz[...]).astype(BF)


def page_kernel(*refs):
    out = refs[TP]
    pw = out.shape[1]
    t = lax.axis_index("tp")
    width = pw // TP
    col = lax.broadcasted_iota(jnp.int32, (pw, 1), 0)
    hots = []
    for s in range(TP):
        v = col - width * jnp.bitwise_xor(t, s) - SHIFT
        v = jnp.where(v < 0, v + pw, v)
        v = jnp.where(v < width, v, -1000)
        hots.append(onehot(v, SEG))
    hot = jnp.concatenate(hots, axis=1)
    for r in range(WIN):
        off = STRIP + r * SEG if r < SHIFT else (r - SHIFT) * SEG
        parts = [ul[off : off + SEG, :] for ul in refs[:TP]]
        out[r] = dot(hot, jnp.concatenate(parts, axis=0)).astype(BF)


def swap_tp(x, bit):
    return lax.ppermute(x, "tp", [(i, i ^ bit) for i in range(TP)])


def swap_rows(x, bit):
    return lax.ppermute(x, "rows", [(i, i ^ bit) for i in range(lax.axis_size("rows"))])


def shift_rows(x, distance):
    n = lax.axis_size("rows")
    return lax.ppermute(x, "rows", [(i, (i + distance) % n) for i in range(n)])


def row_bits():
    n = lax.axis_size("rows")
    bits = []
    while 1 << len(bits) < n:
        bits.append(1 << len(bits))
    return bits


def blocks_for(rows):
    blocks = 1
    while 2 * blocks <= lax.axis_size("rows") and rows % (2 * blocks) == 0 and rows // (2 * blocks) >= 16:
        blocks *= 2
    return blocks


def added(arrays):
    total = arrays[0].astype(F32)
    for extra in arrays[1:]:
        total = total + extra.astype(F32)
    return total.astype(BF)


def scatter_step(arrays, bit, blocks):
    total = added(arrays)
    if bit < blocks:
        half = total.shape[0] // 2
        return [total[:half], swap_rows(total[half:], bit)]
    return [total, swap_rows(total, bit)]


def gather_step(total, bit):
    return jnp.concatenate([total, swap_rows(total, bit)], axis=0)


def finish_kernel(blocks, n_in, *refs):
    ins, outs = refs[:n_in], refs[n_in:]
    part = ins[0].shape[0] * n_in // blocks
    each = blocks // n_in
    mine = my_block(blocks)
    both = len(outs) == 2
    half = part // 2
    for p in range(blocks):
        b = jnp.bitwise_xor(mine, p)
        piece = ins[p // each][(p % each) * part : (p % each + 1) * part, :].astype(F32)
        if both:
            at = pl.ds(pl.multiple_of(b * half, half), half)
            outs[0][at, :] = piece[:half]
            outs[1][at, :] = piece[half:]
        else:
            outs[2][pl.ds(pl.multiple_of(b * part, part), part), :] = piece
    if both:
        return
    qkv, proj, whole = outs
    for c in range(D // LANES):
        if c < 3:
            qkv[c] = whole[:, c * LANES : (c + 1) * LANES]
        proj[:, c * LANES : (c + 1) * LANES] = whole[c * LANES : (c + 1) * LANES, 3 * LANES :]


def finish(pieces, blocks, name):
    attn = name == "finish_attn"
    return call(
        functools.partial(finish_kernel, blocks, len(pieces)),
        pieces,
        [((3, D, LANES), F32), ((LANES, D), F32)] if attn else [((D, D), F32)] * 2,
        scratch=[pltpu.VMEM((D, D), F32)] if attn else [],
        name=name,
    )


def small_step(x, hop):
    axis, bit = hop
    return x + (swap_tp(x, bit) if axis == "tp" else swap_rows(x, bit))


def page(pieces, page_shape, name):
    return call(page_kernel, pieces, [(page_shape, BF)], name=name)[0]


def per_device(
    patches,
    cotangent,
    page_bounds,
    attn_gain,
    attn_shift,
    qkv_weight,
    qv_bias,
    pos_table,
    proj_weight,
    proj_bias,
    mlp_gain,
    mlp_shift,
    up_weight,
    up_bias,
    down_weight,
    down_bias,
):
    t = lax.axis_index("tp")
    pw = patches.shape[1]
    nwl = pw // WIN // TP
    width = nwl * WIN
    rows = rows_of(nwl)
    idx_strip, idx_win_up, idx_win_low, idx_out_up, idx_out_low = index_tables(nwl)
    em_np, fm_np, spread_np, back_np, groups_np = attention_tables()
    spread, back, groups = (jnp.asarray(a, BF) for a in (spread_np, back_np, groups_np))
    bits = row_bits()
    blocks = blocks_for(D)

    args = [patches, idx_strip, qkv_weight, proj_weight, pos_table.T, qv_bias]
    strip_x, pack1 = windowed_call(
        functools.partial(head_kernel, width),
        args,
        [half_spec(patches, 0)] + [whole_spec(a) for a in args[1:]],
        [((STRIP, D), BF), ((PACK1, LANES), BF)],
        "head",
    )
    recv_x = shift_rows(strip_x, -1)
    pack1_x = swap_tp(pack1, 2)
    pack1_c = swap_tp(pack1, 1)
    field_g = after(cotangent, strip_x)
    args = [field_g, patches, cotangent, idx_strip, idx_win_up, up_weight, down_weight, up_bias[None]]
    strip_g, up_x, up_g, pack2 = windowed_call(
        functools.partial(rest_kernel, width),
        args,
        [half_spec(cotangent, 0), half_spec(patches, 1), half_spec(cotangent, 1)]
        + [whole_spec(a) for a in args[3:]],
        [((STRIP, D), BF), ((rows, D), BF), ((rows, D), BF), ((PACK2, D), BF)],
        "rest",
    )
    recv_g = shift_rows(strip_g, -1)
    vecs = jnp.stack([attn_gain, attn_shift, mlp_gain, mlp_shift, proj_bias, down_bias]).astype(F32)
    pack1_cx = swap_tp(after(pack1_x, strip_g, recv_x), 1)
    packs1 = [pack1, pack1_c, pack1_x, pack1_cx]
    pack2 = after(pack2, pack1_x)
    pack2_x = swap_tp(pack2, 2)
    pack2_c = swap_tp(pack2, 1)

    outs = call(
        functools.partial(attn_fwd_kernel, nwl),
        [up_x, recv_x, idx_win_low, vecs, em_np, fm_np, spread] + packs1,
        [((3, rows, LANES), BF)] * TP
        + [((nwl, STACK, LANES), BF)] * TP
        + [((rows, LANES), BF)] * TP
        + [((rows, D), BF), ((rows, D), BF), ((rows, D), F32), ((rows, D), BF)],
        scratch=[
            pltpu.VMEM((TP, STACK, LANES), F32),
            pltpu.VMEM((TOKENS * TP * HEADS_HERE, 2 * LANES), BF),
            pltpu.VMEM((WROW * TP * HEADS_HERE, LANES), F32),
            pltpu.VMEM((D, D), BF),
        ],
        scalars=[page_bounds],
        name="attn_fwd",
    )
    qkv, probs, o = outs[:TP], outs[TP : 2 * TP], outs[2 * TP : 3 * TP]
    x_win, z1, hs, z2 = outs[3 * TP :]

    def mlp_fwd(shards, packs, first, extra):
        ns = len(shards)
        outs = [((D, D), BF)] * ns + [((rows, D), BF)] * ns
        outs += [((rows, D), BF), ((rows, D), F32)] if first else [((2 * STRIP, D), BF)]
        scratch = [pltpu.VMEM((rows, D), BF)]
        return call(
            functools.partial(mlp_fwd_kernel, shards, first, blocks),
            packs + [z2] + extra,
            outs,
            scratch=scratch if first else [pltpu.VMEM((rows, D), F32)] + scratch,
            name="mlp_fwd_a" if first else "mlp_fwd_b",
        )

    gd0, gd1, slope0, slope1, gs, acc_y = mlp_fwd(
        (0, 1), [pack2, pack2_c], True, [up_g, recv_g, idx_win_low]
    )
    got_d1 = swap_tp(gd1, 1)
    pack2_cx = swap_tp(after(pack2_x, acc_y), 1)
    packs2 = [pack2, pack2_c, pack2_x, pack2_cx]
    gd2, gd3, slope2, slope3, out_ul = mlp_fwd(
        (2, 3), packs2[2:], False, [gs, acc_y, hs, idx_out_up, idx_out_low, vecs]
    )
    got_d3 = swap_tp(gd3, 1)
    lower_y = shift_rows(out_ul[STRIP:], 1)
    slopes = [slope0, slope1, slope2, slope3]

    def mlp_bwd(shards, first, z2, extra):
        outs = [((2 * D, D), BF), ((2 * D // LANES, LANES), F32)]
        if first:
            outs += [((rows, D), F32)]
        else:
            outs += [((rows, D), F32), ((rows, D), BF), ((4 * D // LANES, LANES), F32)]
        scratch = [pltpu.VMEM((rows, D), BF)]
        return call(
            functools.partial(mlp_bwd_kernel, shards, first, blocks),
            [packs2[s] for s in shards] + [z2, gs] + [slopes[s] for s in shards] + extra,
            outs,
            scratch=scratch if first else [pltpu.VMEM((rows, D), F32)] + scratch,
            name="mlp_bwd_a" if first else "mlp_bwd_b",
        )

    gu13, dub13, acc_z = mlp_bwd((1, 3), True, z2, [])
    got_u13 = swap_tp(gu13, 1)
    across_d = added([gd2, got_d3])
    got_dx = swap_tp(across_d, 2)
    gu02, dub02, dh, dhb, vec_mlp = mlp_bwd((0, 2), False, after(z2, across_d), [acc_z, hs, vecs])
    across_u = added([gu02[D:], got_u13[D:]])
    got_ux = swap_tp(across_u, 2)

    def attn_bwd(shards, dhb, extra, last):
        ns = len(shards)
        outs = [((ns * D, D), BF)]
        if last:
            outs += [((2 * STRIP, D), BF), ((SMALL_VECS + TP * SMALL_SHARD, LANES), F32)]
        else:
            outs += [((ns * 16, LANES), F32)]
        scratch = [
            pltpu.VMEM((ns, STACK, LANES), F32),
            pltpu.VMEM((ns, rows, LANES), BF),
            pltpu.VMEM((ns, rows, 3 * LANES), BF),
        ]
        if last:
            scratch = [pltpu.VMEM((16, LANES), F32), pltpu.VMEM((rows, D), BF)] + scratch
        else:
            outs += [((rows, D), F32)]
        return call(
            functools.partial(attn_bwd_kernel, ns, not extra, last, nwl, blocks),
            [dhb, z1]
            + [a[s] for a in (o, qkv, probs, packs1) for s in shards]
            + [back, groups]
            + extra,
            outs,
            scratch=scratch,
            name="attn_bwd_" + "".join(map(str, shards)),
        )

    a13, small13, dz = attn_bwd((1, 3), after(dhb, across_u), [], False)
    got_a13 = swap_tp(a13, 1)
    page_own = jnp.concatenate([after(out_ul, a13)[:STRIP], lower_y], axis=0)
    from_x = swap_tp(page_own, 2)
    from_c = swap_tp(page_own, 1)
    down = scatter_step([gd0, got_d1, got_dx], bits[0], blocks)
    a2, small2, dz = attn_bwd((2,), after(dhb, down[0], page_own), [dz], False)
    across_a = added([a2, got_a13[D:]])
    got_ax = swap_tp(across_a, 2)
    up = scatter_step([gu02[:D], got_u13[:D], got_ux], bits[0], blocks)
    down = scatter_step(down, bits[1], blocks) if len(bits) > 1 else down
    a0, out_g, small = attn_bwd(
        (0,),
        after(dhb, across_a, up[0], down[0]),
        [dz, x_win, dh, vecs, idx_out_up, idx_out_low, vec_mlp, small13, small2, dub13, dub02],
        True,
    )

    lower_g = shift_rows(out_g[STRIP:], 1)
    attn = [a0, got_a13[:D], got_ax]
    small_bits = [("tp", 1), ("tp", 2)] + [("rows", bit) for bit in bits]
    pair = None
    for i, bit in enumerate(bits):
        attn[0] = added(attn)
        mark = attn[0]
        attn = scatter_step(attn[:1], bit, blocks)
        small = small_step(after(small, mark), small_bits.pop(0))
        if i + 1 < len(bits):
            up = scatter_step([after(up[0], mark)] + up[1:], bits[i + 1], blocks)
        if i + 2 < len(bits):
            down = scatter_step([after(down[0], mark)] + down[1:], bits[i + 2], blocks)
        if i == 0:
            from_cx = swap_tp(after(from_x, mark), 1)
        if i == 1:
            own_g = jnp.concatenate([out_g[:STRIP], after(lower_g, mark)], axis=0)
            g_x = swap_tp(own_g, 2)
            g_c = swap_tp(own_g, 1)
    down, up = after(added(down), mark), added(up)
    mlp = jnp.concatenate([down, up], axis=0)
    inner = [b for b in bits if b < blocks]
    mlp = gather_step(mlp, inner[-1])
    attn = added(attn)
    for i in reversed(range(1, len(inner))):
        small = small_step(after(small, attn), small_bits.pop(0)) if small_bits else small
        mlp_next = swap_rows(after(mlp, attn), inner[i - 1])
        attn = gather_step(attn, inner[i])
        if i > 1:
            mlp = jnp.concatenate([mlp, mlp_next], axis=0)
    while small_bits:
        small = small_step(small, small_bits.pop(0))
    g_cx = swap_tp(after(g_x, attn), 1)
    attn_next = swap_rows(attn, inner[0])
    block_out = page([page_own, from_c, from_x, from_cx], patches.shape, "page_y")
    grad_patches = page([own_g, g_c, g_x, g_cx], patches.shape, "page_g")
    grad_down, grad_up = finish([mlp, mlp_next], blocks, "finish_mlp")
    grad_qkv, grad_proj = finish([attn, attn_next], blocks, "finish_attn")

    v = small[:SMALL_VECS].reshape(6, D)
    mine = lax.dynamic_slice_in_dim(small, SMALL_VECS + t * SMALL_SHARD, SMALL_SHARD, 0)
    grad_pos_table = mine[:12].reshape(HEADS_HERE, TABLE_PAD)[:, :TABLE].T

    return (
        block_out,
        grad_patches,
        v[4],
        v[5],
        grad_qkv,
        mine[12:14],
        grad_pos_table,
        grad_proj,
        v[3],
        v[0],
        v[1],
        grad_up,
        mine[16:20].reshape(D),
        grad_down,
        v[2],
    )


def solution(mesh):
    placed = (
        P("rows", None, None),
        P("rows", None, None),
        P("rows", None),
        P(),
        P(),
        P(None, None, "tp"),
        P(None, "tp"),
        P(None, "tp"),
        P("tp", None),
        P(),
        P(),
        P(),
        P(None, "tp"),
        P("tp"),
        P("tp", None),
        P(),
    )
    return jax.shard_map(
        per_device,
        mesh=mesh,
        in_specs=placed,
        out_specs=(
            P("rows", None, None),
            P("rows", None, None),
            P(),
            P(),
            P(None, None, "tp"),
            P(None, "tp"),
            P(None, "tp"),
            P("tp", None),
            P(),
            P(),
            P(),
            P(None, "tp"),
            P("tp"),
            P("tp", None),
            P(),
        ),
        check_vma=False,
    )
```

```python
import functools

import jax
import jax.numpy as jnp
import numpy as np
from jax import lax
from jax.experimental import pallas as pl
from jax.experimental.pallas import tpu as pltpu
from jax.sharding import PartitionSpec as P

D = 512
HD = 32
WIN = 10
SHIFT = 5
TABLE = 361
TABLE_PAD = 384
NORM_EPS = 1e-05
MASKED = -1000000000.0
HIDDEN_KEY = -1e30

TP = 4
HEADS_HERE = 4
LANES = 128
TOKENS = WIN * WIN
WROW = 112
SEG = 64
STRIP = SHIFT * SEG
COLBLK = 16
NBLK = 5
SLAB = SHIFT * NBLK * COLBLK
STACK = HEADS_HERE * WROW
SPAN = 2 * WIN - 1
REACH = SPAN * (WIN - 1) + WIN - 1
PACK1 = 4 * D + 32
SMALL_SHARD = 24
SMALL_ROWS = 32
PACK2 = 2 * D + 16

F32 = jnp.float32
BF = jnp.bfloat16
VMEM_LIMIT = 24
VMEM_OF = {"head": 56, "rest": 56, "attn_fwd": 56}
COST_RATE = 2e8


def dot(a, b):
    return lax.dot_general(a, b, (((1,), (0,)), ((), ())), preferred_element_type=F32)


def dot_nt(a, b):
    return lax.dot_general(a, b, (((1,), (1,)), ((), ())), preferred_element_type=F32)


def dot_tn(a, b):
    return lax.dot_general(a, b, (((0,), (0,)), ((), ())), preferred_element_type=F32)


def onehot(idx, width):
    lanes = lax.broadcasted_iota(jnp.int32, (idx.shape[0], width), 1)
    return jnp.where(idx == lanes, 1.0, 0.0).astype(BF)


def rows_of(nwl):
    return -(-(nwl * WROW + 16) // 64) * 64


def tens(v):
    return sum((v >= WIN * m).astype(jnp.int32) for m in range(1, WIN))


def column(n):
    return lax.broadcasted_iota(jnp.int32, (n, 1), 0)


def lane_row(n):
    return lax.broadcasted_iota(jnp.int32, (1, n), 1)


def strip_places():
    d = column(STRIP)
    a = sum((d >= SEG * m).astype(jnp.int32) for m in range(1, SHIFT))
    return a, d - SEG * a


def window_places(rows, nwl):
    r = column(rows)
    j = sum((r >= WROW * m).astype(jnp.int32) for m in range(1, nwl + 1))
    return j, r - WROW * j


def strip_from_slab(nwl):
    a, c = strip_places()
    return jnp.where(c < nwl * WIN, a * (NBLK * COLBLK) + c, -1000)


def window_from(rows, nwl, low, row_width):
    j, i = window_places(rows, nwl)
    a = tens(i)
    found = (a - (SHIFT if low else 0)) * row_width + WIN * j + i - WIN * a
    first = TOKENS // 2 if low else 0
    ok = (i >= first) & (i < first + TOKENS // 2) & (j < nwl)
    return jnp.where(ok, found, -1000)


def strip_from_window(nwl, low):
    a, c = strip_places()
    j = tens(c)
    found = j * WROW + (a + (SHIFT if low else 0)) * WIN + c - WIN * j
    return jnp.where(c < nwl * WIN, found, -1000)


def pick_rows(places, source):
    return dot(onehot(places, source.shape[0]), source).astype(BF)


KERNEL_US = {
    "head": 3.0,
    "rest": 5.0,
    "attn_fwd": 14.0,
    "mlp_first": 9.0,
    "mlp_mid": 5.0,
    "mlp_last": 5.0,
    "attn_bwd_3": 7.0,
    "attn_bwd_2": 7.0,
    "attn_bwd_01": 11.0,
    "final": 1.0,
}


def cost(name):
    return pl.CostEstimate(
        flops=int(KERNEL_US.get(name, 0.01) * COST_RATE), bytes_accessed=1024, transcendentals=0
    )


def vspec():
    return pl.BlockSpec(memory_space=pltpu.VMEM)


def after(x, *others):
    return lax.optimization_barrier((x, *others))[0]


def call(kernel, args, outs, scratch=(), scalars=(), hbm=0, name=None):
    in_hbm = pl.BlockSpec(memory_space=pltpu.HBM)
    return pl.pallas_call(
        kernel,
        out_shape=[jax.ShapeDtypeStruct(s, d) for s, d in outs],
        in_specs=[pl.BlockSpec(memory_space=pltpu.SMEM) for _ in scalars]
        + [in_hbm if i < hbm else vspec() for i in range(len(args))],
        out_specs=[vspec() for _ in outs],
        scratch_shapes=list(scratch),
        compiler_params=pltpu.CompilerParams(vmem_limit_bytes=VMEM_OF.get(name, VMEM_LIMIT) * 2**20),
        cost_estimate=cost(name),
        name=name,
    )(*scalars, *[pltpu.with_memory_space_constraint(a, pltpu.HBM) for a in args[:hbm]], *args[hbm:])


def first_column(width):
    c = lax.axis_index("tp") * width + SHIFT
    off = lax.rem(c, COLBLK)
    return c - off, off


def slab_copies(field, half, start, slab, sems, k):
    main = (NBLK - 1) * COLBLK
    last = lax.rem(start + main, field.shape[1])
    rows = pl.ds(half * SHIFT, SHIFT)
    return [
        pltpu.make_async_copy(
            field.at[rows, pl.ds(pl.multiple_of(start, COLBLK), main), :],
            slab.at[:, :main, :],
            sems.at[k],
        ),
        pltpu.make_async_copy(
            field.at[rows, pl.ds(pl.multiple_of(last, COLBLK), COLBLK), :],
            slab.at[:, main:, :],
            sems.at[k + 1],
        ),
    ]


def head_kernel(width, x, wqkv, wproj, table, bias, strip, pack, slab, sems):
    start, off = first_column(width)
    rows = slab_copies(x, 0, start, slab, sems, 0)
    copies = [pltpu.make_async_copy(wqkv, pack.at[: 3 * D, :], sems.at[2])]
    for c in range(D // LANES):
        at = 3 * D + c * LANES
        copies.append(
            pltpu.make_async_copy(
                wproj.at[:, c * LANES : (c + 1) * LANES], pack.at[at : at + LANES, :], sems.at[3 + c]
            )
        )
    for copy in rows + copies:
        copy.start()
    row = lax.broadcasted_iota(jnp.int32, (TABLE, TABLE_PAD), 0)
    lane = lax.broadcasted_iota(jnp.int32, (TABLE, TABLE_PAD), 1)
    flip = jnp.where(row + lane == TABLE - 1, 1.0, 0.0).astype(BF)
    rev = dot(table[...], flip)
    lines = [rev[:, c * LANES : (c + 1) * LANES] for c in range(TABLE_PAD // LANES)]
    lines += [bias[...].astype(F32), jnp.zeros((PACK1 - 4 * D - 14, LANES), F32)]
    pack[4 * D :, :] = jnp.concatenate(lines, axis=0).astype(BF)
    hot = onehot(strip_from_slab(width // WIN) + off, SLAB)
    for copy in rows:
        copy.wait()
    strip[...] = dot(hot, slab[...].reshape(SLAB, D)).astype(BF)
    for copy in copies:
        copy.wait()


def rest_kernel(width, x, g, up, down, ubias, strip_g, win_x, win_g, pack, slabs, sems):
    start, off = first_column(width)
    rows = []
    for k, (field, half) in enumerate(((g, 0), (x, 1), (g, 1))):
        rows.append(slab_copies(field, half, start, slabs.at[k], sems, 2 * k))
    copies = [
        pltpu.make_async_copy(up, pack.at[:D, :], sems.at[6]),
        pltpu.make_async_copy(down, pack.at[D : 2 * D, :], sems.at[7]),
    ]
    for copy in sum(rows, []) + copies:
        copy.start()
    pack[2 * D :, :] = jnp.broadcast_to(ubias[...], (PACK2 - 2 * D, D))
    nwl = width // WIN
    wide = window_from(win_x.shape[0], nwl, False, NBLK * COLBLK)
    hots = [onehot(strip_from_slab(nwl) + off, SLAB), onehot(wide + off, SLAB)]
    for k, out in enumerate((strip_g, win_x, win_g)):
        for copy in rows[k]:
            copy.wait()
        out[...] = dot(hots[min(k, 1)], slabs[k].reshape(SLAB, D)).astype(BF)
    for copy in copies:
        copy.wait()


def norm_stats(x):
    mean = jnp.mean(x, axis=-1, keepdims=True)
    center = x - mean
    spread = jnp.mean(center * center, axis=-1, keepdims=True)
    inv = lax.rsqrt(spread + NORM_EPS)
    return center * inv, inv


def norm_back(dz, n, inv, gain):
    gz = dz * gain
    m1 = jnp.mean(gz, axis=-1, keepdims=True)
    m2 = jnp.mean(gz * n, axis=-1, keepdims=True)
    return (gz - m1 - n * m2) * inv


def row_chunks(rows, count):
    size = rows // count
    return [(c * size, size) for c in range(count)]


def head_masks():
    lane = lax.broadcasted_iota(jnp.int32, (1, LANES), 1)
    return [(lane >= h * HD) & (lane < (h + 1) * HD) for h in range(HEADS_HERE)]


def stacked(x, masks):
    return jnp.concatenate([jnp.where(m, x, jnp.zeros_like(x)) for m in masks], axis=0)


def unstacked(y, masks):
    total = jnp.where(masks[0], y[:WROW], 0.0)
    for h in range(1, HEADS_HERE):
        total = jnp.where(masks[h], y[h * WROW : (h + 1) * WROW], total)
    return total


def attn_fwd_kernel(nwl, bounds, *refs):
    packs, (upx, recv, vecs) = refs[:TP], refs[TP : TP + 3]
    refs = refs[TP + 3 :]
    qkv, probs, o_out = refs[:TP], refs[TP : 2 * TP], refs[2 * TP : 3 * TP]
    x_out, z1_out, hs_out, z2_out, bias_sc, roll_sc, row_sc, w_sc, small_sc, fm, sems = refs[3 * TP :]
    rows = x_out.shape[0]
    smalls, weights, projs = [], [], []
    for s in range(TP):
        lanes = slice(s * LANES, (s + 1) * LANES)
        smalls.append(
            pltpu.make_async_copy(packs[s].at[4 * D :, :], small_sc.at[s], sems.at[8 * s])
        )
        for m in range(3):
            weights.append(
                pltpu.make_async_copy(
                    packs[s].at[m * D : (m + 1) * D, :], w_sc.at[m, :, lanes], sems.at[8 * s + 1 + m]
                )
            )
        for c in range(D // LANES):
            projs.append(
                pltpu.make_async_copy(
                    packs[s].at[3 * D + c * LANES : 3 * D + (c + 1) * LANES, :],
                    w_sc.at[3, lanes, c * LANES : (c + 1) * LANES],
                    sems.at[8 * s + 4 + c],
                )
            )
    for copy in smalls + weights + projs:
        copy.start()
    is_end = jnp.where(bounds[0, 1] == lax.axis_index("rows"), 1.0, 0.0)
    last = jnp.where(lax.axis_index("tp") == TP - 1, 1.0, 0.0)
    g1, b1, g2, b2, bp = (vecs[i : i + 1, :] for i in range(5))

    for copy in smalls:
        copy.wait()
    table = jnp.concatenate(
        [
            jnp.concatenate(
                [small_sc[s, 4 * c : 4 * c + 4, :].astype(F32) for c in range(TABLE_PAD // LANES)],
                axis=1,
            )
            for s in range(TP)
        ],
        axis=0,
    )
    for i in range(TOKENS):
        shift = TABLE_PAD - REACH + SPAN * (i // WIN) + i % WIN
        rolled = pltpu.roll(table, shift, 1)
        roll_sc[i * TP * HEADS_HERE : (i + 1) * TP * HEADS_HERE, :] = rolled[:, : 2 * LANES].astype(BF)
    n16 = TOKENS * TP * HEADS_HERE
    lane = lane_row(LANES)
    at_lane = jnp.where(lane < TOKENS, lane + (SPAN - WIN) * tens(lane), -1000)
    spread = jnp.where(column(2 * LANES) == at_lane, 1.0, 0.0).astype(BF)
    row_sc[:n16, :] = dot(roll_sc[...], spread)
    row_sc[n16:, :] = jnp.zeros((WROW * TP * HEADS_HERE - n16, LANES), F32)
    row = column(WROW)
    real = (row < TOKENS) & (lane < TOKENS)
    low_differ = ((row >= TOKENS // 2) != (lane >= TOKENS // 2)) & real
    right_differ = ((row - WIN * tens(row) >= SHIFT) != (lane - WIN * tens(lane) >= SHIFT)) & real
    extra = jnp.where(lane < TOKENS, 0.0, HIDDEN_KEY) + jnp.where(low_differ, MASKED * is_end, 0.0)
    fm[...] = jnp.where(right_differ, MASKED * last, 0.0)
    for s in range(TP):
        for h in range(HEADS_HERE):
            rows_h = row_sc[pl.ds(s * HEADS_HERE + h, WROW, TP * HEADS_HERE), :]
            bias_sc[s, h * WROW : (h + 1) * WROW, :] = rows_h + extra

    places = window_from(rows, nwl, True, SEG)
    for r0, n in row_chunks(rows, 4):
        x = upx[r0 : r0 + n, :].astype(F32) + dot(onehot(places[r0 : r0 + n, :], STRIP), recv[...])
        x_out[r0 : r0 + n, :] = x.astype(BF)
        z, _ = norm_stats(x)
        z1_out[r0 : r0 + n, :] = (z * g1 + b1).astype(BF)
    scale = HD ** (-0.5)
    for copy in weights:
        copy.wait()
    for m in range(3):
        for r0, n in row_chunks(rows, 2):
            y = dot(z1_out[r0 : r0 + n, :], w_sc[m])
            for s in range(TP):
                part = y[:, s * LANES : (s + 1) * LANES]
                if m == 0:
                    part = (part + small_sc[s, 12:13, :].astype(F32)) * scale
                if m == 2:
                    part = part + small_sc[s, 13:14, :].astype(F32)
                qkv[s][m, r0 : r0 + n, :] = part.astype(BF)
    for s in range(TP):
        o_out[s][nwl * WROW :, :] = jnp.zeros((rows - nwl * WROW, LANES), BF)

    def window(j, carry):
        masks = head_masks()
        base = pl.multiple_of(j * WROW, 16)
        flag = jnp.where(j == nwl - 1, 1.0, 0.0)
        fm4 = jnp.concatenate([fm[...] * flag] * HEADS_HERE, axis=0)
        for s in range(TP):
            q = qkv[s][0, pl.ds(base, WROW), :]
            k = qkv[s][1, pl.ds(base, LANES), :]
            v = qkv[s][2, pl.ds(base, LANES), :]
            sco = dot_nt(stacked(q, masks), k) + bias_sc[s] + fm4
            top = jnp.max(sco, axis=-1, keepdims=True)
            e = jnp.exp(sco - top)
            total = jnp.sum(e, axis=-1, keepdims=True)
            p = (e / total).astype(BF)
            probs[s][j] = p
            o = unstacked(dot(p, v), masks)
            o_out[s][pl.ds(base, WROW), :] = o.astype(BF)
        return carry

    lax.fori_loop(0, nwl, window, 0)
    for copy in projs:
        copy.wait()
    for r0, n in row_chunks(rows, 2):
        o = jnp.concatenate([o_out[s][r0 : r0 + n, :] for s in range(TP)], axis=1)
        acc = x_out[r0 : r0 + n, :].astype(F32) + bp + dot(o, w_sc[3])
        hs_out[r0 : r0 + n, :] = acc
        z, _ = norm_stats(acc)
        z2_out[r0 : r0 + n, :] = (z * g2 + b2).astype(BF)


def my_block(blocks):
    w = lax.axis_index("rows")
    mine = 0
    size = blocks
    while size > 1:
        size //= 2
        mine = mine * 2 + lax.rem(w, 2)
        w = lax.div(w, 2)
    return mine


def store_blocks(out, r0, value, blocks, cols=None):
    size = value.shape[0] // blocks
    mine = my_block(blocks)
    for b in range(blocks):
        at = pl.multiple_of(r0 + jnp.bitwise_xor(mine, b) * size, size)
        part = value[b * size : (b + 1) * size, :]
        if cols is None:
            out[pl.ds(at, size), :] = part
        else:
            out[pl.ds(at, size), cols[0] : cols[1]] = part


def mlp_kernel(ns, first, last, nwl, blocks, *refs):
    refs = list(refs)
    packs = refs[:ns]
    if first:
        held, sems = refs[-1 - ns : -1], refs[-1]
        copies = loads(packs, held, sems)
        packs, refs = held, refs[: -1 - ns]
    z2 = refs[ns]
    refs = refs[ns + 1 :]
    if first:
        gup, grecv = refs[:2]
        refs = refs[2:]
    else:
        gs, y_in, z_in = refs[:3]
        refs = refs[3:]
    if last:
        hs, vecs = refs[:2]
        refs = refs[2:]
    grads, dub = refs[:ns], refs[ns]
    refs = refs[ns + 1 :]
    if first:
        gs = refs.pop(0)
    if last:
        out_up, out_low, dh_out, dhb_out, vec_out = refs[:5]
        refs = refs[5:]
    acc_y, acc_z, act_sc, du_sc = refs
    rows = z2.shape[0]
    if first:
        places = window_from(rows, nwl, True, SEG)
        for r0, n in row_chunks(rows, 4):
            gs[r0 : r0 + n, :] = (
                gup[r0 : r0 + n, :].astype(F32)
                + dot(onehot(places[r0 : r0 + n, :], STRIP), grecv[...])
            ).astype(BF)
    for k in range(ns):
        if first:
            copies[k].wait()
        ub = packs[k][2 * D : 2 * D + 1, :].astype(F32)
        dub_total = jnp.zeros((1, D), F32)
        for r0, n in row_chunks(rows, 2):
            sl = slice(r0, r0 + n)
            u = dot(z2[sl, :], packs[k][:D, :]) + ub
            phi = 0.5 * (1.0 + lax.erf(u * np.float32(np.sqrt(0.5))))
            act = (u * phi).astype(BF)
            slope = phi + u * (jnp.exp(-0.5 * u * u) * np.float32(1 / np.sqrt(2 * np.pi)))
            act_sc[sl, :] = act
            ga = dot_nt(gs[sl, :], packs[k][D : 2 * D, :])
            du = (slope * ga).astype(BF)
            du_sc[sl, :] = du
            dub_total += jnp.sum(du.astype(F32), axis=0, keepdims=True)
            y = dot(act, packs[k][D : 2 * D, :])
            z = dot_nt(du, packs[k][:D, :])
            if k > 0:
                acc_y[sl, :] += y
                acc_z[sl, :] += z
            elif first:
                acc_y[sl, :] = y
                acc_z[sl, :] = z
            else:
                acc_y[sl, :] = y + y_in[sl, :]
                acc_z[sl, :] = z + z_in[sl, :]
        for c in range(D // LANES):
            line = k * (D // LANES) + c
            dub[line : line + 1, :] = dub_total[:, c * LANES : (c + 1) * LANES]
        store_blocks(grads[k], 0, dot_tn(act_sc[...], gs[...]).astype(BF), blocks)
        store_blocks(grads[k], D, dot_tn(z2[...], du_sc[...]).astype(BF), blocks)
    if not last:
        return
    g2, bd = vecs[2:3, :], vecs[5:6, :]
    sums = [jnp.zeros((1, D), F32) for _ in range(4)]
    for r0, n in row_chunks(rows, 4):
        sl = slice(r0, r0 + n)
        dz = acc_z[sl, :]
        g = gs[sl, :].astype(F32)
        h = hs[sl, :]
        nrm, inv = norm_stats(h)
        dh = g + norm_back(dz, nrm, inv, g2)
        dh_out[sl, :] = dh
        dhb_out[sl, :] = dh.astype(BF)
        act_sc[sl, :] = (h + acc_y[sl, :] + bd).astype(BF)
        for i, term in enumerate((dz * nrm, dz, g, dh)):
            sums[i] = sums[i] + jnp.sum(term, axis=0, keepdims=True)
    vec_out[...] = jnp.concatenate(sums, axis=0)
    out_up[...] = pick_rows(strip_from_window(nwl, False), act_sc[...])
    out_low[...] = pick_rows(strip_from_window(nwl, True), act_sc[...])


def loads(sources, targets, sems, at=0):
    copies = [
        pltpu.make_async_copy(x, y, sems.at[at + i]) for i, (x, y) in enumerate(zip(sources, targets))
    ]
    for copy in copies:
        copy.start()
    return copies


def attn_bwd_kernel(ns, nwl, blocks, *refs):
    refs = list(refs)

    def take(n):
        found = refs[:n]
        del refs[:n]
        return found

    n_in = 4 * ns
    sources = take(n_in)
    dhb, z1 = take(2)
    grads = take(ns)
    dpos, *dx_sc = take(1 + ns)
    dsum, do_sc = take(2)
    held = take(n_in)
    (sems,) = refs
    copies = loads(sources, held, sems)
    packs, o, qkv, probs = (held[i * ns : (i + 1) * ns] for i in range(4))
    rows = dhb.shape[0]
    scale = HD ** (-0.5)
    masks = head_masks()
    lin = column(LANES)
    lin = jnp.where(lin < TOKENS, REACH - lin - (SPAN - WIN) * tens(lin), -1000)
    back = onehot(lin, TABLE_PAD)
    place = lane_row(STACK)
    head = sum((place >= WROW * m).astype(jnp.int32) for m in range(1, HEADS_HERE))
    place = place - WROW * head
    line = jnp.where(place < TOKENS, tens(place) * 8 + head, -1000)
    groups = jnp.where(column(WIN * 8) == line, 1.0, 0.0).astype(BF)
    for k in range(ns):
        copies[k].wait()
        total = None
        for c in range(D // LANES):
            w = packs[k][3 * D + c * LANES : 3 * D + (c + 1) * LANES, :]
            term = dot_nt(dhb[:, c * LANES : (c + 1) * LANES], w)
            total = term if total is None else total + term
        do_sc[k] = total.astype(BF)
        copies[ns + k].wait()
        gp = dot_tn(o[k][...], dhb[...]).astype(BF)
        gp = jnp.concatenate([gp[:, c * LANES : (c + 1) * LANES] for c in range(D // LANES)], axis=0)
        store_blocks(grads[k], 0, gp, blocks, (3 * LANES, 4 * LANES))
        dx_sc[k][nwl * WROW :, :] = jnp.zeros((rows - nwl * WROW, 3 * LANES), BF)
        dsum[k] = jnp.zeros(dsum.shape[1:], F32)
        copies[2 * ns + k].wait()
        copies[3 * ns + k].wait()

        def window(j, carry, k=k):
            base = pl.multiple_of(j * WROW, 16)
            q = stacked(qkv[k][0, pl.ds(base, WROW), :], masks)
            key = qkv[k][1, pl.ds(base, LANES), :]
            v = qkv[k][2, pl.ds(base, LANES), :]
            do = stacked(do_sc[k, pl.ds(base, WROW), :], masks)
            p = probs[k][j]
            p32 = p.astype(F32)
            pdp = p32 * dot_nt(do, v)
            ds = (pdp - p32 * jnp.sum(pdp, axis=-1, keepdims=True)).astype(BF)
            dsum[k] += ds.astype(F32)
            dv = dot_tn(p, do)
            dk = dot_tn(ds, q)
            dq = unstacked(dot(ds, key), masks) * scale
            dx_sc[k][pl.ds(base, WROW), :LANES] = dq.astype(BF)
            dx_sc[k][pl.ds(base, WROW), LANES : 2 * LANES] = dk[:WROW].astype(BF)
            dx_sc[k][pl.ds(base, WROW), 2 * LANES :] = dv[:WROW].astype(BF)
            return carry

        lax.fori_loop(0, nwl, window, 0)
    for k in range(ns):
        store_blocks(grads[k], 0, dot_tn(z1[...], dx_sc[k][...]).astype(BF), blocks, (0, 3 * LANES))
        high = dsum[k].astype(BF)
        low = (dsum[k] - high.astype(F32)).astype(BF)
        lanes = dot(high, back) + dot(low, back)
        turned = jnp.concatenate(
            [
                pltpu.roll(lanes[h * WROW : (h + 1) * WROW, :], 0, 1, stride=1, stride_axis=0)
                for h in range(HEADS_HERE)
            ],
            axis=0,
        )
        high = turned.astype(BF)
        low = (turned - high.astype(F32)).astype(BF)
        summed = dot(groups, high) + dot(groups, low)
        total = summed[:8, :]
        for a in range(1, WIN):
            total = total + pltpu.roll(summed[a * 8 : (a + 1) * 8, :], (SPAN - WIN) * a, 1)
        per = 16
        for h in range(HEADS_HERE):
            for c in range(TABLE_PAD // LANES):
                line = k * per + h * (TABLE_PAD // LANES) + c
                dpos[line : line + 1, :] = total[h : h + 1, c * LANES : (c + 1) * LANES]
        for i, m in enumerate((0, 2)):
            part = dx_sc[k][:, m * LANES : (m + 1) * LANES].astype(F32)
            line = k * per + 12 + i
            dpos[line : line + 1, :] = jnp.sum(part, axis=0, keepdims=True)
        dpos[k * per + 14 : (k + 1) * per, :] = jnp.zeros((2, LANES), F32)


def final_kernel(nwl, *refs):
    refs = list(refs)
    sources, refs = refs[: 2 * TP + 2], refs[2 * TP + 2 :]
    vecs, vec_mlp, small3, small2, small01, dub01, dub2, dub3 = refs[:8]
    out_up, out_low, small_out, small_f32, dz = refs[8:13]
    held, sems = refs[13:-1], refs[-1]
    copies = loads(sources, held, sems)
    x_ref, dh = held[2 * TP :]
    rows = x_ref.shape[0]
    for copy in copies:
        copy.wait()
    parts = list(zip(held[:TP], held[TP : 2 * TP]))
    weights = [
        jnp.concatenate([pack[m * D : (m + 1) * D, :] for m in range(3)], axis=1) for _, pack in parts
    ]
    sums = [jnp.zeros((1, D), F32) for _ in range(2)]
    for r0, n in row_chunks(rows, 4):
        sl = slice(r0, r0 + n)
        total = None
        for (dx, _), weight in zip(parts, weights):
            term = dot_nt(dx[sl, :], weight)
            total = term if total is None else total + term
        nrm, inv = norm_stats(x_ref[sl, :].astype(F32))
        dz[sl, :] = (dh[sl, :] + norm_back(total, nrm, inv, vecs[0:1, :])).astype(BF)
        sums[0] = sums[0] + jnp.sum(total * nrm, axis=0, keepdims=True)
        sums[1] = sums[1] + jnp.sum(total, axis=0, keepdims=True)
    t = lax.axis_index("tp")
    pieces = [
        (small01[:16, :], dub01[:4, :]),
        (small01[16:, :], dub01[4:, :]),
        (small2[...], dub2[...]),
        (small3[...], dub3[...]),
    ]
    for s, (lines, dub) in enumerate(pieces):
        at = pl.multiple_of(jnp.bitwise_xor(t, s) * LANES, LANES)
        both = jnp.concatenate([lines, dub, jnp.zeros((4, LANES), F32)], axis=0)
        small_f32[: SMALL_SHARD, pl.ds(at, LANES)] = both
    small_f32[SMALL_SHARD:, :] = jnp.concatenate(
        [vec_mlp[...]] + sums + [jnp.zeros((SMALL_ROWS - SMALL_SHARD - 6, D), F32)], axis=0
    )
    small_out[...] = small_f32[...].astype(BF)
    out_up[...] = pick_rows(strip_from_window(nwl, False), dz[...])
    out_low[...] = pick_rows(strip_from_window(nwl, True), dz[...])


def page_kernel(*refs):
    out = refs[TP]
    pw = out.shape[1]
    t = lax.axis_index("tp")
    width = pw // TP
    col = lax.broadcasted_iota(jnp.int32, (pw, 1), 0)
    hots = []
    for s in range(TP):
        v = col - width * jnp.bitwise_xor(t, s) - SHIFT
        v = jnp.where(v < 0, v + pw, v)
        v = jnp.where(v < width, v, -1000)
        hots.append(onehot(v, SEG))
    hot = jnp.concatenate(hots, axis=1)
    for r in range(WIN):
        off = STRIP + r * SEG if r < SHIFT else (r - SHIFT) * SEG
        parts = [ul[off : off + SEG, :] for ul in refs[:TP]]
        out[r] = dot(hot, jnp.concatenate(parts, axis=0)).astype(BF)


def swap_tp(x, bit):
    return lax.ppermute(x, "tp", [(i, i ^ bit) for i in range(TP)])


def swap_rows(x, bit):
    return lax.ppermute(x, "rows", [(i, i ^ bit) for i in range(lax.axis_size("rows"))])


def shift_rows(x, distance):
    n = lax.axis_size("rows")
    return lax.ppermute(x, "rows", [(i, (i + distance) % n) for i in range(n)])


def row_bits():
    n = lax.axis_size("rows")
    bits = []
    while 1 << len(bits) < n:
        bits.append(1 << len(bits))
    return bits


def blocks_for(rows):
    blocks = 1
    while 2 * blocks <= lax.axis_size("rows") and rows % (2 * blocks) == 0 and rows // (2 * blocks) >= 16:
        blocks *= 2
    return blocks


def added(arrays):
    total = arrays[0].astype(F32)
    for extra in arrays[1:]:
        total = total + extra.astype(F32)
    return total.astype(BF)


def scatter_step(arrays, bit, blocks):
    total = added(arrays)
    if bit < blocks:
        half = total.shape[0] // 2
        return [total[:half], swap_rows(total[half:], bit)]
    return [total, swap_rows(total, bit)]


def finish_kernel(blocks, order, n_in, *refs):
    ins, outs = refs[:n_in], refs[n_in:]
    part = ins[0].shape[0] * n_in // blocks
    each = blocks // n_in
    mine = my_block(blocks)
    both = len(outs) == 2
    half = part // 2
    for p in range(blocks):
        b = jnp.bitwise_xor(mine, sum(((p >> k) & 1) << to for k, to in enumerate(order)))
        piece = ins[p // each][(p % each) * part : (p % each + 1) * part, :].astype(F32)
        if both:
            at = pl.ds(pl.multiple_of(b * half, half), half)
            outs[0][at, :] = piece[:half]
            outs[1][at, :] = piece[half:]
        else:
            outs[2][pl.ds(pl.multiple_of(b * part, part), part), :] = piece
    if both:
        return
    qkv, proj, whole = outs
    for c in range(D // LANES):
        if c < 3:
            qkv[c] = whole[:, c * LANES : (c + 1) * LANES]
        proj[:, c * LANES : (c + 1) * LANES] = whole[c * LANES : (c + 1) * LANES, 3 * LANES :]


def finish(pieces, blocks, gathered, name):
    attn = name == "finish_attn"
    order = [len(gathered) - bit.bit_length() for bit in gathered]
    return call(
        functools.partial(finish_kernel, blocks, order, len(pieces)),
        pieces,
        [((3, D, LANES), F32), ((LANES, D), F32)] if attn else [((D, D), F32)] * 2,
        scratch=[pltpu.VMEM((D, D), F32)] if attn else [],
        name=name,
    )


def interleaved(parts, blocks):
    n = blocks
    cut = [p.reshape(n, 1, p.shape[0] // n, p.shape[1]) for p in parts]
    return jnp.concatenate(cut, axis=1).reshape(-1, parts[0].shape[1])


def riding_step(arrays, small, bit, blocks):
    total = added(arrays)
    small = added(small)
    half = total.shape[0] // 2 if bit < blocks else total.shape[0]
    got = swap_rows(jnp.concatenate([total[-half:], small], axis=0), bit)
    return [total[:half], got[:half]], [small, got[half:]]


def small_kernel(*refs):
    ins, vecs, shard = refs[:TP], refs[TP : TP + 6], refs[TP + 6]
    total = ins[0][...].astype(F32)
    for r in ins[1:]:
        total += r[...].astype(F32)
    for i in range(6):
        vecs[i][...] = total[SMALL_SHARD + i : SMALL_SHARD + i + 1, :]
    t = lax.axis_index("tp")
    mine = jnp.zeros(shard.shape, F32)
    for a in range(TP):
        mine = jnp.where(t == a, total[:SMALL_SHARD, a * LANES : (a + 1) * LANES], mine)
    shard[...] = mine


def page(pieces, page_shape, name):
    return call(page_kernel, pieces, [(page_shape, BF)], name=name)[0]


def per_device(
    patches,
    cotangent,
    page_bounds,
    attn_gain,
    attn_shift,
    qkv_weight,
    qv_bias,
    pos_table,
    proj_weight,
    proj_bias,
    mlp_gain,
    mlp_shift,
    up_weight,
    up_bias,
    down_weight,
    down_bias,
):
    t = lax.axis_index("tp")
    pw = patches.shape[1]
    nwl = pw // WIN // TP
    width = nwl * WIN
    rows = rows_of(nwl)
    bits = row_bits()
    blocks = blocks_for(D)

    slab = (SHIFT, NBLK * COLBLK, D)
    strip_x, pack1 = call(
        functools.partial(head_kernel, width),
        [patches, qkv_weight.reshape(3 * D, LANES), proj_weight, pos_table.T, qv_bias],
        [((STRIP, D), BF), ((PACK1, LANES), BF)],
        scratch=[
            pltpu.VMEM(slab, BF),
            pltpu.SemaphoreType.DMA((7,)),
        ],
        hbm=3,
        name="head",
    )
    recv_x = shift_rows(strip_x, -1)
    pack1_x = swap_tp(pack1, 2)
    pack1_c = swap_tp(pack1, 1)
    strip_g, up_x, up_g, pack2 = call(
        functools.partial(rest_kernel, width),
        [patches, after(cotangent, strip_x), up_weight, down_weight, up_bias[None]],
        [((STRIP, D), BF), ((rows, D), BF), ((rows, D), BF), ((PACK2, D), BF)],
        scratch=[
            pltpu.VMEM((3,) + slab, BF),
            pltpu.SemaphoreType.DMA((8,)),
        ],
        hbm=4,
        name="rest",
    )
    recv_g = shift_rows(strip_g, -1)
    vecs = jnp.stack([attn_gain, attn_shift, mlp_gain, mlp_shift, proj_bias, down_bias]).astype(F32)
    pack1_cx = swap_tp(after(pack1_x, strip_g, recv_x), 1)
    packs1 = [pack1, pack1_c, pack1_x, pack1_cx]
    pack2 = after(pack2, pack1_cx)
    pack2_x = swap_tp(pack2, 2)
    pack2_c = swap_tp(pack2, 1)

    outs = call(
        functools.partial(attn_fwd_kernel, nwl),
        packs1 + [up_x, recv_x, vecs],
        [((3, rows, LANES), BF)] * TP
        + [((nwl, STACK, LANES), BF)] * TP
        + [((rows, LANES), BF)] * TP
        + [((rows, D), BF), ((rows, D), BF), ((rows, D), F32), ((rows, D), BF)],
        scratch=[
            pltpu.VMEM((TP, STACK, LANES), F32),
            pltpu.VMEM((TOKENS * TP * HEADS_HERE, 2 * LANES), BF),
            pltpu.VMEM((WROW * TP * HEADS_HERE, LANES), F32),
            pltpu.VMEM((4, D, D), BF),
            pltpu.VMEM((TP, PACK1 - 4 * D, LANES), BF),
            pltpu.VMEM((WROW, LANES), F32),
            pltpu.SemaphoreType.DMA((8 * TP,)),
        ],
        scalars=[page_bounds],
        hbm=TP,
        name="attn_fwd",
    )
    qkv, probs, o = outs[:TP], outs[TP : 2 * TP], outs[2 * TP : 3 * TP]
    x_win, z1, hs, z2 = outs[3 * TP :]

    def mlp(packs, extra, first, last):
        ns = len(packs)
        outs = [((2 * D, D), BF)] * ns + [((ns * D // LANES, LANES), F32)]
        if first:
            outs += [((rows, D), BF)]
        if last:
            outs += [((STRIP, D), BF)] * 2 + [((rows, D), F32), ((rows, D), BF), ((4, D), F32)]
        accs = [((rows, D), F32)] * 2
        return call(
            functools.partial(mlp_kernel, ns, first, last, nwl, blocks),
            packs + [z2] + extra,
            outs if last else outs + accs,
            scratch=([pltpu.VMEM(*a) for a in accs] if last else [])
            + [pltpu.VMEM((rows, D), BF)] * 2
            + ([pltpu.VMEM((PACK2, D), BF)] * ns + [pltpu.SemaphoreType.DMA((ns,))] if first else []),
            hbm=ns if first else 0,
            name="mlp_last" if last else "mlp_first" if first else "mlp_mid",
        )

    g0, g1, dub01, gs, acc_y, acc_z = mlp([pack2, pack2_c], [up_g, recv_g], True, False)
    got_g1 = swap_tp(g1, 1)
    pack2_cx = swap_tp(after(pack2_x, acc_y), 1)
    g2, dub2, acc_y, acc_z = mlp([pack2_x], [gs, acc_y, acc_z], False, False)
    g3, dub3, up_y, low_y, dh, dhb, vec_mlp = mlp(
        [pack2_cx],
        [gs, acc_y, acc_z, hs, vecs],
        False,
        True,
    )
    got_g3 = swap_tp(g3, 1)
    lower_y = shift_rows(low_y, 1)

    def attn_bwd(shards, dhb):
        ns = len(shards)
        loaded = [a[s] for a in (packs1, o, qkv, probs) for s in shards]
        return call(
            functools.partial(attn_bwd_kernel, ns, nwl, blocks),
            loaded + [dhb, z1],
            [((D, D), BF)] * ns + [((ns * 16, LANES), F32)] + [((rows, 3 * LANES), BF)] * ns,
            scratch=[pltpu.VMEM((ns, STACK, LANES), F32), pltpu.VMEM((ns, rows, LANES), BF)]
            + [pltpu.VMEM(a.shape, a.dtype) for a in loaded]
            + [pltpu.SemaphoreType.DMA((len(loaded),))],
            hbm=len(loaded),
            name="attn_bwd_" + "".join(map(str, shards)),
        )

    a3, small3, dx3 = attn_bwd((3,), dhb)
    got_a3 = swap_tp(a3, 1)
    across_d = added([g2[:D], after(got_g3, a3)[:D]])
    got_dx = swap_tp(across_d, 2)
    up0 = added([after(g0, across_d)[D:], got_g1[D:]])
    up2 = added([g2[D:], got_g3[D:]])
    half = D // 2
    up_got = swap_rows(jnp.concatenate([up0[half:], up2[half:]], axis=0), bits[0])
    a2, small2, dx2 = attn_bwd((2,), after(dhb, across_d, up0, up2))
    across_a = added([a2, got_a3])
    got_ax = swap_tp(across_a, 2)
    a0, a1, small01, dx0, dx1 = attn_bwd((0, 1), after(dhb, across_a))
    got_a1 = swap_tp(a1, 1)
    page_own = jnp.concatenate([after(up_y, a2), lower_y], axis=0)
    from_c = swap_tp(page_own, 1)

    down = scatter_step([after(g0, a0)[:D], after(got_g1, a0)[:D], got_dx], bits[0], blocks)
    up_got = after(up_got, down[0])
    up0 = added([up0[:half], up_got[:half]])
    up2 = added([up2[:half], up_got[half:]])
    up_x = swap_tp(up2, 2)
    attn = [after(a0, up0, up2, down[0]), got_a1, got_ax]
    mlp = None
    gather_a = [b for b in reversed(bits) if b < blocks]
    gather_m = gather_a[:-2] + gather_a[:-3:-1]
    steps = len(bits) + len(gather_a)
    for i in range(steps):
        if i == 0:
            mark = added(attn)
            attn = scatter_step([mark], bits[i], blocks)
            loaded = [after(dx0, mark), dx1, dx2, dx3] + packs1 + [x_win, dh]
            up_g, low_g, small = call(
                functools.partial(final_kernel, nwl),
                loaded + [vecs, vec_mlp, small3, small2, small01, dub01, dub2, dub3],
                [((STRIP, D), BF)] * 2 + [((SMALL_ROWS, D), BF)],
                scratch=[pltpu.VMEM((SMALL_ROWS, D), F32), pltpu.VMEM((rows, D), BF)]
                + [pltpu.VMEM(a.shape, a.dtype) for a in loaded]
                + [pltpu.SemaphoreType.DMA((len(loaded),))],
                hbm=len(loaded),
                name="final",
            )
            small = [small]
            lower_g = shift_rows(low_g, 1)
        elif i < len(bits):
            mark = added(attn)
            attn, small = riding_step([mark], small, bits[i], blocks)
        else:
            mark = added(attn) if i == len(bits) else jnp.concatenate(attn, axis=0)
            attn = [mark, swap_rows(mark, gather_a[i - len(bits)])]
        if i == 0:
            down = added([after(down[0], mark), down[1]])
            up = added([up0, up_x])
            mlp = scatter_step([interleaved([down, up], blocks // 2)], bits[1], blocks)
            from_x = swap_tp(after(page_own, mark), 2)
        elif i + 1 < steps:
            kept = after(mlp[0], mark)
            if i + 1 < len(bits):
                mlp = scatter_step([kept, mlp[1]], bits[i + 1], blocks)
            else:
                first = i + 1 == len(bits)
                total = added([kept, mlp[1]]) if first else jnp.concatenate([kept, mlp[1]], axis=0)
                mlp = [total, swap_rows(total, gather_m[i + 1 - len(bits)])]
        if i == 2:
            own_g = jnp.concatenate([after(up_g, mark), lower_g], axis=0)
            g_x = swap_tp(own_g, 2)
            g_c = swap_tp(own_g, 1)
        if i == len(bits):
            small = added([after(small[0], mark), small[1]])
            small = [small, swap_rows(small, bits[0])]
            from_cx = swap_tp(after(from_x, mark), 1)
        if i == len(bits) + 1:
            small = added([after(small[0], mark), small[1]])
            s_x = swap_tp(small, 2)
            s_c = swap_tp(small, 1)
    g_cx = swap_tp(after(g_x, mark), 1)
    s_cx = swap_tp(after(s_x, mark), 1)
    block_out = page([after(page_own, mark), from_c, from_x, from_cx], patches.shape, "page_y")
    grad_patches = page([after(own_g, mark), g_c, g_x, g_cx], patches.shape, "page_g")
    *v, mine = call(
        small_kernel,
        [small, s_c, s_x, s_cx],
        [((1, D), F32)] * 6 + [((SMALL_SHARD, LANES), F32)],
        name="small",
    )
    attn[0] = after(attn[0], block_out, grad_patches, mine)
    grad_qkv, grad_proj = finish(attn, blocks, gather_a, "finish_attn")
    grad_down, grad_up = finish([after(mlp[0], grad_qkv), mlp[1]], blocks, gather_m, "finish_mlp")

    v = [line.reshape(D) for line in v]
    grad_pos_table = mine[:12].reshape(HEADS_HERE, TABLE_PAD)[:, :TABLE].T

    return (
        block_out,
        grad_patches,
        v[4],
        v[5],
        grad_qkv,
        mine[12:14],
        grad_pos_table,
        grad_proj,
        v[3],
        v[0],
        v[1],
        grad_up,
        mine[16:20].reshape(D),
        grad_down,
        v[2],
    )


def solution(mesh):
    placed = (
        P("rows", None, None),
        P("rows", None, None),
        P("rows", None),
        P(),
        P(),
        P(None, None, "tp"),
        P(None, "tp"),
        P(None, "tp"),
        P("tp", None),
        P(),
        P(),
        P(),
        P(None, "tp"),
        P("tp"),
        P("tp", None),
        P(),
    )
    return jax.shard_map(
        per_device,
        mesh=mesh,
        in_specs=placed,
        out_specs=(
            P("rows", None, None),
            P("rows", None, None),
            P(),
            P(),
            P(None, None, "tp"),
            P(None, "tp"),
            P(None, "tp"),
            P("tp", None),
            P(),
            P(),
            P(),
            P(None, "tp"),
            P("tp"),
            P("tp", None),
            P(),
        ),
        check_vma=False,
    )
```

```python
import functools

import jax
import jax.numpy as jnp
import numpy as np
from jax import lax
from jax.experimental import pallas as pl
from jax.experimental.pallas import tpu as pltpu
from jax.sharding import PartitionSpec as P

D = 512
HD = 32
WIN = 10
SHIFT = 5
TABLE = 361
TABLE_PAD = 384
NORM_EPS = 1e-05
MASKED = -1000000000.0
HIDDEN_KEY = -1e30

TP = 4
HEADS_HERE = 4
LANES = 128
TOKENS = WIN * WIN
WROW = 112
SEG = 64
STRIP = SHIFT * SEG
COLBLK = 16
NBLK = 5
SLAB = SHIFT * NBLK * COLBLK
STACK = HEADS_HERE * WROW
SPAN = 2 * WIN - 1
REACH = SPAN * (WIN - 1) + WIN - 1
PACK1 = 4 * D + 32
SMALL_SHARD = 24
SMALL_ROWS = 32
PACK2 = 2 * D + 16

F32 = jnp.float32
BF = jnp.bfloat16
VMEM_LIMIT = 24
VMEM_OF = {"head": 56, "rest": 56, "attn_fwd": 56}
COST_RATE = 2e8
UNROLL = 2
UNROLL_F = 2


def dot(a, b):
    return lax.dot_general(a, b, (((1,), (0,)), ((), ())), preferred_element_type=F32)


def dot_nt(a, b):
    return lax.dot_general(a, b, (((1,), (1,)), ((), ())), preferred_element_type=F32)


def dot_tn(a, b):
    return lax.dot_general(a, b, (((0,), (0,)), ((), ())), preferred_element_type=F32)


def onehot(idx, width):
    lanes = lax.broadcasted_iota(jnp.int32, (idx.shape[0], width), 1)
    return jnp.where(idx == lanes, 1.0, 0.0).astype(BF)


def rows_of(nwl):
    return -(-(nwl * WROW + 16) // 64) * 64


def tens(v):
    return sum((v >= WIN * m).astype(jnp.int32) for m in range(1, WIN))


def column(n):
    return lax.broadcasted_iota(jnp.int32, (n, 1), 0)


def lane_row(n):
    return lax.broadcasted_iota(jnp.int32, (1, n), 1)


def strip_places():
    d = column(STRIP)
    a = sum((d >= SEG * m).astype(jnp.int32) for m in range(1, SHIFT))
    return a, d - SEG * a


def window_places(rows, nwl):
    r = column(rows)
    j = sum((r >= WROW * m).astype(jnp.int32) for m in range(1, nwl + 1))
    return j, r - WROW * j


def strip_from_slab(nwl):
    a, c = strip_places()
    return jnp.where(c < nwl * WIN, a * (NBLK * COLBLK) + c, -1000)


def window_from(rows, nwl, low, row_width):
    j, i = window_places(rows, nwl)
    a = tens(i)
    found = (a - (SHIFT if low else 0)) * row_width + WIN * j + i - WIN * a
    first = TOKENS // 2 if low else 0
    ok = (i >= first) & (i < first + TOKENS // 2) & (j < nwl)
    return jnp.where(ok, found, -1000)


def strip_from_window(nwl, low):
    a, c = strip_places()
    j = tens(c)
    found = j * WROW + (a + (SHIFT if low else 0)) * WIN + c - WIN * j
    return jnp.where(c < nwl * WIN, found, -1000)


def pick_rows(places, source):
    return dot(onehot(places, source.shape[0]), source).astype(BF)


KERNEL_US = {
    "head": 3.0,
    "rest": 5.0,
    "attn_fwd": 14.0,
    "mlp_first": 9.0,
    "mlp_mid": 5.0,
    "mlp_last": 5.0,
    "attn_bwd_3": 7.0,
    "attn_bwd_2": 7.0,
    "attn_bwd_01": 11.0,
    "final": 1.0,
}


def cost(name):
    return pl.CostEstimate(
        flops=int(KERNEL_US.get(name, 0.01) * COST_RATE), bytes_accessed=1024, transcendentals=0
    )


def vspec():
    return pl.BlockSpec(memory_space=pltpu.VMEM)


def after(x, *others):
    return lax.optimization_barrier((x, *others))[0]


def call(kernel, args, outs, scratch=(), scalars=(), hbm=0, hbm_out=0, name=None):
    in_hbm = pl.BlockSpec(memory_space=pltpu.HBM)
    return pl.pallas_call(
        kernel,
        out_shape=[jax.ShapeDtypeStruct(s, d) for s, d in outs],
        in_specs=[pl.BlockSpec(memory_space=pltpu.SMEM) for _ in scalars]
        + [in_hbm if i < hbm else vspec() for i in range(len(args))],
        out_specs=[in_hbm if i < hbm_out else vspec() for i in range(len(outs))],
        scratch_shapes=list(scratch),
        compiler_params=pltpu.CompilerParams(vmem_limit_bytes=VMEM_OF.get(name, VMEM_LIMIT) * 2**20),
        cost_estimate=cost(name),
        name=name,
    )(*scalars, *[pltpu.with_memory_space_constraint(a, pltpu.HBM) for a in args[:hbm]], *args[hbm:])


def first_column(width):
    c = lax.axis_index("tp") * width + SHIFT
    off = lax.rem(c, COLBLK)
    return c - off, off


def slab_copies(field, half, start, slab, sems, k):
    main = (NBLK - 1) * COLBLK
    last = lax.rem(start + main, field.shape[1])
    rows = pl.ds(half * SHIFT, SHIFT)
    return [
        pltpu.make_async_copy(
            field.at[rows, pl.ds(pl.multiple_of(start, COLBLK), main), :],
            slab.at[:, :main, :],
            sems.at[k],
        ),
        pltpu.make_async_copy(
            field.at[rows, pl.ds(pl.multiple_of(last, COLBLK), COLBLK), :],
            slab.at[:, main:, :],
            sems.at[k + 1],
        ),
    ]


def head_kernel(width, x, wqkv, wproj, table, bias, strip, pack, slab, sems):
    start, off = first_column(width)
    rows = slab_copies(x, 0, start, slab, sems, 0)
    copies = [pltpu.make_async_copy(wqkv, pack.at[: 3 * D, :], sems.at[2])]
    for c in range(D // LANES):
        at = 3 * D + c * LANES
        copies.append(
            pltpu.make_async_copy(
                wproj.at[:, c * LANES : (c + 1) * LANES], pack.at[at : at + LANES, :], sems.at[3 + c]
            )
        )
    for copy in rows + copies:
        copy.start()
    row = lax.broadcasted_iota(jnp.int32, (TABLE, TABLE_PAD), 0)
    lane = lax.broadcasted_iota(jnp.int32, (TABLE, TABLE_PAD), 1)
    flip = jnp.where(row + lane == TABLE - 1, 1.0, 0.0).astype(BF)
    rev = dot(table[...], flip)
    lines = [rev[:, c * LANES : (c + 1) * LANES] for c in range(TABLE_PAD // LANES)]
    lines += [bias[...].astype(F32), jnp.zeros((PACK1 - 4 * D - 14, LANES), F32)]
    pack[4 * D :, :] = jnp.concatenate(lines, axis=0).astype(BF)
    hot = onehot(strip_from_slab(width // WIN) + off, SLAB)
    for copy in rows:
        copy.wait()
    strip[...] = dot(hot, slab[...].reshape(SLAB, D)).astype(BF)
    for copy in copies:
        copy.wait()


def rest_kernel(width, x, g, up, down, ubias, strip_g, win_x, win_g, pack, slabs, sems):
    start, off = first_column(width)
    rows = []
    for k, (field, half) in enumerate(((g, 0), (x, 1), (g, 1))):
        rows.append(slab_copies(field, half, start, slabs.at[k], sems, 2 * k))
    copies = [
        pltpu.make_async_copy(up, pack.at[:D, :], sems.at[6]),
        pltpu.make_async_copy(down, pack.at[D : 2 * D, :], sems.at[7]),
    ]
    for copy in sum(rows, []) + copies:
        copy.start()
    pack[2 * D :, :] = jnp.broadcast_to(ubias[...], (PACK2 - 2 * D, D))
    nwl = width // WIN
    wide = window_from(win_x.shape[0], nwl, False, NBLK * COLBLK)
    hots = [onehot(strip_from_slab(nwl) + off, SLAB), onehot(wide + off, SLAB)]
    for k, out in enumerate((strip_g, win_x, win_g)):
        for copy in rows[k]:
            copy.wait()
        out[...] = dot(hots[min(k, 1)], slabs[k].reshape(SLAB, D)).astype(BF)
    for copy in copies:
        copy.wait()


def norm_stats(x):
    mean = jnp.mean(x, axis=-1, keepdims=True)
    center = x - mean
    spread = jnp.mean(center * center, axis=-1, keepdims=True)
    inv = lax.rsqrt(spread + NORM_EPS)
    return center * inv, inv


def norm_back(dz, n, inv, gain):
    gz = dz * gain
    m1 = jnp.mean(gz, axis=-1, keepdims=True)
    m2 = jnp.mean(gz * n, axis=-1, keepdims=True)
    return (gz - m1 - n * m2) * inv


def row_chunks(rows, count):
    size = rows // count
    return [(c * size, size) for c in range(count)]


def head_masks():
    lane = lax.broadcasted_iota(jnp.int32, (1, LANES), 1)
    return [(lane >= h * HD) & (lane < (h + 1) * HD) for h in range(HEADS_HERE)]


def stacked(x, masks):
    return jnp.concatenate([jnp.where(m, x, jnp.zeros_like(x)) for m in masks], axis=0)


def unstacked(y, masks):
    total = jnp.where(masks[0], y[:WROW], 0.0)
    for h in range(1, HEADS_HERE):
        total = jnp.where(masks[h], y[h * WROW : (h + 1) * WROW], total)
    return total


def attn_fwd_kernel(nwl, bounds, *refs):
    packs, (upx, recv, vecs) = refs[:TP], refs[TP : TP + 3]
    refs = refs[TP + 3 :]
    qkv, probs, o_out = refs[:TP], refs[TP : 2 * TP], refs[2 * TP : 3 * TP]
    x_out, z1_out, hs_out, z2_out, bias_sc, roll_sc, row_sc, w_sc, small_sc, fm = refs[3 * TP : 3 * TP + 10]
    x_sc, z1_sc, qkv_sc, p_sc, o_sc, sems = refs[3 * TP + 10 :]
    rows = x_out.shape[0]
    smalls, weights, projs = [], [], []
    for s in range(TP):
        lanes = slice(s * LANES, (s + 1) * LANES)
        smalls.append(
            pltpu.make_async_copy(packs[s].at[4 * D :, :], small_sc.at[s], sems.at[8 * s])
        )
        for m in range(3):
            weights.append(
                pltpu.make_async_copy(
                    packs[s].at[m * D : (m + 1) * D, :], w_sc.at[m, :, lanes], sems.at[8 * s + 1 + m]
                )
            )
        for c in range(D // LANES):
            projs.append(
                pltpu.make_async_copy(
                    packs[s].at[3 * D + c * LANES : 3 * D + (c + 1) * LANES, :],
                    w_sc.at[3, lanes, c * LANES : (c + 1) * LANES],
                    sems.at[8 * s + 4 + c],
                )
            )
    for copy in smalls + weights + projs:
        copy.start()
    is_end = jnp.where(bounds[0, 1] == lax.axis_index("rows"), 1.0, 0.0)
    last = jnp.where(lax.axis_index("tp") == TP - 1, 1.0, 0.0)
    g1, b1, g2, b2, bp = (vecs[i : i + 1, :] for i in range(5))

    for copy in smalls:
        copy.wait()
    table = jnp.concatenate(
        [
            jnp.concatenate(
                [small_sc[s, 4 * c : 4 * c + 4, :].astype(F32) for c in range(TABLE_PAD // LANES)],
                axis=1,
            )
            for s in range(TP)
        ],
        axis=0,
    )
    for i in range(TOKENS):
        shift = TABLE_PAD - REACH + SPAN * (i // WIN) + i % WIN
        rolled = pltpu.roll(table, shift, 1)
        roll_sc[i * TP * HEADS_HERE : (i + 1) * TP * HEADS_HERE, :] = rolled[:, : 2 * LANES].astype(BF)
    n16 = TOKENS * TP * HEADS_HERE
    lane = lane_row(LANES)
    at_lane = jnp.where(lane < TOKENS, lane + (SPAN - WIN) * tens(lane), -1000)
    spread = jnp.where(column(2 * LANES) == at_lane, 1.0, 0.0).astype(BF)
    row_sc[:n16, :] = dot(roll_sc[...], spread)
    row_sc[n16:, :] = jnp.zeros((WROW * TP * HEADS_HERE - n16, LANES), F32)
    row = column(WROW)
    real = (row < TOKENS) & (lane < TOKENS)
    low_differ = ((row >= TOKENS // 2) != (lane >= TOKENS // 2)) & real
    right_differ = ((row - WIN * tens(row) >= SHIFT) != (lane - WIN * tens(lane) >= SHIFT)) & real
    extra = jnp.where(lane < TOKENS, 0.0, HIDDEN_KEY) + jnp.where(low_differ, MASKED * is_end, 0.0)
    fm[...] = jnp.where(right_differ, MASKED * last, 0.0)
    for s in range(TP):
        for h in range(HEADS_HERE):
            rows_h = row_sc[pl.ds(s * HEADS_HERE + h, WROW, TP * HEADS_HERE), :]
            bias_sc[s, h * WROW : (h + 1) * WROW, :] = rows_h + extra

    places = window_from(rows, nwl, True, SEG)
    for r0, n in row_chunks(rows, 4):
        x = upx[r0 : r0 + n, :].astype(F32) + dot(onehot(places[r0 : r0 + n, :], STRIP), recv[...])
        x_sc[r0 : r0 + n, :] = x.astype(BF)
        z, _ = norm_stats(x)
        z1_sc[r0 : r0 + n, :] = (z * g1 + b1).astype(BF)
    outgoing = loads([x_sc, z1_sc], [x_out, z1_out], sems, 8 * TP)
    scale = HD ** (-0.5)
    for copy in weights:
        copy.wait()
    for m in range(3):
        for r0, n in row_chunks(rows, 2):
            y = dot(z1_sc[r0 : r0 + n, :], w_sc[m])
            for s in range(TP):
                part = y[:, s * LANES : (s + 1) * LANES]
                if m == 0:
                    part = (part + small_sc[s, 12:13, :].astype(F32)) * scale
                if m == 2:
                    part = part + small_sc[s, 13:14, :].astype(F32)
                qkv_sc[s, m, r0 : r0 + n, :] = part.astype(BF)
    outgoing += loads([qkv_sc.at[s] for s in range(TP)], qkv, sems, 8 * TP + 2)
    for s in range(TP):
        o_sc[s, nwl * WROW :, :] = jnp.zeros((rows - nwl * WROW, LANES), BF)

    def window(j, carry):
        masks = head_masks()
        base = pl.multiple_of(j * WROW, 16)
        flag = jnp.where(j == nwl - 1, 1.0, 0.0)
        fm4 = jnp.concatenate([fm[...] * flag] * HEADS_HERE, axis=0)
        for s in range(TP):
            q = qkv_sc[s, 0, pl.ds(base, WROW), :]
            k = qkv_sc[s, 1, pl.ds(base, LANES), :]
            v = qkv_sc[s, 2, pl.ds(base, LANES), :]
            sco = dot_nt(stacked(q, masks), k) + bias_sc[s] + fm4
            top = jnp.max(sco, axis=-1, keepdims=True)
            e = jnp.exp(sco - top)
            total = jnp.sum(e, axis=-1, keepdims=True)
            p = (e / total).astype(BF)
            p_sc[s, j] = p
            o = unstacked(dot(p, v), masks)
            o_sc[s, pl.ds(base, WROW), :] = o.astype(BF)
        return carry

    lax.fori_loop(0, nwl, window, 0, unroll=UNROLL_F)
    outgoing += loads([p_sc.at[s] for s in range(TP)], probs, sems, 8 * TP + 6)
    outgoing += loads([o_sc.at[s] for s in range(TP)], o_out, sems, 8 * TP + 10)
    for copy in projs:
        copy.wait()
    for r0, n in row_chunks(rows, 2):
        o = jnp.concatenate([o_sc[s, r0 : r0 + n, :] for s in range(TP)], axis=1)
        acc = x_sc[r0 : r0 + n, :].astype(F32) + bp + dot(o, w_sc[3])
        hs_out[r0 : r0 + n, :] = acc
        z, _ = norm_stats(acc)
        z2_out[r0 : r0 + n, :] = (z * g2 + b2).astype(BF)
    for copy in outgoing:
        copy.wait()


def bits_in_order(blocks, down):
    bits = [1 << k for k in range(blocks.bit_length() - 1)]
    return bits[1::-1] + bits[2:] if down else bits


def my_block(blocks, down=False):
    w = lax.axis_index("rows")
    mine = 0
    for bit in bits_in_order(blocks, down):
        mine = mine * 2 + lax.rem(lax.div(w, bit), 2)
    return mine


def store_blocks(out, r0, value, blocks, cols=None, down=False):
    size = value.shape[0] // blocks
    mine = my_block(blocks, down)
    for b in range(blocks):
        at = pl.multiple_of(r0 + jnp.bitwise_xor(mine, b) * size, size)
        part = value[b * size : (b + 1) * size, :]
        if cols is None:
            out[pl.ds(at, size), :] = part
        else:
            out[pl.ds(at, size), cols[0] : cols[1]] = part


def mlp_kernel(ns, first, last, nwl, blocks, *refs):
    refs = list(refs)
    packs = refs[:ns]
    if first:
        held, sems = refs[-1 - ns : -1], refs[-1]
        copies = loads(packs, held, sems)
        packs, refs = held, refs[: -1 - ns]
    z2 = refs[ns]
    refs = refs[ns + 1 :]
    if first:
        gup, grecv = refs[:2]
        refs = refs[2:]
    else:
        gs, y_in, z_in = refs[:3]
        refs = refs[3:]
    if last:
        hs, vecs = refs[:2]
        refs = refs[2:]
    grads, dub = refs[:ns], refs[ns]
    refs = refs[ns + 1 :]
    if first:
        gs = refs.pop(0)
    if last:
        out_up, out_low, dh_out, dhb_out, vec_out = refs[:5]
        refs = refs[5:]
    acc_y, acc_z, act_sc, du_sc = refs
    rows = z2.shape[0]
    if first:
        places = window_from(rows, nwl, True, SEG)
        for r0, n in row_chunks(rows, 4):
            gs[r0 : r0 + n, :] = (
                gup[r0 : r0 + n, :].astype(F32)
                + dot(onehot(places[r0 : r0 + n, :], STRIP), grecv[...])
            ).astype(BF)
    for k in range(ns):
        if first:
            copies[k].wait()
        ub = packs[k][2 * D : 2 * D + 1, :].astype(F32)
        dub_total = jnp.zeros((1, D), F32)
        for r0, n in row_chunks(rows, 2):
            sl = slice(r0, r0 + n)
            u = dot(z2[sl, :], packs[k][:D, :]) + ub
            phi = 0.5 * (1.0 + lax.erf(u * np.float32(np.sqrt(0.5))))
            act = (u * phi).astype(BF)
            slope = phi + u * (jnp.exp(-0.5 * u * u) * np.float32(1 / np.sqrt(2 * np.pi)))
            act_sc[sl, :] = act
            ga = dot_nt(gs[sl, :], packs[k][D : 2 * D, :])
            du = (slope * ga).astype(BF)
            du_sc[sl, :] = du
            dub_total += jnp.sum(du.astype(F32), axis=0, keepdims=True)
            y = dot(act, packs[k][D : 2 * D, :])
            z = dot_nt(du, packs[k][:D, :])
            if k > 0:
                acc_y[sl, :] += y
                acc_z[sl, :] += z
            elif first:
                acc_y[sl, :] = y
                acc_z[sl, :] = z
            else:
                acc_y[sl, :] = y + y_in[sl, :]
                acc_z[sl, :] = z + z_in[sl, :]
        for c in range(D // LANES):
            line = k * (D // LANES) + c
            dub[line : line + 1, :] = dub_total[:, c * LANES : (c + 1) * LANES]
        store_blocks(grads[k], 0, dot_tn(act_sc[...], gs[...]).astype(BF), blocks, down=True)
        store_blocks(grads[k], D, dot_tn(z2[...], du_sc[...]).astype(BF), blocks)
    if not last:
        return
    g2, bd = vecs[2:3, :], vecs[5:6, :]
    sums = [jnp.zeros((1, D), F32) for _ in range(4)]
    for r0, n in row_chunks(rows, 4):
        sl = slice(r0, r0 + n)
        dz = acc_z[sl, :]
        g = gs[sl, :].astype(F32)
        h = hs[sl, :]
        nrm, inv = norm_stats(h)
        dh = g + norm_back(dz, nrm, inv, g2)
        dh_out[sl, :] = dh
        dhb_out[sl, :] = dh.astype(BF)
        act_sc[sl, :] = (h + acc_y[sl, :] + bd).astype(BF)
        for i, term in enumerate((dz * nrm, dz, g, dh)):
            sums[i] = sums[i] + jnp.sum(term, axis=0, keepdims=True)
    vec_out[...] = jnp.concatenate(sums, axis=0)
    out_up[...] = pick_rows(strip_from_window(nwl, False), act_sc[...])
    out_low[...] = pick_rows(strip_from_window(nwl, True), act_sc[...])


def loads(sources, targets, sems, at=0):
    copies = [
        pltpu.make_async_copy(x, y, sems.at[at + i]) for i, (x, y) in enumerate(zip(sources, targets))
    ]
    for copy in copies:
        copy.start()
    return copies


def attn_bwd_kernel(ns, nwl, blocks, *refs):
    refs = list(refs)

    def take(n):
        found = refs[:n]
        del refs[:n]
        return found

    n_in = 4 * ns
    sources = take(n_in)
    dhb, z1 = take(2)
    grads = take(ns)
    dpos, *dx_sc = take(1 + ns)
    dsum, do_sc = take(2)
    held = take(n_in)
    (sems,) = refs
    copies = loads(sources, held, sems)
    packs, o, qkv, probs = (held[i * ns : (i + 1) * ns] for i in range(4))
    rows = dhb.shape[0]
    scale = HD ** (-0.5)
    masks = head_masks()
    lin = column(LANES)
    lin = jnp.where(lin < TOKENS, REACH - lin - (SPAN - WIN) * tens(lin), -1000)
    back = onehot(lin, TABLE_PAD)
    place = lane_row(STACK)
    head = sum((place >= WROW * m).astype(jnp.int32) for m in range(1, HEADS_HERE))
    place = place - WROW * head
    line = jnp.where(place < TOKENS, tens(place) * 8 + head, -1000)
    groups = jnp.where(column(WIN * 8) == line, 1.0, 0.0).astype(BF)
    for k in range(ns):
        copies[k].wait()
        total = None
        for c in range(D // LANES):
            w = packs[k][3 * D + c * LANES : 3 * D + (c + 1) * LANES, :]
            term = dot_nt(dhb[:, c * LANES : (c + 1) * LANES], w)
            total = term if total is None else total + term
        do_sc[k] = total.astype(BF)
        copies[ns + k].wait()
        gp = dot_tn(o[k][...], dhb[...]).astype(BF)
        gp = jnp.concatenate([gp[:, c * LANES : (c + 1) * LANES] for c in range(D // LANES)], axis=0)
        store_blocks(grads[k], 0, gp, blocks, (3 * LANES, 4 * LANES))
        dx_sc[k][nwl * WROW :, :] = jnp.zeros((rows - nwl * WROW, 3 * LANES), BF)
        dsum[k] = jnp.zeros(dsum.shape[1:], F32)
        copies[2 * ns + k].wait()
        copies[3 * ns + k].wait()

        def window(j, carry, k=k):
            base = pl.multiple_of(j * WROW, 16)
            q = stacked(qkv[k][0, pl.ds(base, WROW), :], masks)
            key = qkv[k][1, pl.ds(base, LANES), :]
            v = qkv[k][2, pl.ds(base, LANES), :]
            do = stacked(do_sc[k, pl.ds(base, WROW), :], masks)
            p = probs[k][j]
            p32 = p.astype(F32)
            pdp = p32 * dot_nt(do, v)
            ds = (pdp - p32 * jnp.sum(pdp, axis=-1, keepdims=True)).astype(BF)
            dsum[k] += ds.astype(F32)
            dv = dot_tn(p, do)
            dk = dot_tn(ds, q)
            dq = unstacked(dot(ds, key), masks) * scale
            dx_sc[k][pl.ds(base, WROW), :LANES] = dq.astype(BF)
            dx_sc[k][pl.ds(base, WROW), LANES : 2 * LANES] = dk[:WROW].astype(BF)
            dx_sc[k][pl.ds(base, WROW), 2 * LANES :] = dv[:WROW].astype(BF)
            return carry

        lax.fori_loop(0, nwl, window, 0, unroll=UNROLL)
    for k in range(ns):
        store_blocks(grads[k], 0, dot_tn(z1[...], dx_sc[k][...]).astype(BF), blocks, (0, 3 * LANES))
        high = dsum[k].astype(BF)
        low = (dsum[k] - high.astype(F32)).astype(BF)
        lanes = dot(high, back) + dot(low, back)
        turned = jnp.concatenate(
            [
                pltpu.roll(lanes[h * WROW : (h + 1) * WROW, :], 0, 1, stride=1, stride_axis=0)
                for h in range(HEADS_HERE)
            ],
            axis=0,
        )
        high = turned.astype(BF)
        low = (turned - high.astype(F32)).astype(BF)
        summed = dot(groups, high) + dot(groups, low)
        total = summed[:8, :]
        for a in range(1, WIN):
            total = total + pltpu.roll(summed[a * 8 : (a + 1) * 8, :], (SPAN - WIN) * a, 1)
        per = 16
        for h in range(HEADS_HERE):
            for c in range(TABLE_PAD // LANES):
                line = k * per + h * (TABLE_PAD // LANES) + c
                dpos[line : line + 1, :] = total[h : h + 1, c * LANES : (c + 1) * LANES]
        for i, m in enumerate((0, 2)):
            part = dx_sc[k][:, m * LANES : (m + 1) * LANES].astype(F32)
            line = k * per + 12 + i
            dpos[line : line + 1, :] = jnp.sum(part, axis=0, keepdims=True)
        dpos[k * per + 14 : (k + 1) * per, :] = jnp.zeros((2, LANES), F32)


def final_kernel(nwl, *refs):
    refs = list(refs)
    packs, dxs, refs = refs[:TP], refs[TP : 2 * TP], refs[2 * TP :]
    x_ref, dh, vecs, vec_mlp, small3, small2, small01, dub01, dub2, dub3 = refs[:10]
    out_up, out_low, small_out, small_f32, dz = refs[10:15]
    held, sems = refs[15:-1], refs[-1]
    copies = loads(packs, held, sems)
    rows = x_ref.shape[0]
    for copy in copies:
        copy.wait()
    parts = list(zip(dxs, held))
    weights = [
        jnp.concatenate([pack[m * D : (m + 1) * D, :] for m in range(3)], axis=1) for _, pack in parts
    ]
    sums = [jnp.zeros((1, D), F32) for _ in range(2)]
    for r0, n in row_chunks(rows, 2):
        sl = slice(r0, r0 + n)
        total = None
        for (dx, _), weight in zip(parts, weights):
            term = dot_nt(dx[sl, :], weight)
            total = term if total is None else total + term
        nrm, inv = norm_stats(x_ref[sl, :].astype(F32))
        dz[sl, :] = (dh[sl, :] + norm_back(total, nrm, inv, vecs[0:1, :])).astype(BF)
        sums[0] = sums[0] + jnp.sum(total * nrm, axis=0, keepdims=True)
        sums[1] = sums[1] + jnp.sum(total, axis=0, keepdims=True)
    t = lax.axis_index("tp")
    pieces = [
        (small01[:16, :], dub01[:4, :]),
        (small01[16:, :], dub01[4:, :]),
        (small2[...], dub2[...]),
        (small3[...], dub3[...]),
    ]
    for s, (lines, dub) in enumerate(pieces):
        at = pl.multiple_of(jnp.bitwise_xor(t, s) * LANES, LANES)
        both = jnp.concatenate([lines, dub, jnp.zeros((4, LANES), F32)], axis=0)
        small_f32[: SMALL_SHARD, pl.ds(at, LANES)] = both
    small_f32[SMALL_SHARD:, :] = jnp.concatenate(
        [vec_mlp[...]] + sums + [jnp.zeros((SMALL_ROWS - SMALL_SHARD - 6, D), F32)], axis=0
    )
    small_out[...] = small_f32[...].astype(BF)
    out_up[...] = pick_rows(strip_from_window(nwl, False), dz[...])
    out_low[...] = pick_rows(strip_from_window(nwl, True), dz[...])


def page_kernel(*refs):
    out = refs[TP]
    pw = out.shape[1]
    t = lax.axis_index("tp")
    width = pw // TP
    col = lax.broadcasted_iota(jnp.int32, (pw, 1), 0)
    hots = []
    for s in range(TP):
        v = col - width * jnp.bitwise_xor(t, s) - SHIFT
        v = jnp.where(v < 0, v + pw, v)
        v = jnp.where(v < width, v, -1000)
        hots.append(onehot(v, SEG))
    hot = jnp.concatenate(hots, axis=1)
    for r in range(WIN):
        off = STRIP + r * SEG if r < SHIFT else (r - SHIFT) * SEG
        parts = [ul[off : off + SEG, :] for ul in refs[:TP]]
        out[r] = dot(hot, jnp.concatenate(parts, axis=0)).astype(BF)


def swap_tp(x, bit):
    return lax.ppermute(x, "tp", [(i, i ^ bit) for i in range(TP)])


def swap_rows(x, bit):
    return lax.ppermute(x, "rows", [(i, i ^ bit) for i in range(lax.axis_size("rows"))])


def shift_rows(x, distance):
    n = lax.axis_size("rows")
    return lax.ppermute(x, "rows", [(i, (i + distance) % n) for i in range(n)])


def row_bits():
    n = lax.axis_size("rows")
    bits = []
    while 1 << len(bits) < n:
        bits.append(1 << len(bits))
    return bits


def blocks_for(rows):
    blocks = 1
    while 2 * blocks <= lax.axis_size("rows") and rows % (2 * blocks) == 0 and rows // (2 * blocks) >= 16:
        blocks *= 2
    return blocks


def added(arrays):
    total = arrays[0].astype(F32)
    for extra in arrays[1:]:
        total = total + extra.astype(F32)
    return total.astype(BF)


def scatter_step(arrays, bit, blocks):
    total = added(arrays)
    if bit < blocks:
        half = total.shape[0] // 2
        return [total[:half], swap_rows(total[half:], bit)]
    return [total, swap_rows(total, bit)]


def finish_kernel(blocks, gathered, n_in, *refs):
    ins, outs = refs[:n_in], refs[n_in:]
    part = ins[0].shape[0] * n_in // blocks
    each = blocks // n_in
    both = len(outs) == 2
    half = part // 2

    def place(p, down):
        order = bits_in_order(blocks, down)
        moved = sum(
            ((p >> k) & 1) << (len(order) - 1 - order.index(bit)) for k, bit in enumerate(gathered)
        )
        return jnp.bitwise_xor(my_block(blocks, down), moved)

    for p in range(blocks):
        piece = ins[p // each][(p % each) * part : (p % each + 1) * part, :].astype(F32)
        if both:
            for out, value, down in zip(outs, (piece[:half], piece[half:]), (True, False)):
                out[pl.ds(pl.multiple_of(place(p, down) * half, half), half), :] = value
        else:
            outs[2][pl.ds(pl.multiple_of(place(p, False) * part, part), part), :] = piece
    if both:
        return
    qkv, proj, whole = outs
    for c in range(D // LANES):
        if c < 3:
            qkv[c] = whole[:, c * LANES : (c + 1) * LANES]
        proj[:, c * LANES : (c + 1) * LANES] = whole[c * LANES : (c + 1) * LANES, 3 * LANES :]


def finish(pieces, blocks, gathered, name):
    attn = name == "finish_attn"
    return call(
        functools.partial(finish_kernel, blocks, gathered, len(pieces)),
        pieces,
        [((3, D, LANES), F32), ((LANES, D), F32)] if attn else [((D, D), F32)] * 2,
        scratch=[pltpu.VMEM((D, D), F32)] if attn else [],
        name=name,
    )


def interleaved(parts, blocks):
    n = blocks
    cut = [p.reshape(n, 1, p.shape[0] // n, p.shape[1]) for p in parts]
    return jnp.concatenate(cut, axis=1).reshape(-1, parts[0].shape[1])


def riding_step(arrays, small, bit, blocks):
    total = added(arrays)
    small = added(small)
    half = total.shape[0] // 2 if bit < blocks else total.shape[0]
    got = swap_rows(jnp.concatenate([total[-half:], small], axis=0), bit)
    return [total[:half], got[:half]], [small, got[half:]]


def small_kernel(*refs):
    ins, outs = refs[:TP], refs[TP:]
    total = ins[0][2 * STRIP :, :].astype(F32)
    for r in ins[1:]:
        total += r[2 * STRIP :, :].astype(F32)
    for i in range(6):
        outs[i][...] = total[SMALL_SHARD + i : SMALL_SHARD + i + 1, :]
    t = lax.axis_index("tp")
    mine = jnp.zeros((SMALL_SHARD, LANES), F32)
    for a in range(TP):
        mine = jnp.where(t == a, total[:SMALL_SHARD, a * LANES : (a + 1) * LANES], mine)
    qvb, up, table = outs[6:]
    qvb[...] = mine[12:14, :]
    up[...] = mine[16:20, :]
    per = TABLE_PAD // LANES
    for h in range(HEADS_HERE):
        line = jnp.concatenate([mine[h * per + c : h * per + c + 1, :] for c in range(per)], axis=1)
        table[h : h + 1, :] = line[:, :TABLE]


def page(pieces, page_shape, name):
    return call(page_kernel, pieces, [(page_shape, BF)], name=name)[0]


def per_device(
    patches,
    cotangent,
    page_bounds,
    attn_gain,
    attn_shift,
    qkv_weight,
    qv_bias,
    pos_table,
    proj_weight,
    proj_bias,
    mlp_gain,
    mlp_shift,
    up_weight,
    up_bias,
    down_weight,
    down_bias,
):
    t = lax.axis_index("tp")
    pw = patches.shape[1]
    nwl = pw // WIN // TP
    width = nwl * WIN
    rows = rows_of(nwl)
    bits = row_bits()
    blocks = blocks_for(D)

    vecs = jnp.stack([attn_gain, attn_shift, mlp_gain, mlp_shift, proj_bias, down_bias]).astype(F32)
    slab = (SHIFT, NBLK * COLBLK, D)
    strip_x, pack1 = call(
        functools.partial(head_kernel, width),
        [patches, qkv_weight.reshape(3 * D, LANES), proj_weight, pos_table.T, qv_bias],
        [((STRIP, D), BF), ((PACK1, LANES), BF)],
        scratch=[
            pltpu.VMEM(slab, BF),
            pltpu.SemaphoreType.DMA((7,)),
        ],
        hbm=3,
        name="head",
    )
    recv_x = shift_rows(strip_x, -1)
    pack1_x = swap_tp(pack1, 2)
    pack1_c = swap_tp(pack1, 1)
    strip_g, up_x, up_g, pack2 = call(
        functools.partial(rest_kernel, width),
        [patches, after(cotangent, strip_x, vecs), up_weight, down_weight, up_bias[None]],
        [((STRIP, D), BF), ((rows, D), BF), ((rows, D), BF), ((PACK2, D), BF)],
        scratch=[
            pltpu.VMEM((3,) + slab, BF),
            pltpu.SemaphoreType.DMA((8,)),
        ],
        hbm=4,
        name="rest",
    )
    recv_g = shift_rows(strip_g, -1)
    pack1_cx = swap_tp(after(pack1_x, strip_g, recv_x, pack1_c), 1)
    packs1 = [pack1, pack1_c, pack1_x, pack1_cx]
    pack2_x = swap_tp(after(pack2, pack1_x), 2)
    pack2_c = swap_tp(pack2, 1)

    outs = call(
        functools.partial(attn_fwd_kernel, nwl),
        packs1 + [up_x, recv_x, vecs],
        [((3, rows, LANES), BF)] * TP
        + [((nwl, STACK, LANES), BF)] * TP
        + [((rows, LANES), BF)] * TP
        + [((rows, D), BF), ((rows, D), BF), ((rows, D), F32), ((rows, D), BF)],
        scratch=[
            pltpu.VMEM((TP, STACK, LANES), F32),
            pltpu.VMEM((TOKENS * TP * HEADS_HERE, 2 * LANES), BF),
            pltpu.VMEM((WROW * TP * HEADS_HERE, LANES), F32),
            pltpu.VMEM((4, D, D), BF),
            pltpu.VMEM((TP, PACK1 - 4 * D, LANES), BF),
            pltpu.VMEM((WROW, LANES), F32),
            pltpu.VMEM((rows, D), BF),
            pltpu.VMEM((rows, D), BF),
            pltpu.VMEM((TP, 3, rows, LANES), BF),
            pltpu.VMEM((TP, nwl, STACK, LANES), BF),
            pltpu.VMEM((TP, rows, LANES), BF),
            pltpu.SemaphoreType.DMA((8 * TP + 2 + 3 * TP,)),
        ],
        scalars=[page_bounds],
        hbm=TP,
        hbm_out=3 * TP + 2,
        name="attn_fwd",
    )
    qkv, probs, o = outs[:TP], outs[TP : 2 * TP], outs[2 * TP : 3 * TP]
    x_win, z1, hs, z2 = outs[3 * TP :]

    def mlp(packs, extra, first, last):
        ns = len(packs)
        outs = [((2 * D, D), BF)] * ns + [((ns * D // LANES, LANES), F32)]
        if first:
            outs += [((rows, D), BF)]
        if last:
            outs += [((STRIP, D), BF)] * 2 + [((rows, D), F32), ((rows, D), BF), ((4, D), F32)]
        accs = [((rows, D), F32)] * 2
        return call(
            functools.partial(mlp_kernel, ns, first, last, nwl, blocks),
            packs + [z2] + extra,
            outs if last else outs + accs,
            scratch=([pltpu.VMEM(*a) for a in accs] if last else [])
            + [pltpu.VMEM((rows, D), BF)] * 2
            + ([pltpu.VMEM((PACK2, D), BF)] * ns + [pltpu.SemaphoreType.DMA((ns,))] if first else []),
            hbm=ns if first else 0,
            name="mlp_last" if last else "mlp_first" if first else "mlp_mid",
        )

    g0, g1, dub01, gs, acc_y, acc_z = mlp([pack2, pack2_c], [up_g, recv_g], True, False)
    got_g1 = swap_tp(g1, 1)
    pack2_cx = swap_tp(after(pack2_x, acc_y), 1)
    g2, dub2, acc_y, acc_z = mlp([pack2_x], [gs, acc_y, acc_z], False, False)
    g3, dub3, up_y, low_y, dh, dhb, vec_mlp = mlp(
        [pack2_cx],
        [gs, acc_y, acc_z, hs, vecs],
        False,
        True,
    )
    got_g3 = swap_tp(g3, 1)
    lower_y = shift_rows(low_y, 1)

    def attn_bwd(shards, dhb):
        ns = len(shards)
        loaded = [a[s] for a in (packs1, o, qkv, probs) for s in shards]
        return call(
            functools.partial(attn_bwd_kernel, ns, nwl, blocks),
            loaded + [dhb, z1],
            [((D, D), BF)] * ns + [((ns * 16, LANES), F32)] + [((rows, 3 * LANES), BF)] * ns,
            scratch=[pltpu.VMEM((ns, STACK, LANES), F32), pltpu.VMEM((ns, rows, LANES), BF)]
            + [pltpu.VMEM(a.shape, a.dtype) for a in loaded]
            + [pltpu.SemaphoreType.DMA((len(loaded),))],
            hbm=len(loaded),
            name="attn_bwd_" + "".join(map(str, shards)),
        )

    a3, small3, dx3 = attn_bwd((3,), dhb)
    got_a3 = swap_tp(a3, 1)
    across_d = added([g2[:D], after(got_g3, a3)[:D]])
    got_dx = swap_tp(across_d, 2)
    up0 = added([after(g0, across_d)[D:], got_g1[D:]])
    up2 = added([g2[D:], got_g3[D:]])
    half = D // 2
    up_got = swap_rows(jnp.concatenate([up0[half:], up2[half:]], axis=0), bits[0])
    a2, small2, dx2 = attn_bwd((2,), after(dhb, across_d, up0, up2))
    across_a = added([a2, got_a3])
    got_ax = swap_tp(across_a, 2)
    a0, a1, small01, dx0, dx1 = attn_bwd((0, 1), after(dhb, across_a))
    got_a1 = swap_tp(a1, 1)
    page_own = jnp.concatenate([after(up_y, a2), lower_y], axis=0)
    from_c = swap_tp(page_own, 1)

    down = scatter_step([after(g0, a0)[:D], after(got_g1, a0)[:D], got_dx], bits[1], blocks)
    up_got = after(up_got, down[0])
    up0 = added([up0[:half], up_got[:half]])
    up2 = added([up2[:half], up_got[half:]])
    up_x = swap_tp(up2, 2)
    up_g, low_g, small = call(
        functools.partial(final_kernel, nwl),
        packs1
        + [after(dx0, down[0], up2), dx1, dx2, dx3, x_win, dh, vecs, vec_mlp]
        + [small3, small2, small01, dub01, dub2, dub3],
        [((STRIP, D), BF)] * 2 + [((SMALL_ROWS, D), BF)],
        scratch=[pltpu.VMEM((SMALL_ROWS, D), F32), pltpu.VMEM((rows, D), BF)]
        + [pltpu.VMEM((PACK1, LANES), BF)] * TP
        + [pltpu.SemaphoreType.DMA((TP,))],
        hbm=TP,
        name="final",
    )
    lower_g = shift_rows(low_g, 1)

    attn = [after(a0, low_g), got_a1, got_ax]
    small = [small]
    mlp = None
    gather_a = [b for b in reversed(bits) if b < blocks]
    gather_m = gather_a[:-2] + gather_a[:-3:-1]
    steps = len(bits) + len(gather_a)
    for i in range(steps):
        if i < len(bits):
            mark = added(attn)
            attn, small = riding_step([mark], small, bits[i], blocks)
        else:
            mark = added(attn) if i == len(bits) else jnp.concatenate(attn, axis=0)
            attn = [mark, swap_rows(mark, gather_a[i - len(bits)])]
        if i == 0:
            down = scatter_step([after(down[0], mark), down[1]], bits[0], blocks)
            up = scatter_step([after(up0, mark), up_x], bits[1], blocks)
            from_x = swap_tp(after(page_own, mark), 2)
        elif i + 1 < steps:
            if i == 1:
                mlp = [added([after(down[0], mark), down[1]]), added([after(up[0], mark), up[1]])]
                mlp = scatter_step([interleaved(mlp, blocks // 4)], bits[2], blocks)
            elif i + 1 < len(bits):
                mlp = scatter_step([after(mlp[0], mark), mlp[1]], bits[i + 1], blocks)
            else:
                kept = after(mlp[0], mark)
                first = i + 1 == len(bits)
                total = added([kept, mlp[1]]) if first else jnp.concatenate([kept, mlp[1]], axis=0)
                mlp = [total, swap_rows(total, gather_m[i + 1 - len(bits)])]
        if i == len(bits):
            small = added([after(small[0], mark), small[1]])
            own_g = jnp.concatenate([up_g, lower_g, small], axis=0)
            g_x = swap_tp(own_g, 2)
            g_c = swap_tp(own_g, 1)
            from_cx = swap_tp(after(from_x, mark), 1)
    g_cx = swap_tp(after(g_x, mark), 1)
    block_out = page([after(page_own, mark), from_c, from_x, from_cx], patches.shape, "page_y")
    grad_patches = page([after(own_g, mark), g_c, g_x, g_cx], patches.shape, "page_g")
    *v, qvb_line, up_line, table = call(
        small_kernel,
        [own_g, g_c, g_x, g_cx],
        [((1, D), F32)] * 6 + [((2, LANES), F32), ((D // LANES, LANES), F32), ((HEADS_HERE, TABLE), F32)],
        name="small",
    )
    attn[0] = after(attn[0], block_out, grad_patches, table)
    grad_qkv, grad_proj = finish(attn, blocks, gather_a, "finish_attn")
    grad_down, grad_up = finish([after(mlp[0], grad_qkv), mlp[1]], blocks, gather_m, "finish_mlp")

    v = [line.reshape(D) for line in v]

    return (
        block_out,
        grad_patches,
        v[4],
        v[5],
        grad_qkv,
        qvb_line,
        table.T,
        grad_proj,
        v[3],
        v[0],
        v[1],
        grad_up,
        up_line.reshape(D),
        grad_down,
        v[2],
    )


def solution(mesh):
    placed = (
        P("rows", None, None),
        P("rows", None, None),
        P("rows", None),
        P(),
        P(),
        P(None, None, "tp"),
        P(None, "tp"),
        P(None, "tp"),
        P("tp", None),
        P(),
        P(),
        P(),
        P(None, "tp"),
        P("tp"),
        P("tp", None),
        P(),
    )
    return jax.shard_map(
        per_device,
        mesh=mesh,
        in_specs=placed,
        out_specs=(
            P("rows", None, None),
            P("rows", None, None),
            P(),
            P(),
            P(None, None, "tp"),
            P(None, "tp"),
            P(None, "tp"),
            P("tp", None),
            P(),
            P(),
            P(),
            P(None, "tp"),
            P("tp"),
            P("tp", None),
            P(),
        ),
        check_vma=False,
    )
```

```python
import functools

import jax
import jax.numpy as jnp
import numpy as np
from jax import lax
from jax.experimental import pallas as pl
from jax.experimental.pallas import tpu as pltpu
from jax.sharding import PartitionSpec as P

D = 512
HD = 32
WIN = 10
SHIFT = 5
TABLE = 361
TABLE_PAD = 384
NORM_EPS = 1e-05
MASKED = -1000000000.0
HIDDEN_KEY = -1e30

TP = 4
HEADS_HERE = 4
LANES = 128
TOKENS = WIN * WIN
WROW = 112
SEG = 64
STRIP = SHIFT * SEG
COLBLK = 16
NBLK = 5
SLAB = SHIFT * NBLK * COLBLK
STACK = HEADS_HERE * WROW
SPAN = 2 * WIN - 1
REACH = SPAN * (WIN - 1) + WIN - 1
PACK1 = 4 * D + 32
SMALL_SHARD = 24
SMALL_ROWS = 32
PACK2 = 2 * D + 16

F32 = jnp.float32
BF = jnp.bfloat16
VMEM_LIMIT = 24
VMEM_OF = {"head": 56, "rest": 56, "attn_fwd": 56}
COST_RATE = 2e8
UNROLL = 2
UNROLL_F = 2


def dot(a, b):
    return lax.dot_general(a, b, (((1,), (0,)), ((), ())), preferred_element_type=F32)


def dot_nt(a, b):
    return lax.dot_general(a, b, (((1,), (1,)), ((), ())), preferred_element_type=F32)


def dot_tn(a, b):
    return lax.dot_general(a, b, (((0,), (0,)), ((), ())), preferred_element_type=F32)


def onehot(idx, width):
    lanes = lax.broadcasted_iota(jnp.int32, (idx.shape[0], width), 1)
    return jnp.where(idx == lanes, 1.0, 0.0).astype(BF)


def rows_of(nwl):
    return -(-(nwl * WROW + 16) // 64) * 64


def tens(v):
    return sum((v >= WIN * m).astype(jnp.int32) for m in range(1, WIN))


def column(n):
    return lax.broadcasted_iota(jnp.int32, (n, 1), 0)


def lane_row(n):
    return lax.broadcasted_iota(jnp.int32, (1, n), 1)


def strip_places():
    d = column(STRIP)
    a = sum((d >= SEG * m).astype(jnp.int32) for m in range(1, SHIFT))
    return a, d - SEG * a


def window_places(rows, nwl):
    r = column(rows)
    j = sum((r >= WROW * m).astype(jnp.int32) for m in range(1, nwl + 1))
    return j, r - WROW * j


def strip_from_slab(nwl):
    a, c = strip_places()
    return jnp.where(c < nwl * WIN, a * (NBLK * COLBLK) + c, -1000)


def window_from(rows, nwl, low, row_width):
    j, i = window_places(rows, nwl)
    a = tens(i)
    found = (a - (SHIFT if low else 0)) * row_width + WIN * j + i - WIN * a
    first = TOKENS // 2 if low else 0
    ok = (i >= first) & (i < first + TOKENS // 2) & (j < nwl)
    return jnp.where(ok, found, -1000)


def strip_from_window(nwl, low):
    a, c = strip_places()
    j = tens(c)
    found = j * WROW + (a + (SHIFT if low else 0)) * WIN + c - WIN * j
    return jnp.where(c < nwl * WIN, found, -1000)


def pick_rows(places, source):
    return dot(onehot(places, source.shape[0]), source).astype(BF)


KERNEL_US = {
    "head": 3.0,
    "rest": 5.0,
    "attn_fwd": 14.0,
    "mlp_first": 9.0,
    "mlp_mid": 5.0,
    "mlp_last": 5.0,
    "attn_bwd_3": 7.0,
    "attn_bwd_2": 7.0,
    "attn_bwd_01": 11.0,
    "final": 1.0,
}


def cost(name):
    return pl.CostEstimate(
        flops=int(KERNEL_US.get(name, 0.01) * COST_RATE), bytes_accessed=1024, transcendentals=0
    )


def vspec():
    return pl.BlockSpec(memory_space=pltpu.VMEM)


def after(x, *others):
    return lax.optimization_barrier((x, *others))[0]


def pinned(x):
    return pltpu.with_memory_space_constraint(x, pltpu.HBM)


def call(kernel, args, outs, scratch=(), scalars=(), hbm=0, hbm_out=0, pin=True, name=None):
    in_hbm = pl.BlockSpec(memory_space=pltpu.HBM)
    return pl.pallas_call(
        kernel,
        out_shape=[jax.ShapeDtypeStruct(s, d) for s, d in outs],
        in_specs=[pl.BlockSpec(memory_space=pltpu.SMEM) for _ in scalars]
        + [in_hbm if i < hbm else vspec() for i in range(len(args))],
        out_specs=[in_hbm if i < hbm_out else vspec() for i in range(len(outs))],
        scratch_shapes=list(scratch),
        compiler_params=pltpu.CompilerParams(vmem_limit_bytes=VMEM_OF.get(name, VMEM_LIMIT) * 2**20),
        cost_estimate=cost(name),
        name=name,
    )(*scalars, *[pinned(a) if pin else a for a in args[:hbm]], *args[hbm:])


def first_column(width):
    c = lax.axis_index("tp") * width + SHIFT
    off = lax.rem(c, COLBLK)
    return c - off, off


def slab_copies(field, half, start, slab, sems, k):
    main = (NBLK - 1) * COLBLK
    last = lax.rem(start + main, field.shape[1])
    rows = pl.ds(half * SHIFT, SHIFT)
    return [
        pltpu.make_async_copy(
            field.at[rows, pl.ds(pl.multiple_of(start, COLBLK), main), :],
            slab.at[:, :main, :],
            sems.at[k],
        ),
        pltpu.make_async_copy(
            field.at[rows, pl.ds(pl.multiple_of(last, COLBLK), COLBLK), :],
            slab.at[:, main:, :],
            sems.at[k + 1],
        ),
    ]


def head_kernel(width, x, wqkv, wproj, table, bias, strip, pack, slab, sems):
    start, off = first_column(width)
    rows = slab_copies(x, 0, start, slab, sems, 0)
    copies = [pltpu.make_async_copy(wqkv, pack.at[: 3 * D, :], sems.at[2])]
    for c in range(D // LANES):
        at = 3 * D + c * LANES
        copies.append(
            pltpu.make_async_copy(
                wproj.at[:, c * LANES : (c + 1) * LANES], pack.at[at : at + LANES, :], sems.at[3 + c]
            )
        )
    for copy in rows + copies:
        copy.start()
    row = lax.broadcasted_iota(jnp.int32, (TABLE, TABLE_PAD), 0)
    lane = lax.broadcasted_iota(jnp.int32, (TABLE, TABLE_PAD), 1)
    flip = jnp.where(row + lane == TABLE - 1, 1.0, 0.0).astype(BF)
    rev = dot(table[...], flip)
    lines = [rev[:, c * LANES : (c + 1) * LANES] for c in range(TABLE_PAD // LANES)]
    lines += [bias[...].astype(F32), jnp.zeros((PACK1 - 4 * D - 14, LANES), F32)]
    pack[4 * D :, :] = jnp.concatenate(lines, axis=0).astype(BF)
    hot = onehot(strip_from_slab(width // WIN) + off, SLAB)
    for copy in rows:
        copy.wait()
    strip[...] = dot(hot, slab[...].reshape(SLAB, D)).astype(BF)
    for copy in copies:
        copy.wait()


def rest_kernel(width, x, g, up, down, ubias, strip_g, win_x, win_g, pack, slabs, sems):
    start, off = first_column(width)
    rows = []
    for k, (field, half) in enumerate(((g, 0), (x, 1), (g, 1))):
        rows.append(slab_copies(field, half, start, slabs.at[k], sems, 2 * k))
    copies = [
        pltpu.make_async_copy(up, pack.at[:D, :], sems.at[6]),
        pltpu.make_async_copy(down, pack.at[D : 2 * D, :], sems.at[7]),
    ]
    for copy in sum(rows, []) + copies:
        copy.start()
    pack[2 * D :, :] = jnp.broadcast_to(ubias[...], (PACK2 - 2 * D, D))
    nwl = width // WIN
    wide = window_from(win_x.shape[0], nwl, False, NBLK * COLBLK)
    hots = [onehot(strip_from_slab(nwl) + off, SLAB), onehot(wide + off, SLAB)]
    for k, out in enumerate((strip_g, win_x, win_g)):
        for copy in rows[k]:
            copy.wait()
        out[...] = dot(hots[min(k, 1)], slabs[k].reshape(SLAB, D)).astype(BF)
    for copy in copies:
        copy.wait()


def norm_stats(x):
    mean = jnp.mean(x, axis=-1, keepdims=True)
    center = x - mean
    spread = jnp.mean(center * center, axis=-1, keepdims=True)
    inv = lax.rsqrt(spread + NORM_EPS)
    return center * inv, inv


def norm_back(dz, n, inv, gain):
    gz = dz * gain
    m1 = jnp.mean(gz, axis=-1, keepdims=True)
    m2 = jnp.mean(gz * n, axis=-1, keepdims=True)
    return (gz - m1 - n * m2) * inv


def row_chunks(rows, count):
    size = rows // count
    return [(c * size, size) for c in range(count)]


def head_masks():
    lane = lax.broadcasted_iota(jnp.int32, (1, LANES), 1)
    return [(lane >= h * HD) & (lane < (h + 1) * HD) for h in range(HEADS_HERE)]


def stacked(x, masks):
    return jnp.concatenate([jnp.where(m, x, jnp.zeros_like(x)) for m in masks], axis=0)


def unstacked(y, masks):
    total = jnp.where(masks[0], y[:WROW], 0.0)
    for h in range(1, HEADS_HERE):
        total = jnp.where(masks[h], y[h * WROW : (h + 1) * WROW], total)
    return total


def attn_fwd_kernel(nwl, bounds, *refs):
    packs, (upx, recv, vecs) = refs[:TP], refs[TP : TP + 3]
    refs = refs[TP + 3 :]
    qkv, probs, o_out = refs[:TP], refs[TP : 2 * TP], refs[2 * TP : 3 * TP]
    x_out, z1_out, hs_out, z2_out, bias_sc, roll_sc, row_sc, w_sc, small_sc, fm = refs[3 * TP : 3 * TP + 10]
    x_sc, z1_sc, qkv_sc, p_sc, o_sc, sems = refs[3 * TP + 10 :]
    rows = x_out.shape[0]
    smalls, weights, projs = [], [], []
    for s in range(TP):
        lanes = slice(s * LANES, (s + 1) * LANES)
        smalls.append(
            pltpu.make_async_copy(packs[s].at[4 * D :, :], small_sc.at[s], sems.at[8 * s])
        )
        for m in range(3):
            weights.append(
                pltpu.make_async_copy(
                    packs[s].at[m * D : (m + 1) * D, :], w_sc.at[m, :, lanes], sems.at[8 * s + 1 + m]
                )
            )
        for c in range(D // LANES):
            projs.append(
                pltpu.make_async_copy(
                    packs[s].at[3 * D + c * LANES : 3 * D + (c + 1) * LANES, :],
                    w_sc.at[3, lanes, c * LANES : (c + 1) * LANES],
                    sems.at[8 * s + 4 + c],
                )
            )
    for copy in smalls + weights + projs:
        copy.start()
    is_end = jnp.where(bounds[0, 1] == lax.axis_index("rows"), 1.0, 0.0)
    last = jnp.where(lax.axis_index("tp") == TP - 1, 1.0, 0.0)
    g1, b1, g2, b2, bp = (vecs[i : i + 1, :] for i in range(5))

    for copy in smalls:
        copy.wait()
    table = jnp.concatenate(
        [
            jnp.concatenate(
                [small_sc[s, 4 * c : 4 * c + 4, :].astype(F32) for c in range(TABLE_PAD // LANES)],
                axis=1,
            )
            for s in range(TP)
        ],
        axis=0,
    )
    for i in range(TOKENS):
        shift = TABLE_PAD - REACH + SPAN * (i // WIN) + i % WIN
        rolled = pltpu.roll(table, shift, 1)
        roll_sc[i * TP * HEADS_HERE : (i + 1) * TP * HEADS_HERE, :] = rolled[:, : 2 * LANES].astype(BF)
    n16 = TOKENS * TP * HEADS_HERE
    lane = lane_row(LANES)
    at_lane = jnp.where(lane < TOKENS, lane + (SPAN - WIN) * tens(lane), -1000)
    spread = jnp.where(column(2 * LANES) == at_lane, 1.0, 0.0).astype(BF)
    row_sc[:n16, :] = dot(roll_sc[...], spread)
    row_sc[n16:, :] = jnp.zeros((WROW * TP * HEADS_HERE - n16, LANES), F32)
    row = column(WROW)
    real = (row < TOKENS) & (lane < TOKENS)
    low_differ = ((row >= TOKENS // 2) != (lane >= TOKENS // 2)) & real
    right_differ = ((row - WIN * tens(row) >= SHIFT) != (lane - WIN * tens(lane) >= SHIFT)) & real
    extra = jnp.where(lane < TOKENS, 0.0, HIDDEN_KEY) + jnp.where(low_differ, MASKED * is_end, 0.0)
    fm[...] = jnp.where(right_differ, MASKED * last, 0.0)
    for s in range(TP):
        for h in range(HEADS_HERE):
            rows_h = row_sc[pl.ds(s * HEADS_HERE + h, WROW, TP * HEADS_HERE), :]
            bias_sc[s, h * WROW : (h + 1) * WROW, :] = rows_h + extra

    places = window_from(rows, nwl, True, SEG)
    for r0, n in row_chunks(rows, 4):
        x = upx[r0 : r0 + n, :].astype(F32) + dot(onehot(places[r0 : r0 + n, :], STRIP), recv[...])
        x_sc[r0 : r0 + n, :] = x.astype(BF)
        z, _ = norm_stats(x)
        z1_sc[r0 : r0 + n, :] = (z * g1 + b1).astype(BF)
    outgoing = loads([x_sc, z1_sc], [x_out, z1_out], sems, 8 * TP)
    scale = HD ** (-0.5)
    for copy in weights:
        copy.wait()
    for m in range(3):
        for r0, n in row_chunks(rows, 2):
            y = dot(z1_sc[r0 : r0 + n, :], w_sc[m])
            for s in range(TP):
                part = y[:, s * LANES : (s + 1) * LANES]
                if m == 0:
                    part = (part + small_sc[s, 12:13, :].astype(F32)) * scale
                if m == 2:
                    part = part + small_sc[s, 13:14, :].astype(F32)
                qkv_sc[s, m, r0 : r0 + n, :] = part.astype(BF)
    outgoing += loads([qkv_sc.at[s] for s in range(TP)], qkv, sems, 8 * TP + 2)
    for s in range(TP):
        o_sc[s, nwl * WROW :, :] = jnp.zeros((rows - nwl * WROW, LANES), BF)

    def window(j, carry):
        masks = head_masks()
        base = pl.multiple_of(j * WROW, 16)
        flag = jnp.where(j == nwl - 1, 1.0, 0.0)
        fm4 = jnp.concatenate([fm[...] * flag] * HEADS_HERE, axis=0)
        for s in range(TP):
            q = qkv_sc[s, 0, pl.ds(base, WROW), :]
            k = qkv_sc[s, 1, pl.ds(base, LANES), :]
            v = qkv_sc[s, 2, pl.ds(base, LANES), :]
            sco = dot_nt(stacked(q, masks), k) + bias_sc[s] + fm4
            top = jnp.max(sco, axis=-1, keepdims=True)
            e = jnp.exp(sco - top)
            total = jnp.sum(e, axis=-1, keepdims=True)
            p = (e / total).astype(BF)
            p_sc[s, j] = p
            o = unstacked(dot(p, v), masks)
            o_sc[s, pl.ds(base, WROW), :] = o.astype(BF)
        return carry

    lax.fori_loop(0, nwl, window, 0, unroll=UNROLL_F)
    outgoing += loads([p_sc.at[s] for s in range(TP)], probs, sems, 8 * TP + 6)
    outgoing += loads([o_sc.at[s] for s in range(TP)], o_out, sems, 8 * TP + 10)
    for copy in projs:
        copy.wait()
    for r0, n in row_chunks(rows, 2):
        o = jnp.concatenate([o_sc[s, r0 : r0 + n, :] for s in range(TP)], axis=1)
        acc = x_sc[r0 : r0 + n, :].astype(F32) + bp + dot(o, w_sc[3])
        hs_out[r0 : r0 + n, :] = acc
        z, _ = norm_stats(acc)
        z2_out[r0 : r0 + n, :] = (z * g2 + b2).astype(BF)
    for copy in outgoing:
        copy.wait()


def bits_in_order(blocks, down):
    bits = [1 << k for k in range(blocks.bit_length() - 1)]
    return bits[1::-1] + bits[2:] if down else bits


def my_block(blocks, down=False):
    w = lax.axis_index("rows")
    mine = 0
    for bit in bits_in_order(blocks, down):
        mine = mine * 2 + lax.rem(lax.div(w, bit), 2)
    return mine


def store_blocks(out, r0, value, blocks, cols=None, down=False):
    size = value.shape[0] // blocks
    mine = my_block(blocks, down)
    for b in range(blocks):
        at = pl.multiple_of(r0 + jnp.bitwise_xor(mine, b) * size, size)
        part = value[b * size : (b + 1) * size, :]
        if cols is None:
            out[pl.ds(at, size), :] = part
        else:
            out[pl.ds(at, size), cols[0] : cols[1]] = part


def mlp_kernel(ns, first, last, nwl, blocks, *refs):
    refs = list(refs)
    packs = refs[:ns]
    if first:
        held, sems = refs[-2:]
        copies = loads(packs[:1], [held], sems)
        packs, refs = [held] + packs[1:], refs[:-2]
    z2 = refs[ns]
    refs = refs[ns + 1 :]
    if first:
        gup, grecv = refs[:2]
        refs = refs[2:]
    else:
        gs, y_in, z_in = refs[:3]
        refs = refs[3:]
    if last:
        hs, vecs = refs[:2]
        refs = refs[2:]
    grads, dub = refs[:ns], refs[ns]
    refs = refs[ns + 1 :]
    if first:
        gs = refs.pop(0)
    if last:
        out_up, out_low, dh_out, dhb_out, vec_out = refs[:5]
        refs = refs[5:]
    acc_y, acc_z, act_sc, du_sc = refs
    rows = z2.shape[0]
    if first:
        places = window_from(rows, nwl, True, SEG)
        for r0, n in row_chunks(rows, 4):
            gs[r0 : r0 + n, :] = (
                gup[r0 : r0 + n, :].astype(F32)
                + dot(onehot(places[r0 : r0 + n, :], STRIP), grecv[...])
            ).astype(BF)
    for k in range(ns):
        if first and k == 0:
            copies[k].wait()
        ub = packs[k][2 * D : 2 * D + 1, :].astype(F32)
        dub_total = jnp.zeros((1, D), F32)
        for r0, n in row_chunks(rows, 2):
            sl = slice(r0, r0 + n)
            u = dot(z2[sl, :], packs[k][:D, :]) + ub
            phi = 0.5 * (1.0 + lax.erf(u * np.float32(np.sqrt(0.5))))
            act = (u * phi).astype(BF)
            slope = phi + u * (jnp.exp(-0.5 * u * u) * np.float32(1 / np.sqrt(2 * np.pi)))
            act_sc[sl, :] = act
            ga = dot_nt(gs[sl, :], packs[k][D : 2 * D, :])
            du = (slope * ga).astype(BF)
            du_sc[sl, :] = du
            dub_total += jnp.sum(du.astype(F32), axis=0, keepdims=True)
            y = dot(act, packs[k][D : 2 * D, :])
            z = dot_nt(du, packs[k][:D, :])
            if k > 0:
                acc_y[sl, :] += y
                acc_z[sl, :] += z
            elif first:
                acc_y[sl, :] = y
                acc_z[sl, :] = z
            else:
                acc_y[sl, :] = y + y_in[sl, :]
                acc_z[sl, :] = z + z_in[sl, :]
        for c in range(D // LANES):
            line = k * (D // LANES) + c
            dub[line : line + 1, :] = dub_total[:, c * LANES : (c + 1) * LANES]
        store_blocks(grads[k], 0, dot_tn(act_sc[...], gs[...]).astype(BF), blocks, down=True)
        store_blocks(grads[k], D, dot_tn(z2[...], du_sc[...]).astype(BF), blocks)
    if not last:
        return
    g2, bd = vecs[2:3, :], vecs[5:6, :]
    sums = [jnp.zeros((1, D), F32) for _ in range(4)]
    for r0, n in row_chunks(rows, 4):
        sl = slice(r0, r0 + n)
        dz = acc_z[sl, :]
        g = gs[sl, :].astype(F32)
        h = hs[sl, :]
        nrm, inv = norm_stats(h)
        dh = g + norm_back(dz, nrm, inv, g2)
        dh_out[sl, :] = dh
        dhb_out[sl, :] = dh.astype(BF)
        act_sc[sl, :] = (h + acc_y[sl, :] + bd).astype(BF)
        for i, term in enumerate((dz * nrm, dz, g, dh)):
            sums[i] = sums[i] + jnp.sum(term, axis=0, keepdims=True)
    vec_out[...] = jnp.concatenate(sums, axis=0)
    out_up[...] = pick_rows(strip_from_window(nwl, False), act_sc[...])
    out_low[...] = pick_rows(strip_from_window(nwl, True), act_sc[...])


def loads(sources, targets, sems, at=0):
    copies = [
        pltpu.make_async_copy(x, y, sems.at[at + i]) for i, (x, y) in enumerate(zip(sources, targets))
    ]
    for copy in copies:
        copy.start()
    return copies


def attn_bwd_kernel(ns, nwl, blocks, last, *refs):
    refs = list(refs)

    def take(n):
        found = refs[:n]
        del refs[:n]
        return found

    n_in = 4 * ns + (TP - ns if last else 0)
    sources = take(n_in)
    dhb, z1 = take(2)
    if last:
        tail = take(11)
    grads = take(ns)
    if last:
        tail += take(3)
    dpos, *dx_sc = take(1 + ns)
    if last:
        tail += take(2)
    dsum, do_sc = take(2)
    held = take(n_in)
    (sems,) = refs
    copies = loads(sources, held, sems)
    packs, o, qkv, probs = (held[i * ns : (i + 1) * ns] for i in range(4))
    rows = dhb.shape[0]
    scale = HD ** (-0.5)
    masks = head_masks()
    lin = column(LANES)
    lin = jnp.where(lin < TOKENS, REACH - lin - (SPAN - WIN) * tens(lin), -1000)
    back = onehot(lin, TABLE_PAD)
    place = lane_row(STACK)
    head = sum((place >= WROW * m).astype(jnp.int32) for m in range(1, HEADS_HERE))
    place = place - WROW * head
    line = jnp.where(place < TOKENS, tens(place) * 8 + head, -1000)
    groups = jnp.where(column(WIN * 8) == line, 1.0, 0.0).astype(BF)
    for k in range(ns):
        copies[k].wait()
        total = None
        for c in range(D // LANES):
            w = packs[k][3 * D + c * LANES : 3 * D + (c + 1) * LANES, :]
            term = dot_nt(dhb[:, c * LANES : (c + 1) * LANES], w)
            total = term if total is None else total + term
        do_sc[k] = total.astype(BF)
        copies[ns + k].wait()
        gp = dot_tn(o[k][...], dhb[...]).astype(BF)
        gp = jnp.concatenate([gp[:, c * LANES : (c + 1) * LANES] for c in range(D // LANES)], axis=0)
        store_blocks(grads[k], 0, gp, blocks, (3 * LANES, 4 * LANES))
        dx_sc[k][nwl * WROW :, :] = jnp.zeros((rows - nwl * WROW, 3 * LANES), BF)
        dsum[k] = jnp.zeros(dsum.shape[1:], F32)
        copies[2 * ns + k].wait()
        copies[3 * ns + k].wait()

        def window(j, carry, k=k):
            base = pl.multiple_of(j * WROW, 16)
            q = stacked(qkv[k][0, pl.ds(base, WROW), :], masks)
            key = qkv[k][1, pl.ds(base, LANES), :]
            v = qkv[k][2, pl.ds(base, LANES), :]
            do = stacked(do_sc[k, pl.ds(base, WROW), :], masks)
            p = probs[k][j]
            p32 = p.astype(F32)
            pdp = p32 * dot_nt(do, v)
            ds = (pdp - p32 * jnp.sum(pdp, axis=-1, keepdims=True)).astype(BF)
            dsum[k] += ds.astype(F32)
            dv = dot_tn(p, do)
            dk = dot_tn(ds, q)
            dq = unstacked(dot(ds, key), masks) * scale
            dx_sc[k][pl.ds(base, WROW), :LANES] = dq.astype(BF)
            dx_sc[k][pl.ds(base, WROW), LANES : 2 * LANES] = dk[:WROW].astype(BF)
            dx_sc[k][pl.ds(base, WROW), 2 * LANES :] = dv[:WROW].astype(BF)
            return carry

        lax.fori_loop(0, nwl, window, 0, unroll=UNROLL)
    for k in range(ns):
        store_blocks(grads[k], 0, dot_tn(z1[...], dx_sc[k][...]).astype(BF), blocks, (0, 3 * LANES))
        high = dsum[k].astype(BF)
        low = (dsum[k] - high.astype(F32)).astype(BF)
        lanes = dot(high, back) + dot(low, back)
        turned = jnp.concatenate(
            [
                pltpu.roll(lanes[h * WROW : (h + 1) * WROW, :], 0, 1, stride=1, stride_axis=0)
                for h in range(HEADS_HERE)
            ],
            axis=0,
        )
        high = turned.astype(BF)
        low = (turned - high.astype(F32)).astype(BF)
        summed = dot(groups, high) + dot(groups, low)
        total = summed[:8, :]
        for a in range(1, WIN):
            total = total + pltpu.roll(summed[a * 8 : (a + 1) * 8, :], (SPAN - WIN) * a, 1)
        per = 16
        for h in range(HEADS_HERE):
            for c in range(TABLE_PAD // LANES):
                line = k * per + h * (TABLE_PAD // LANES) + c
                dpos[line : line + 1, :] = total[h : h + 1, c * LANES : (c + 1) * LANES]
        for i, m in enumerate((0, 2)):
            part = dx_sc[k][:, m * LANES : (m + 1) * LANES].astype(F32)
            line = k * per + 12 + i
            dpos[line : line + 1, :] = jnp.sum(part, axis=0, keepdims=True)
        dpos[k * per + 14 : (k + 1) * per, :] = jnp.zeros((2, LANES), F32)
    if last:
        for copy in copies[4 * ns :]:
            copy.wait()
        end_of_backward(nwl, dx_sc, packs + held[4 * ns :], dpos, *tail)


def end_of_backward(nwl, dxs, packs, small01, *refs):
    dx2, dx3, x_ref, dh, vecs, vec_mlp, small3, small2, dub01, dub2, dub3 = refs[:11]
    out_up, out_low, small_out, small_f32, dz = refs[11:]
    rows = x_ref.shape[0]
    parts = list(zip(dxs + [dx2, dx3], packs))
    weights = [
        jnp.concatenate([pack[m * D : (m + 1) * D, :] for m in range(3)], axis=1) for _, pack in parts
    ]
    sums = [jnp.zeros((1, D), F32) for _ in range(2)]
    for r0, n in row_chunks(rows, 2):
        sl = slice(r0, r0 + n)
        total = None
        for (dx, _), weight in zip(parts, weights):
            term = dot_nt(dx[sl, :], weight)
            total = term if total is None else total + term
        nrm, inv = norm_stats(x_ref[sl, :].astype(F32))
        dz[sl, :] = (dh[sl, :] + norm_back(total, nrm, inv, vecs[0:1, :])).astype(BF)
        sums[0] = sums[0] + jnp.sum(total * nrm, axis=0, keepdims=True)
        sums[1] = sums[1] + jnp.sum(total, axis=0, keepdims=True)
    t = lax.axis_index("tp")
    pieces = [
        (small01[:16, :], dub01[:4, :]),
        (small01[16:, :], dub01[4:, :]),
        (small2[...], dub2[...]),
        (small3[...], dub3[...]),
    ]
    for s, (lines, dub) in enumerate(pieces):
        at = pl.multiple_of(jnp.bitwise_xor(t, s) * LANES, LANES)
        both = jnp.concatenate([lines, dub, jnp.zeros((4, LANES), F32)], axis=0)
        small_f32[: SMALL_SHARD, pl.ds(at, LANES)] = both
    small_f32[SMALL_SHARD:, :] = jnp.concatenate(
        [vec_mlp[...]] + sums + [jnp.zeros((SMALL_ROWS - SMALL_SHARD - 6, D), F32)], axis=0
    )
    small_out[...] = small_f32[...].astype(BF)
    out_up[...] = pick_rows(strip_from_window(nwl, False), dz[...])
    out_low[...] = pick_rows(strip_from_window(nwl, True), dz[...])


def page_kernel(*refs):
    out = refs[TP]
    pw = out.shape[1]
    t = lax.axis_index("tp")
    width = pw // TP
    col = lax.broadcasted_iota(jnp.int32, (pw, 1), 0)
    hots = []
    for s in range(TP):
        v = col - width * jnp.bitwise_xor(t, s) - SHIFT
        v = jnp.where(v < 0, v + pw, v)
        v = jnp.where(v < width, v, -1000)
        hots.append(onehot(v, SEG))
    hot = jnp.concatenate(hots, axis=1)
    for r in range(WIN):
        off = STRIP + r * SEG if r < SHIFT else (r - SHIFT) * SEG
        parts = [ul[off : off + SEG, :] for ul in refs[:TP]]
        out[r] = dot(hot, jnp.concatenate(parts, axis=0)).astype(BF)


def swap_tp(x, bit):
    return lax.ppermute(x, "tp", [(i, i ^ bit) for i in range(TP)])


def swap_rows(x, bit):
    return lax.ppermute(x, "rows", [(i, i ^ bit) for i in range(lax.axis_size("rows"))])


def shift_rows(x, distance):
    n = lax.axis_size("rows")
    return lax.ppermute(x, "rows", [(i, (i + distance) % n) for i in range(n)])


def row_bits():
    n = lax.axis_size("rows")
    bits = []
    while 1 << len(bits) < n:
        bits.append(1 << len(bits))
    return bits


def blocks_for(rows):
    blocks = 1
    while 2 * blocks <= lax.axis_size("rows") and rows % (2 * blocks) == 0 and rows // (2 * blocks) >= 16:
        blocks *= 2
    return blocks


def added(arrays):
    total = arrays[0].astype(F32)
    for extra in arrays[1:]:
        total = total + extra.astype(F32)
    return total.astype(BF)


def scatter_step(arrays, bit, blocks):
    total = added(arrays)
    if bit < blocks:
        half = total.shape[0] // 2
        return [total[:half], swap_rows(total[half:], bit)]
    return [total, swap_rows(total, bit)]


def finish_kernel(blocks, gathered, n_in, *refs):
    ins, outs = refs[:n_in], refs[n_in:]
    part = ins[0].shape[0] * n_in // blocks
    each = blocks // n_in
    both = len(outs) == 2
    half = part // 2

    def place(p, down):
        order = bits_in_order(blocks, down)
        moved = sum(
            ((p >> k) & 1) << (len(order) - 1 - order.index(bit)) for k, bit in enumerate(gathered)
        )
        return jnp.bitwise_xor(my_block(blocks, down), moved)

    for p in range(blocks):
        piece = ins[p // each][(p % each) * part : (p % each + 1) * part, :].astype(F32)
        if both:
            for out, value, down in zip(outs, (piece[:half], piece[half:]), (True, False)):
                out[pl.ds(pl.multiple_of(place(p, down) * half, half), half), :] = value
        else:
            outs[2][pl.ds(pl.multiple_of(place(p, False) * part, part), part), :] = piece
    if both:
        return
    qkv, proj, whole = outs
    for c in range(D // LANES):
        if c < 3:
            qkv[c] = whole[:, c * LANES : (c + 1) * LANES]
        proj[:, c * LANES : (c + 1) * LANES] = whole[c * LANES : (c + 1) * LANES, 3 * LANES :]


def finish(pieces, blocks, gathered, name):
    attn = name == "finish_attn"
    return call(
        functools.partial(finish_kernel, blocks, gathered, len(pieces)),
        pieces,
        [((3, D, LANES), F32), ((LANES, D), F32)] if attn else [((D, D), F32)] * 2,
        scratch=[pltpu.VMEM((D, D), F32)] if attn else [],
        name=name,
    )


def interleaved(parts, blocks):
    n = blocks
    cut = [p.reshape(n, 1, p.shape[0] // n, p.shape[1]) for p in parts]
    return jnp.concatenate(cut, axis=1).reshape(-1, parts[0].shape[1])


def riding_step(arrays, small, bit, blocks):
    total = added(arrays)
    small = added(small)
    half = total.shape[0] // 2 if bit < blocks else total.shape[0]
    got = swap_rows(jnp.concatenate([total[-half:], small], axis=0), bit)
    return [total[:half], got[:half]], [small, got[half:]]


def small_kernel(*refs):
    ins, outs = refs[:TP], refs[TP:]
    total = ins[0][2 * STRIP :, :].astype(F32)
    for r in ins[1:]:
        total += r[2 * STRIP :, :].astype(F32)
    for i in range(6):
        outs[i][...] = total[SMALL_SHARD + i : SMALL_SHARD + i + 1, :]
    t = lax.axis_index("tp")
    mine = jnp.zeros((SMALL_SHARD, LANES), F32)
    for a in range(TP):
        mine = jnp.where(t == a, total[:SMALL_SHARD, a * LANES : (a + 1) * LANES], mine)
    qvb, up, table = outs[6:]
    qvb[...] = mine[12:14, :]
    up[...] = mine[16:20, :]
    per = TABLE_PAD // LANES
    for h in range(HEADS_HERE):
        line = jnp.concatenate([mine[h * per + c : h * per + c + 1, :] for c in range(per)], axis=1)
        table[h : h + 1, :] = line[:, :TABLE]


def page(pieces, page_shape, name):
    return call(page_kernel, pieces, [(page_shape, BF)], name=name)[0]


def per_device(
    patches,
    cotangent,
    page_bounds,
    attn_gain,
    attn_shift,
    qkv_weight,
    qv_bias,
    pos_table,
    proj_weight,
    proj_bias,
    mlp_gain,
    mlp_shift,
    up_weight,
    up_bias,
    down_weight,
    down_bias,
):
    t = lax.axis_index("tp")
    pw = patches.shape[1]
    nwl = pw // WIN // TP
    width = nwl * WIN
    rows = rows_of(nwl)
    bits = row_bits()
    blocks = blocks_for(D)

    vecs = jnp.stack([attn_gain, attn_shift, mlp_gain, mlp_shift, proj_bias, down_bias]).astype(F32)
    slab = (SHIFT, NBLK * COLBLK, D)
    strip_x, pack1 = call(
        functools.partial(head_kernel, width),
        [patches, qkv_weight.reshape(3 * D, LANES), proj_weight, pos_table.T, qv_bias],
        [((STRIP, D), BF), ((PACK1, LANES), BF)],
        scratch=[
            pltpu.VMEM(slab, BF),
            pltpu.SemaphoreType.DMA((7,)),
        ],
        hbm=3,
        name="head",
    )
    recv_x = shift_rows(strip_x, -1)
    pack1_x = swap_tp(pack1, 2)
    pack1_c = swap_tp(pack1, 1)
    strip_g, up_x, up_g, pack2 = call(
        functools.partial(rest_kernel, width),
        [patches, after(cotangent, strip_x, vecs), up_weight, down_weight, up_bias[None]],
        [((STRIP, D), BF), ((rows, D), BF), ((rows, D), BF), ((PACK2, D), BF)],
        scratch=[
            pltpu.VMEM((3,) + slab, BF),
            pltpu.SemaphoreType.DMA((8,)),
        ],
        hbm=4,
        name="rest",
    )
    recv_g = shift_rows(strip_g, -1)
    pack1_cx = swap_tp(after(pack1_x, strip_g, recv_x, pack1_c), 1)
    packs1 = [pack1, pack1_c, pack1_x, pack1_cx]
    pack2_x = swap_tp(after(pack2, pack1_x), 2)
    pack2_c = swap_tp(pack2, 1)

    outs = call(
        functools.partial(attn_fwd_kernel, nwl),
        packs1 + [up_x, recv_x, vecs],
        [((3, rows, LANES), BF)] * TP
        + [((nwl, STACK, LANES), BF)] * TP
        + [((rows, LANES), BF)] * TP
        + [((rows, D), BF), ((rows, D), BF), ((rows, D), F32), ((rows, D), BF)],
        scratch=[
            pltpu.VMEM((TP, STACK, LANES), F32),
            pltpu.VMEM((TOKENS * TP * HEADS_HERE, 2 * LANES), BF),
            pltpu.VMEM((WROW * TP * HEADS_HERE, LANES), F32),
            pltpu.VMEM((4, D, D), BF),
            pltpu.VMEM((TP, PACK1 - 4 * D, LANES), BF),
            pltpu.VMEM((WROW, LANES), F32),
            pltpu.VMEM((rows, D), BF),
            pltpu.VMEM((rows, D), BF),
            pltpu.VMEM((TP, 3, rows, LANES), BF),
            pltpu.VMEM((TP, nwl, STACK, LANES), BF),
            pltpu.VMEM((TP, rows, LANES), BF),
            pltpu.SemaphoreType.DMA((8 * TP + 2 + 3 * TP,)),
        ],
        scalars=[page_bounds],
        hbm=TP,
        hbm_out=3 * TP + 2,
        pin=False,
        name="attn_fwd",
    )
    qkv, probs, o = outs[:TP], outs[TP : 2 * TP], outs[2 * TP : 3 * TP]
    x_win, z1, hs, z2 = outs[3 * TP :]

    def mlp(packs, extra, first, last):
        ns = len(packs)
        outs = [((2 * D, D), BF)] * ns + [((ns * D // LANES, LANES), F32)]
        if first:
            outs += [((rows, D), BF)]
        if last:
            outs += [((STRIP, D), BF)] * 2 + [((rows, D), F32), ((rows, D), BF), ((4, D), F32)]
        accs = [((rows, D), F32)] * 2
        return call(
            functools.partial(mlp_kernel, ns, first, last, nwl, blocks),
            packs + [z2] + extra,
            outs if last else outs + accs,
            scratch=([pltpu.VMEM(*a) for a in accs] if last else [])
            + [pltpu.VMEM((rows, D), BF)] * 2
            + ([pltpu.VMEM((PACK2, D), BF), pltpu.SemaphoreType.DMA((1,))] if first else []),
            hbm=1 if first else 0,
            name="mlp_last" if last else "mlp_first" if first else "mlp_mid",
        )

    g0, g1, dub01, gs, acc_y, acc_z = mlp([pack2, pack2_c], [up_g, recv_g], True, False)
    got_g1 = swap_tp(g1, 1)
    pack2_cx = swap_tp(after(pack2_x, acc_y), 1)
    g2, dub2, acc_y, acc_z = mlp([pack2_x], [gs, acc_y, acc_z], False, False)
    g3, dub3, up_y, low_y, dh, dhb, vec_mlp = mlp(
        [pack2_cx],
        [gs, acc_y, acc_z, hs, vecs],
        False,
        True,
    )
    got_g3 = swap_tp(g3, 1)
    lower_y = shift_rows(low_y, 1)

    def attn_bwd(shards, dhb, tail=()):
        ns = len(shards)
        loaded = [a[s] for a in (packs1, o, qkv, probs) for s in shards]
        outs = [((D, D), BF)] * ns
        parts = [((ns * 16, LANES), F32)] + [((rows, 3 * LANES), BF)] * ns
        scratch = []
        if tail:
            loaded += [packs1[s] for s in range(TP) if s not in shards]
            outs += [((STRIP, D), BF)] * 2 + [((SMALL_ROWS, D), BF)]
            scratch = [pltpu.VMEM(*p) for p in parts]
            scratch += [pltpu.VMEM((SMALL_ROWS, D), F32), pltpu.VMEM((rows, D), BF)]
        else:
            outs += parts
        return call(
            functools.partial(attn_bwd_kernel, ns, nwl, blocks, bool(tail)),
            loaded + [dhb, z1, *tail],
            outs,
            scratch=scratch
            + [pltpu.VMEM((ns, STACK, LANES), F32), pltpu.VMEM((ns, rows, LANES), BF)]
            + [pltpu.VMEM(a.shape, a.dtype) for a in loaded]
            + [pltpu.SemaphoreType.DMA((len(loaded),))],
            hbm=len(loaded),
            name="attn_bwd_" + "".join(map(str, shards)),
        )

    a3, small3, dx3 = attn_bwd((3,), dhb)
    got_a3 = swap_tp(a3, 1)
    across_d = added([g2[:D], after(got_g3, a3)[:D]])
    got_dx = swap_tp(across_d, 2)
    up0 = added([after(g0, across_d)[D:], got_g1[D:]])
    up2 = added([g2[D:], got_g3[D:]])
    half = D // 2
    up_got = swap_rows(jnp.concatenate([up0[half:], up2[half:]], axis=0), bits[0])
    a2, small2, dx2 = attn_bwd((2,), after(dhb, across_d, up0, up2))
    across_a = added([a2, got_a3])
    got_ax = swap_tp(across_a, 2)
    a0, a1, up_g, low_g, small = attn_bwd(
        (0, 1),
        after(dhb, across_a),
        (dx2, dx3, x_win, dh, vecs, vec_mlp, small3, small2, dub01, dub2, dub3),
    )
    lower_g = shift_rows(low_g, 1)
    got_a1 = swap_tp(a1, 1)
    page_own = jnp.concatenate([after(up_y, a2), lower_y], axis=0)
    from_c = swap_tp(page_own, 1)

    up_got = after(up_got, a0)
    up0 = added([up0[:half], up_got[:half]])
    up2 = added([up2[:half], up_got[half:]])
    up_x = swap_tp(up2, 2)
    down = scatter_step([after(g0, up2)[:D], after(got_g1, up2)[:D], got_dx], bits[1], blocks)

    attn = [after(a0, up2, down[0]), got_a1, got_ax]
    small = [small]
    mlp = None
    gather_a = [b for b in reversed(bits) if b < blocks]
    gather_m = gather_a[:-2] + gather_a[:-3:-1]
    steps = len(bits) + len(gather_a)
    for i in range(steps):
        if i < len(bits):
            mark = added(attn)
            attn, small = riding_step([mark], small, bits[i], blocks)
        else:
            mark = added(attn) if i == len(bits) else jnp.concatenate(attn, axis=0)
            attn = [mark, swap_rows(mark, gather_a[i - len(bits)])]
        if i == 0:
            down = scatter_step([after(down[0], mark), down[1]], bits[0], blocks)
            up = scatter_step([after(up0, mark), up_x], bits[1], blocks)
            from_x = swap_tp(after(page_own, mark), 2)
        elif i + 1 < steps:
            if i == 1:
                mlp = [added([after(down[0], mark), down[1]]), added([after(up[0], mark), up[1]])]
                mlp = scatter_step([interleaved(mlp, blocks // 4)], bits[2], blocks)
            elif i + 1 < len(bits):
                mlp = scatter_step([after(mlp[0], mark), mlp[1]], bits[i + 1], blocks)
            else:
                kept = after(mlp[0], mark)
                first = i + 1 == len(bits)
                total = added([kept, mlp[1]]) if first else jnp.concatenate([kept, mlp[1]], axis=0)
                mlp = [total, swap_rows(total, gather_m[i + 1 - len(bits)])]
        if i == len(bits):
            small = added([after(small[0], mark), small[1]])
            own_g = jnp.concatenate([up_g, lower_g, small], axis=0)
            g_x = swap_tp(own_g, 2)
            g_c = swap_tp(own_g, 1)
            from_cx = swap_tp(after(from_x, mark), 1)
    g_cx = swap_tp(after(g_x, mark), 1)
    block_out = page([after(page_own, mark), from_c, from_x, from_cx], patches.shape, "page_y")
    grad_patches = page([after(own_g, mark), g_c, g_x, g_cx], patches.shape, "page_g")
    *v, qvb_line, up_line, table = call(
        small_kernel,
        [own_g, g_c, g_x, g_cx],
        [((1, D), F32)] * 6 + [((2, LANES), F32), ((D // LANES, LANES), F32), ((HEADS_HERE, TABLE), F32)],
        name="small",
    )
    attn[0] = after(attn[0], block_out, grad_patches, table)
    grad_qkv, grad_proj = finish(attn, blocks, gather_a, "finish_attn")
    grad_down, grad_up = finish([after(mlp[0], grad_qkv), mlp[1]], blocks, gather_m, "finish_mlp")

    v = [line.reshape(D) for line in v]

    return (
        block_out,
        grad_patches,
        v[4],
        v[5],
        grad_qkv,
        qvb_line,
        table.T,
        grad_proj,
        v[3],
        v[0],
        v[1],
        grad_up,
        up_line.reshape(D),
        grad_down,
        v[2],
    )


def solution(mesh):
    placed = (
        P("rows", None, None),
        P("rows", None, None),
        P("rows", None),
        P(),
        P(),
        P(None, None, "tp"),
        P(None, "tp"),
        P(None, "tp"),
        P("tp", None),
        P(),
        P(),
        P(),
        P(None, "tp"),
        P("tp"),
        P("tp", None),
        P(),
    )
    return jax.shard_map(
        per_device,
        mesh=mesh,
        in_specs=placed,
        out_specs=(
            P("rows", None, None),
            P("rows", None, None),
            P(),
            P(),
            P(None, None, "tp"),
            P(None, "tp"),
            P(None, "tp"),
            P("tp", None),
            P(),
            P(),
            P(),
            P(None, "tp"),
            P("tp"),
            P("tp", None),
            P(),
        ),
        check_vma=False,
    )
```

```python
import functools

import jax
import jax.numpy as jnp
import numpy as np
from jax import lax
from jax.experimental import pallas as pl
from jax.experimental.pallas import tpu as pltpu
from jax.sharding import PartitionSpec as P

D = 512
HD = 32
WIN = 10
SHIFT = 5
TABLE = 361
TABLE_PAD = 384
NORM_EPS = 1e-05
MASKED = -1000000000.0
HIDDEN_KEY = -1e30

TP = 4
HEADS_HERE = 4
LANES = 128
TOKENS = WIN * WIN
WROW = 112
SEG = 64
STRIP = SHIFT * SEG
COLBLK = 16
NBLK = 5
SLAB = SHIFT * NBLK * COLBLK
STACK = HEADS_HERE * WROW
SPAN = 2 * WIN - 1
REACH = SPAN * (WIN - 1) + WIN - 1
PACK1 = 4 * D + 32
SMALL_SHARD = 24
SMALL_ROWS = 32
PACK2 = 2 * D + 16

F32 = jnp.float32
BF = jnp.bfloat16
VMEM_LIMIT = 24
VMEM_OF = {"head": 56, "rest": 56, "attn_fwd": 56}
COST_RATE = 2e8
UNROLL = 2
UNROLL_F = 2


def dot(a, b):
    return lax.dot_general(a, b, (((1,), (0,)), ((), ())), preferred_element_type=F32)


def dot_nt(a, b):
    return lax.dot_general(a, b, (((1,), (1,)), ((), ())), preferred_element_type=F32)


def dot_tn(a, b):
    return lax.dot_general(a, b, (((0,), (0,)), ((), ())), preferred_element_type=F32)


def onehot(idx, width):
    lanes = lax.broadcasted_iota(jnp.int32, (idx.shape[0], width), 1)
    return jnp.where(idx == lanes, 1.0, 0.0).astype(BF)


def rows_of(nwl):
    return -(-(nwl * WROW + 16) // 64) * 64


def tens(v):
    return sum((v >= WIN * m).astype(jnp.int32) for m in range(1, WIN))


def column(n):
    return lax.broadcasted_iota(jnp.int32, (n, 1), 0)


def lane_row(n):
    return lax.broadcasted_iota(jnp.int32, (1, n), 1)


def strip_places():
    d = column(STRIP)
    a = sum((d >= SEG * m).astype(jnp.int32) for m in range(1, SHIFT))
    return a, d - SEG * a


def window_places(rows, nwl):
    r = column(rows)
    j = sum((r >= WROW * m).astype(jnp.int32) for m in range(1, nwl + 1))
    return j, r - WROW * j


def strip_from_slab(nwl):
    a, c = strip_places()
    return jnp.where(c < nwl * WIN, a * (NBLK * COLBLK) + c, -1000)


def window_from(rows, nwl, low, row_width):
    j, i = window_places(rows, nwl)
    a = tens(i)
    found = (a - (SHIFT if low else 0)) * row_width + WIN * j + i - WIN * a
    first = TOKENS // 2 if low else 0
    ok = (i >= first) & (i < first + TOKENS // 2) & (j < nwl)
    return jnp.where(ok, found, -1000)


def strip_from_window(nwl, low):
    a, c = strip_places()
    j = tens(c)
    found = j * WROW + (a + (SHIFT if low else 0)) * WIN + c - WIN * j
    return jnp.where(c < nwl * WIN, found, -1000)


def pick_rows(places, source):
    return dot(onehot(places, source.shape[0]), source).astype(BF)


KERNEL_US = {
    "head": 3.0,
    "rest": 5.0,
    "attn_fwd": 14.0,
    "mlp_first": 9.0,
    "mlp_mid": 5.0,
    "mlp_last": 5.0,
    "attn_bwd_3": 7.0,
    "attn_bwd_2": 7.0,
    "attn_bwd_01": 11.0,
    "final": 1.0,
}


def cost(name):
    return pl.CostEstimate(
        flops=int(KERNEL_US.get(name, 0.01) * COST_RATE), bytes_accessed=1024, transcendentals=0
    )


def vspec():
    return pl.BlockSpec(memory_space=pltpu.VMEM)


def after(x, *others):
    return lax.optimization_barrier((x, *others))[0]


def pinned(x):
    return pltpu.with_memory_space_constraint(x, pltpu.HBM)


def call(kernel, args, outs, scratch=(), scalars=(), hbm=0, hbm_out=0, pin=True, name=None):
    in_hbm = pl.BlockSpec(memory_space=pltpu.HBM)
    return pl.pallas_call(
        kernel,
        out_shape=[jax.ShapeDtypeStruct(s, d) for s, d in outs],
        in_specs=[pl.BlockSpec(memory_space=pltpu.SMEM) for _ in scalars]
        + [in_hbm if i < hbm else vspec() for i in range(len(args))],
        out_specs=[in_hbm if i < hbm_out else vspec() for i in range(len(outs))],
        scratch_shapes=list(scratch),
        compiler_params=pltpu.CompilerParams(vmem_limit_bytes=VMEM_OF.get(name, VMEM_LIMIT) * 2**20),
        cost_estimate=cost(name),
        name=name,
    )(*scalars, *[pinned(a) if pin else a for a in args[:hbm]], *args[hbm:])


def first_column(width):
    c = lax.axis_index("tp") * width + SHIFT
    off = lax.rem(c, COLBLK)
    return c - off, off


def slab_copies(field, half, start, slab, sems, k):
    main = (NBLK - 1) * COLBLK
    last = lax.rem(start + main, field.shape[1])
    rows = pl.ds(half * SHIFT, SHIFT)
    return [
        pltpu.make_async_copy(
            field.at[rows, pl.ds(pl.multiple_of(start, COLBLK), main), :],
            slab.at[:, :main, :],
            sems.at[k],
        ),
        pltpu.make_async_copy(
            field.at[rows, pl.ds(pl.multiple_of(last, COLBLK), COLBLK), :],
            slab.at[:, main:, :],
            sems.at[k + 1],
        ),
    ]


def head_kernel(width, x, wqkv, wproj, table, bias, strip, pack, slab, sems):
    start, off = first_column(width)
    rows = slab_copies(x, 0, start, slab, sems, 0)
    copies = [pltpu.make_async_copy(wqkv, pack.at[: 3 * D, :], sems.at[2])]
    for c in range(D // LANES):
        at = 3 * D + c * LANES
        copies.append(
            pltpu.make_async_copy(
                wproj.at[:, c * LANES : (c + 1) * LANES], pack.at[at : at + LANES, :], sems.at[3 + c]
            )
        )
    for copy in rows + copies:
        copy.start()
    row = lax.broadcasted_iota(jnp.int32, (TABLE, TABLE_PAD), 0)
    lane = lax.broadcasted_iota(jnp.int32, (TABLE, TABLE_PAD), 1)
    flip = jnp.where(row + lane == TABLE - 1, 1.0, 0.0).astype(BF)
    rev = dot(table[...], flip)
    lines = [rev[:, c * LANES : (c + 1) * LANES] for c in range(TABLE_PAD // LANES)]
    lines += [bias[...].astype(F32), jnp.zeros((PACK1 - 4 * D - 14, LANES), F32)]
    pack[4 * D :, :] = jnp.concatenate(lines, axis=0).astype(BF)
    hot = onehot(strip_from_slab(width // WIN) + off, SLAB)
    for copy in rows:
        copy.wait()
    strip[...] = dot(hot, slab[...].reshape(SLAB, D)).astype(BF)
    for copy in copies:
        copy.wait()


def rest_kernel(width, x, g, up, down, ubias, strip_g, win_x, win_g, pack, slabs, sems):
    start, off = first_column(width)
    rows = []
    for k, (field, half) in enumerate(((g, 0), (x, 1), (g, 1))):
        rows.append(slab_copies(field, half, start, slabs.at[k], sems, 2 * k))
    copies = [
        pltpu.make_async_copy(up, pack.at[:D, :], sems.at[6]),
        pltpu.make_async_copy(down, pack.at[D : 2 * D, :], sems.at[7]),
    ]
    for copy in sum(rows, []) + copies:
        copy.start()
    pack[2 * D :, :] = jnp.broadcast_to(ubias[...], (PACK2 - 2 * D, D))
    nwl = width // WIN
    wide = window_from(win_x.shape[0], nwl, False, NBLK * COLBLK)
    hots = [onehot(strip_from_slab(nwl) + off, SLAB), onehot(wide + off, SLAB)]
    for k, out in enumerate((strip_g, win_x, win_g)):
        for copy in rows[k]:
            copy.wait()
        out[...] = dot(hots[min(k, 1)], slabs[k].reshape(SLAB, D)).astype(BF)
    for copy in copies:
        copy.wait()


def norm_stats(x):
    mean = jnp.mean(x, axis=-1, keepdims=True)
    center = x - mean
    spread = jnp.mean(center * center, axis=-1, keepdims=True)
    inv = lax.rsqrt(spread + NORM_EPS)
    return center * inv, inv


def norm_back(dz, n, inv, gain):
    gz = dz * gain
    m1 = jnp.mean(gz, axis=-1, keepdims=True)
    m2 = jnp.mean(gz * n, axis=-1, keepdims=True)
    return (gz - m1 - n * m2) * inv


def row_chunks(rows, count):
    size = rows // count
    return [(c * size, size) for c in range(count)]


def head_masks():
    lane = lax.broadcasted_iota(jnp.int32, (1, LANES), 1)
    return [(lane >= h * HD) & (lane < (h + 1) * HD) for h in range(HEADS_HERE)]


def stacked(x, masks):
    return jnp.concatenate([jnp.where(m, x, jnp.zeros_like(x)) for m in masks], axis=0)


def unstacked(y, masks):
    total = jnp.where(masks[0], y[:WROW], 0.0)
    for h in range(1, HEADS_HERE):
        total = jnp.where(masks[h], y[h * WROW : (h + 1) * WROW], total)
    return total


def attn_fwd_kernel(nwl, bounds, *refs):
    packs, (upx, recv, vecs) = refs[:TP], refs[TP : TP + 3]
    refs = refs[TP + 3 :]
    qkv, probs, o_out = refs[:TP], refs[TP : 2 * TP], refs[2 * TP : 3 * TP]
    x_out, z1_out, hs_out, z2_out, bias_sc, roll_sc, row_sc, w_sc, small_sc, fm = refs[3 * TP : 3 * TP + 10]
    x_sc, z1_sc, qkv_sc, p_sc, o_sc, sems = refs[3 * TP + 10 :]
    rows = x_out.shape[0]
    smalls, weights, projs = [], [], []
    for s in range(TP):
        lanes = slice(s * LANES, (s + 1) * LANES)
        smalls.append(
            pltpu.make_async_copy(packs[s].at[4 * D :, :], small_sc.at[s], sems.at[8 * s])
        )
        for m in range(3):
            weights.append(
                pltpu.make_async_copy(
                    packs[s].at[m * D : (m + 1) * D, :], w_sc.at[m, :, lanes], sems.at[8 * s + 1 + m]
                )
            )
        for c in range(D // LANES):
            projs.append(
                pltpu.make_async_copy(
                    packs[s].at[3 * D + c * LANES : 3 * D + (c + 1) * LANES, :],
                    w_sc.at[3, lanes, c * LANES : (c + 1) * LANES],
                    sems.at[8 * s + 4 + c],
                )
            )
    for copy in smalls + weights + projs:
        copy.start()
    is_end = jnp.where(bounds[0, 1] == lax.axis_index("rows"), 1.0, 0.0)
    last = jnp.where(lax.axis_index("tp") == TP - 1, 1.0, 0.0)
    g1, b1, g2, b2, bp = (vecs[i : i + 1, :] for i in range(5))

    for copy in smalls:
        copy.wait()
    table = jnp.concatenate(
        [
            jnp.concatenate(
                [small_sc[s, 4 * c : 4 * c + 4, :].astype(F32) for c in range(TABLE_PAD // LANES)],
                axis=1,
            )
            for s in range(TP)
        ],
        axis=0,
    )
    for i in range(TOKENS):
        shift = TABLE_PAD - REACH + SPAN * (i // WIN) + i % WIN
        rolled = pltpu.roll(table, shift, 1)
        roll_sc[i * TP * HEADS_HERE : (i + 1) * TP * HEADS_HERE, :] = rolled[:, : 2 * LANES].astype(BF)
    n16 = TOKENS * TP * HEADS_HERE
    lane = lane_row(LANES)
    at_lane = jnp.where(lane < TOKENS, lane + (SPAN - WIN) * tens(lane), -1000)
    spread = jnp.where(column(2 * LANES) == at_lane, 1.0, 0.0).astype(BF)
    row_sc[:n16, :] = dot(roll_sc[...], spread)
    row_sc[n16:, :] = jnp.zeros((WROW * TP * HEADS_HERE - n16, LANES), F32)
    row = column(WROW)
    real = (row < TOKENS) & (lane < TOKENS)
    low_differ = ((row >= TOKENS // 2) != (lane >= TOKENS // 2)) & real
    right_differ = ((row - WIN * tens(row) >= SHIFT) != (lane - WIN * tens(lane) >= SHIFT)) & real
    extra = jnp.where(lane < TOKENS, 0.0, HIDDEN_KEY) + jnp.where(low_differ, MASKED * is_end, 0.0)
    fm[...] = jnp.where(right_differ, MASKED * last, 0.0)
    for s in range(TP):
        for h in range(HEADS_HERE):
            rows_h = row_sc[pl.ds(s * HEADS_HERE + h, WROW, TP * HEADS_HERE), :]
            bias_sc[s, h * WROW : (h + 1) * WROW, :] = rows_h + extra

    places = window_from(rows, nwl, True, SEG)
    for r0, n in row_chunks(rows, 4):
        x = upx[r0 : r0 + n, :].astype(F32) + dot(onehot(places[r0 : r0 + n, :], STRIP), recv[...])
        x_sc[r0 : r0 + n, :] = x.astype(BF)
        z, _ = norm_stats(x)
        z1_sc[r0 : r0 + n, :] = (z * g1 + b1).astype(BF)
    outgoing = loads([x_sc, z1_sc], [x_out, z1_out], sems, 8 * TP)
    scale = HD ** (-0.5)
    for copy in weights:
        copy.wait()
    for m in range(3):
        for r0, n in row_chunks(rows, 2):
            y = dot(z1_sc[r0 : r0 + n, :], w_sc[m])
            for s in range(TP):
                part = y[:, s * LANES : (s + 1) * LANES]
                if m == 0:
                    part = (part + small_sc[s, 12:13, :].astype(F32)) * scale
                if m == 2:
                    part = part + small_sc[s, 13:14, :].astype(F32)
                qkv_sc[s, m, r0 : r0 + n, :] = part.astype(BF)
    outgoing += loads([qkv_sc.at[s] for s in range(TP)], qkv, sems, 8 * TP + 2)
    for s in range(TP):
        o_sc[s, nwl * WROW :, :] = jnp.zeros((rows - nwl * WROW, LANES), BF)

    def window(j, carry):
        masks = head_masks()
        base = pl.multiple_of(j * WROW, 16)
        flag = jnp.where(j == nwl - 1, 1.0, 0.0)
        fm4 = jnp.concatenate([fm[...] * flag] * HEADS_HERE, axis=0)
        for s in range(TP):
            q = qkv_sc[s, 0, pl.ds(base, WROW), :]
            k = qkv_sc[s, 1, pl.ds(base, LANES), :]
            v = qkv_sc[s, 2, pl.ds(base, LANES), :]
            sco = dot_nt(stacked(q, masks), k) + bias_sc[s] + fm4
            top = jnp.max(sco, axis=-1, keepdims=True)
            e = jnp.exp(sco - top)
            total = jnp.sum(e, axis=-1, keepdims=True)
            p = (e / total).astype(BF)
            p_sc[s, j] = p
            o = unstacked(dot(p, v), masks)
            o_sc[s, pl.ds(base, WROW), :] = o.astype(BF)
        return carry

    lax.fori_loop(0, nwl, window, 0, unroll=UNROLL_F)
    outgoing += loads([p_sc.at[s] for s in range(TP)], probs, sems, 8 * TP + 6)
    outgoing += loads([o_sc.at[s] for s in range(TP)], o_out, sems, 8 * TP + 10)
    for copy in projs:
        copy.wait()
    for r0, n in row_chunks(rows, 2):
        o = jnp.concatenate([o_sc[s, r0 : r0 + n, :] for s in range(TP)], axis=1)
        acc = x_sc[r0 : r0 + n, :].astype(F32) + bp + dot(o, w_sc[3])
        hs_out[r0 : r0 + n, :] = acc
        z, _ = norm_stats(acc)
        z2_out[r0 : r0 + n, :] = (z * g2 + b2).astype(BF)
    for copy in outgoing:
        copy.wait()


def bits_in_order(blocks, down):
    bits = [1 << k for k in range(blocks.bit_length() - 1)]
    return bits[1::-1] + bits[2:] if down else bits


def my_block(blocks, down=False):
    w = lax.axis_index("rows")
    mine = 0
    for bit in bits_in_order(blocks, down):
        mine = mine * 2 + lax.rem(lax.div(w, bit), 2)
    return mine


def store_blocks(out, r0, value, blocks, cols=None, down=False):
    size = value.shape[0] // blocks
    mine = my_block(blocks, down)
    for b in range(blocks):
        at = pl.multiple_of(r0 + jnp.bitwise_xor(mine, b) * size, size)
        part = value[b * size : (b + 1) * size, :]
        if cols is None:
            out[pl.ds(at, size), :] = part
        else:
            out[pl.ds(at, size), cols[0] : cols[1]] = part


def mlp_kernel(ns, first, last, nwl, blocks, *refs):
    refs = list(refs)
    packs = refs[:ns]
    if first:
        held, sems = refs[-2:]
        copies = loads(packs[:1], [held], sems)
        packs, refs = [held] + packs[1:], refs[:-2]
    z2 = refs[ns]
    refs = refs[ns + 1 :]
    if first:
        gup, grecv = refs[:2]
        refs = refs[2:]
    else:
        gs, y_in, z_in = refs[:3]
        refs = refs[3:]
    if last:
        hs, vecs = refs[:2]
        refs = refs[2:]
    grads, dub = refs[:ns], refs[ns]
    refs = refs[ns + 1 :]
    if first:
        gs = refs.pop(0)
    if last:
        out_up, out_low, dh_out, dhb_out, vec_out = refs[:5]
        refs = refs[5:]
    acc_y, acc_z, act_sc, du_sc = refs
    rows = z2.shape[0]
    if first:
        places = window_from(rows, nwl, True, SEG)
        for r0, n in row_chunks(rows, 4):
            gs[r0 : r0 + n, :] = (
                gup[r0 : r0 + n, :].astype(F32)
                + dot(onehot(places[r0 : r0 + n, :], STRIP), grecv[...])
            ).astype(BF)
    for k in range(ns):
        if first and k == 0:
            copies[k].wait()
        ub = packs[k][2 * D : 2 * D + 1, :].astype(F32)
        dub_total = jnp.zeros((1, D), F32)
        for r0, n in row_chunks(rows, 2):
            sl = slice(r0, r0 + n)
            u = dot(z2[sl, :], packs[k][:D, :]) + ub
            phi = 0.5 * (1.0 + lax.erf(u * np.float32(np.sqrt(0.5))))
            act = (u * phi).astype(BF)
            slope = phi + u * (jnp.exp(-0.5 * u * u) * np.float32(1 / np.sqrt(2 * np.pi)))
            act_sc[sl, :] = act
            ga = dot_nt(gs[sl, :], packs[k][D : 2 * D, :])
            du = (slope * ga).astype(BF)
            du_sc[sl, :] = du
            dub_total += jnp.sum(du.astype(F32), axis=0, keepdims=True)
            y = dot(act, packs[k][D : 2 * D, :])
            z = dot_nt(du, packs[k][:D, :])
            if k > 0:
                acc_y[sl, :] += y
                acc_z[sl, :] += z
            elif first:
                acc_y[sl, :] = y
                acc_z[sl, :] = z
            else:
                acc_y[sl, :] = y + y_in[sl, :]
                acc_z[sl, :] = z + z_in[sl, :]
        for c in range(D // LANES):
            line = k * (D // LANES) + c
            dub[line : line + 1, :] = dub_total[:, c * LANES : (c + 1) * LANES]
        store_blocks(grads[k], 0, dot_tn(act_sc[...], gs[...]).astype(BF), blocks, down=True)
        store_blocks(grads[k], D, dot_tn(z2[...], du_sc[...]).astype(BF), blocks)
    if not last:
        return
    g2, bd = vecs[2:3, :], vecs[5:6, :]
    sums = [jnp.zeros((1, D), F32) for _ in range(4)]
    for r0, n in row_chunks(rows, 4):
        sl = slice(r0, r0 + n)
        dz = acc_z[sl, :]
        g = gs[sl, :].astype(F32)
        h = hs[sl, :]
        nrm, inv = norm_stats(h)
        dh = g + norm_back(dz, nrm, inv, g2)
        dh_out[sl, :] = dh
        dhb_out[sl, :] = dh.astype(BF)
        act_sc[sl, :] = (h + acc_y[sl, :] + bd).astype(BF)
        for i, term in enumerate((dz * nrm, dz, g, dh)):
            sums[i] = sums[i] + jnp.sum(term, axis=0, keepdims=True)
    vec_out[...] = jnp.concatenate(sums, axis=0)
    out_up[...] = pick_rows(strip_from_window(nwl, False), act_sc[...])
    out_low[...] = pick_rows(strip_from_window(nwl, True), act_sc[...])


def loads(sources, targets, sems, at=0):
    copies = [
        pltpu.make_async_copy(x, y, sems.at[at + i]) for i, (x, y) in enumerate(zip(sources, targets))
    ]
    for copy in copies:
        copy.start()
    return copies


def attn_bwd_kernel(ns, nwl, blocks, last, *refs):
    refs = list(refs)

    def take(n):
        found = refs[:n]
        del refs[:n]
        return found

    n_in = 4 * ns + (TP - ns if last else 0)
    sources = take(n_in)
    dhb, z1 = take(2)
    if last:
        tail = take(11)
    grads = take(ns)
    if last:
        tail += take(3)
    dpos, *dx_sc = take(1 + ns)
    if last:
        tail += take(2)
    dsum, do_sc = take(2)
    held = take(n_in)
    (sems,) = refs
    copies = loads(sources, held, sems)
    packs, o, qkv, probs = (held[i * ns : (i + 1) * ns] for i in range(4))
    rows = dhb.shape[0]
    scale = HD ** (-0.5)
    masks = head_masks()
    lin = column(LANES)
    lin = jnp.where(lin < TOKENS, REACH - lin - (SPAN - WIN) * tens(lin), -1000)
    back = onehot(lin, TABLE_PAD)
    place = lane_row(STACK)
    head = sum((place >= WROW * m).astype(jnp.int32) for m in range(1, HEADS_HERE))
    place = place - WROW * head
    line = jnp.where(place < TOKENS, tens(place) * 8 + head, -1000)
    groups = jnp.where(column(WIN * 8) == line, 1.0, 0.0).astype(BF)
    for k in range(ns):
        copies[k].wait()
        total = None
        for c in range(D // LANES):
            w = packs[k][3 * D + c * LANES : 3 * D + (c + 1) * LANES, :]
            term = dot_nt(dhb[:, c * LANES : (c + 1) * LANES], w)
            total = term if total is None else total + term
        do_sc[k] = total.astype(BF)
        copies[ns + k].wait()
        gp = dot_tn(o[k][...], dhb[...]).astype(BF)
        gp = jnp.concatenate([gp[:, c * LANES : (c + 1) * LANES] for c in range(D // LANES)], axis=0)
        store_blocks(grads[k], 0, gp, blocks, (3 * LANES, 4 * LANES))
        dx_sc[k][nwl * WROW :, :] = jnp.zeros((rows - nwl * WROW, 3 * LANES), BF)
        dsum[k] = jnp.zeros(dsum.shape[1:], F32)
        copies[2 * ns + k].wait()
        copies[3 * ns + k].wait()

        def window(j, carry, k=k):
            base = pl.multiple_of(j * WROW, 16)
            q = stacked(qkv[k][0, pl.ds(base, WROW), :], masks)
            key = qkv[k][1, pl.ds(base, LANES), :]
            v = qkv[k][2, pl.ds(base, LANES), :]
            do = stacked(do_sc[k, pl.ds(base, WROW), :], masks)
            p = probs[k][j]
            p32 = p.astype(F32)
            pdp = p32 * dot_nt(do, v)
            ds = (pdp - p32 * jnp.sum(pdp, axis=-1, keepdims=True)).astype(BF)
            dsum[k] += ds.astype(F32)
            dv = dot_tn(p, do)
            dk = dot_tn(ds, q)
            dq = unstacked(dot(ds, key), masks) * scale
            dx_sc[k][pl.ds(base, WROW), :LANES] = dq.astype(BF)
            dx_sc[k][pl.ds(base, WROW), LANES : 2 * LANES] = dk[:WROW].astype(BF)
            dx_sc[k][pl.ds(base, WROW), 2 * LANES :] = dv[:WROW].astype(BF)
            return carry

        lax.fori_loop(0, nwl, window, 0, unroll=UNROLL)
    for k in range(ns):
        store_blocks(grads[k], 0, dot_tn(z1[...], dx_sc[k][...]).astype(BF), blocks, (0, 3 * LANES))
        high = dsum[k].astype(BF)
        low = (dsum[k] - high.astype(F32)).astype(BF)
        lanes = dot(high, back) + dot(low, back)
        turned = jnp.concatenate(
            [
                pltpu.roll(lanes[h * WROW : (h + 1) * WROW, :], 0, 1, stride=1, stride_axis=0)
                for h in range(HEADS_HERE)
            ],
            axis=0,
        )
        high = turned.astype(BF)
        low = (turned - high.astype(F32)).astype(BF)
        summed = dot(groups, high) + dot(groups, low)
        total = summed[:8, :]
        for a in range(1, WIN):
            total = total + pltpu.roll(summed[a * 8 : (a + 1) * 8, :], (SPAN - WIN) * a, 1)
        per = 16
        for h in range(HEADS_HERE):
            for c in range(TABLE_PAD // LANES):
                line = k * per + h * (TABLE_PAD // LANES) + c
                dpos[line : line + 1, :] = total[h : h + 1, c * LANES : (c + 1) * LANES]
        for i, m in enumerate((0, 2)):
            part = dx_sc[k][:, m * LANES : (m + 1) * LANES].astype(F32)
            line = k * per + 12 + i
            dpos[line : line + 1, :] = jnp.sum(part, axis=0, keepdims=True)
        dpos[k * per + 14 : (k + 1) * per, :] = jnp.zeros((2, LANES), F32)
    if last:
        for copy in copies[4 * ns :]:
            copy.wait()
        end_of_backward(nwl, dx_sc, packs + held[4 * ns :], dpos, *tail)


def end_of_backward(nwl, dxs, packs, small01, *refs):
    dx2, dx3, x_ref, dh, vecs, vec_mlp, small3, small2, dub01, dub2, dub3 = refs[:11]
    out_up, out_low, small_out, small_f32, dz = refs[11:]
    rows = x_ref.shape[0]
    parts = list(zip(dxs + [dx2, dx3], packs))
    weights = [
        jnp.concatenate([pack[m * D : (m + 1) * D, :] for m in range(3)], axis=1) for _, pack in parts
    ]
    sums = [jnp.zeros((1, D), F32) for _ in range(2)]
    for r0, n in row_chunks(rows, 2):
        sl = slice(r0, r0 + n)
        total = None
        for (dx, _), weight in zip(parts, weights):
            term = dot_nt(dx[sl, :], weight)
            total = term if total is None else total + term
        nrm, inv = norm_stats(x_ref[sl, :].astype(F32))
        dz[sl, :] = (dh[sl, :] + norm_back(total, nrm, inv, vecs[0:1, :])).astype(BF)
        sums[0] = sums[0] + jnp.sum(total * nrm, axis=0, keepdims=True)
        sums[1] = sums[1] + jnp.sum(total, axis=0, keepdims=True)
    t = lax.axis_index("tp")
    pieces = [
        (small01[:16, :], dub01[:4, :]),
        (small01[16:, :], dub01[4:, :]),
        (small2[...], dub2[...]),
        (small3[...], dub3[...]),
    ]
    for s, (lines, dub) in enumerate(pieces):
        at = pl.multiple_of(jnp.bitwise_xor(t, s) * LANES, LANES)
        both = jnp.concatenate([lines, dub, jnp.zeros((4, LANES), F32)], axis=0)
        small_f32[: SMALL_SHARD, pl.ds(at, LANES)] = both
    small_f32[SMALL_SHARD:, :] = jnp.concatenate(
        [vec_mlp[...]] + sums + [jnp.zeros((SMALL_ROWS - SMALL_SHARD - 6, D), F32)], axis=0
    )
    small_out[...] = small_f32[...].astype(BF)
    out_up[...] = pick_rows(strip_from_window(nwl, False), dz[...])
    out_low[...] = pick_rows(strip_from_window(nwl, True), dz[...])


def page_kernel(*refs):
    out = refs[TP]
    pw = out.shape[1]
    t = lax.axis_index("tp")
    width = pw // TP
    col = lax.broadcasted_iota(jnp.int32, (pw, 1), 0)
    hots = []
    for s in range(TP):
        v = col - width * jnp.bitwise_xor(t, s) - SHIFT
        v = jnp.where(v < 0, v + pw, v)
        v = jnp.where(v < width, v, -1000)
        hots.append(onehot(v, SEG))
    hot = jnp.concatenate(hots, axis=1)
    for r in range(WIN):
        off = STRIP + r * SEG if r < SHIFT else (r - SHIFT) * SEG
        parts = [ul[off : off + SEG, :] for ul in refs[:TP]]
        out[r] = dot(hot, jnp.concatenate(parts, axis=0)).astype(BF)


def swap_tp(x, bit):
    return lax.ppermute(x, "tp", [(i, i ^ bit) for i in range(TP)])


def swap_rows(x, bit):
    return lax.ppermute(x, "rows", [(i, i ^ bit) for i in range(lax.axis_size("rows"))])


def shift_rows(x, distance):
    n = lax.axis_size("rows")
    return lax.ppermute(x, "rows", [(i, (i + distance) % n) for i in range(n)])


def row_bits():
    n = lax.axis_size("rows")
    bits = []
    while 1 << len(bits) < n:
        bits.append(1 << len(bits))
    return bits


def blocks_for(rows):
    blocks = 1
    while 2 * blocks <= lax.axis_size("rows") and rows % (2 * blocks) == 0 and rows // (2 * blocks) >= 16:
        blocks *= 2
    return blocks


def added(arrays):
    total = arrays[0].astype(F32)
    for extra in arrays[1:]:
        total = total + extra.astype(F32)
    return total.astype(BF)


def scatter_step(arrays, bit, blocks):
    total = added(arrays)
    if bit < blocks:
        half = total.shape[0] // 2
        return [total[:half], swap_rows(total[half:], bit)]
    return [total, swap_rows(total, bit)]


def finish_kernel(blocks, gathered, n_in, *refs):
    ins, outs = refs[:n_in], refs[n_in:]
    part = ins[0].shape[0] * n_in // blocks
    each = blocks // n_in
    both = len(outs) == 2
    half = part // 2

    def place(p, down):
        order = bits_in_order(blocks, down)
        moved = sum(
            ((p >> k) & 1) << (len(order) - 1 - order.index(bit)) for k, bit in enumerate(gathered)
        )
        return jnp.bitwise_xor(my_block(blocks, down), moved)

    for p in range(blocks):
        piece = ins[p // each][(p % each) * part : (p % each + 1) * part, :].astype(F32)
        if both:
            for out, value, down in zip(outs, (piece[:half], piece[half:]), (True, False)):
                out[pl.ds(pl.multiple_of(place(p, down) * half, half), half), :] = value
        else:
            outs[2][pl.ds(pl.multiple_of(place(p, False) * part, part), part), :] = piece
    if both:
        return
    qkv, proj, whole = outs
    for c in range(D // LANES):
        if c < 3:
            qkv[c] = whole[:, c * LANES : (c + 1) * LANES]
        proj[:, c * LANES : (c + 1) * LANES] = whole[c * LANES : (c + 1) * LANES, 3 * LANES :]


def finish(pieces, blocks, gathered, name):
    attn = name == "finish_attn"
    return call(
        functools.partial(finish_kernel, blocks, gathered, len(pieces)),
        pieces,
        [((3, D, LANES), F32), ((LANES, D), F32)] if attn else [((D, D), F32)] * 2,
        scratch=[pltpu.VMEM((D, D), F32)] if attn else [],
        name=name,
    )


def interleaved(parts, blocks):
    n = blocks
    cut = [p.reshape(n, 1, p.shape[0] // n, p.shape[1]) for p in parts]
    return jnp.concatenate(cut, axis=1).reshape(-1, parts[0].shape[1])


def riding_step(arrays, small, bit, blocks):
    total = added(arrays)
    small = added(small)
    half = total.shape[0] // 2 if bit < blocks else total.shape[0]
    got = swap_rows(jnp.concatenate([total[-half:], small], axis=0), bit)
    return [total[:half], got[:half]], [small, got[half:]]


def small_kernel(*refs):
    ins, outs = refs[:TP], refs[TP:]
    total = ins[0][2 * STRIP :, :].astype(F32)
    for r in ins[1:]:
        total += r[2 * STRIP :, :].astype(F32)
    for i in range(6):
        outs[i][...] = total[SMALL_SHARD + i : SMALL_SHARD + i + 1, :]
    t = lax.axis_index("tp")
    mine = jnp.zeros((SMALL_SHARD, LANES), F32)
    for a in range(TP):
        mine = jnp.where(t == a, total[:SMALL_SHARD, a * LANES : (a + 1) * LANES], mine)
    qvb, up, table = outs[6:]
    qvb[...] = mine[12:14, :]
    up[...] = mine[16:20, :]
    per = TABLE_PAD // LANES
    for h in range(HEADS_HERE):
        line = jnp.concatenate([mine[h * per + c : h * per + c + 1, :] for c in range(per)], axis=1)
        table[h : h + 1, :] = line[:, :TABLE]


def page(pieces, page_shape, name):
    return call(page_kernel, pieces, [(page_shape, BF)], name=name)[0]


def per_device(
    patches,
    cotangent,
    page_bounds,
    attn_gain,
    attn_shift,
    qkv_weight,
    qv_bias,
    pos_table,
    proj_weight,
    proj_bias,
    mlp_gain,
    mlp_shift,
    up_weight,
    up_bias,
    down_weight,
    down_bias,
):
    t = lax.axis_index("tp")
    pw = patches.shape[1]
    nwl = pw // WIN // TP
    width = nwl * WIN
    rows = rows_of(nwl)
    bits = row_bits()
    blocks = blocks_for(D)

    vecs = jnp.stack([attn_gain, attn_shift, mlp_gain, mlp_shift, proj_bias, down_bias]).astype(F32)
    slab = (SHIFT, NBLK * COLBLK, D)
    strip_x, pack1 = call(
        functools.partial(head_kernel, width),
        [patches, qkv_weight.reshape(3 * D, LANES), proj_weight, pos_table.T, qv_bias],
        [((STRIP, D), BF), ((PACK1, LANES), BF)],
        scratch=[
            pltpu.VMEM(slab, BF),
            pltpu.SemaphoreType.DMA((7,)),
        ],
        hbm=3,
        name="head",
    )
    recv_x = shift_rows(strip_x, -1)
    pack1_x = swap_tp(pack1, 2)
    pack1_c = swap_tp(pack1, 1)
    strip_g, up_x, up_g, pack2 = call(
        functools.partial(rest_kernel, width),
        [patches, after(cotangent, strip_x, vecs), up_weight, down_weight, up_bias[None]],
        [((STRIP, D), BF), ((rows, D), BF), ((rows, D), BF), ((PACK2, D), BF)],
        scratch=[
            pltpu.VMEM((3,) + slab, BF),
            pltpu.SemaphoreType.DMA((8,)),
        ],
        hbm=4,
        name="rest",
    )
    recv_g = shift_rows(strip_g, -1)
    pack1_cx = swap_tp(after(pack1_x, strip_g, recv_x, pack1_c), 1)
    packs1 = [pack1, pack1_c, pack1_x, pack1_cx]
    pack2_x = swap_tp(after(pack2, pack1_x), 2)
    pack2_c = swap_tp(pack2, 1)

    outs = call(
        functools.partial(attn_fwd_kernel, nwl),
        packs1 + [up_x, recv_x, vecs],
        [((3, rows, LANES), BF)] * TP
        + [((nwl, STACK, LANES), BF)] * TP
        + [((rows, LANES), BF)] * TP
        + [((rows, D), BF), ((rows, D), BF), ((rows, D), F32), ((rows, D), BF)],
        scratch=[
            pltpu.VMEM((TP, STACK, LANES), F32),
            pltpu.VMEM((TOKENS * TP * HEADS_HERE, 2 * LANES), BF),
            pltpu.VMEM((WROW * TP * HEADS_HERE, LANES), F32),
            pltpu.VMEM((4, D, D), BF),
            pltpu.VMEM((TP, PACK1 - 4 * D, LANES), BF),
            pltpu.VMEM((WROW, LANES), F32),
            pltpu.VMEM((rows, D), BF),
            pltpu.VMEM((rows, D), BF),
            pltpu.VMEM((TP, 3, rows, LANES), BF),
            pltpu.VMEM((TP, nwl, STACK, LANES), BF),
            pltpu.VMEM((TP, rows, LANES), BF),
            pltpu.SemaphoreType.DMA((8 * TP + 2 + 3 * TP,)),
        ],
        scalars=[page_bounds],
        hbm=TP,
        hbm_out=3 * TP + 2,
        pin=False,
        name="attn_fwd",
    )
    qkv, probs, o = outs[:TP], outs[TP : 2 * TP], outs[2 * TP : 3 * TP]
    x_win, z1, hs, z2 = outs[3 * TP :]

    def mlp(packs, extra, first, last):
        ns = len(packs)
        outs = [((2 * D, D), BF)] * ns + [((ns * D // LANES, LANES), F32)]
        if first:
            outs += [((rows, D), BF)]
        if last:
            outs += [((STRIP, D), BF)] * 2 + [((rows, D), F32), ((rows, D), BF), ((4, D), F32)]
        accs = [((rows, D), F32)] * 2
        return call(
            functools.partial(mlp_kernel, ns, first, last, nwl, blocks),
            packs + [z2] + extra,
            outs if last else outs + accs,
            scratch=([pltpu.VMEM(*a) for a in accs] if last else [])
            + [pltpu.VMEM((rows, D), BF)] * 2
            + ([pltpu.VMEM((PACK2, D), BF), pltpu.SemaphoreType.DMA((1,))] if first else []),
            hbm=1 if first else 0,
            name="mlp_last" if last else "mlp_first" if first else "mlp_mid",
        )

    g0, g1, dub01, gs, acc_y, acc_z = mlp([pack2, pack2_c], [up_g, recv_g], True, False)
    got_g1 = swap_tp(g1, 1)
    pack2_cx = swap_tp(after(pack2_x, acc_y), 1)
    g2, dub2, acc_y, acc_z = mlp([pack2_x], [gs, acc_y, acc_z], False, False)
    g3, dub3, up_y, low_y, dh, dhb, vec_mlp = mlp(
        [pack2_cx],
        [gs, acc_y, acc_z, hs, vecs],
        False,
        True,
    )
    got_g3 = swap_tp(g3, 1)
    lower_y = shift_rows(low_y, 1)

    def attn_bwd(shards, dhb, tail=()):
        ns = len(shards)
        loaded = [a[s] for a in (packs1, o, qkv, probs) for s in shards]
        outs = [((D, D), BF)] * ns
        parts = [((ns * 16, LANES), F32)] + [((rows, 3 * LANES), BF)] * ns
        scratch = []
        if tail:
            loaded += [packs1[s] for s in range(TP) if s not in shards]
            outs += [((STRIP, D), BF)] * 2 + [((SMALL_ROWS, D), BF)]
            scratch = [pltpu.VMEM(*p) for p in parts]
            scratch += [pltpu.VMEM((SMALL_ROWS, D), F32), pltpu.VMEM((rows, D), BF)]
        else:
            outs += parts
        return call(
            functools.partial(attn_bwd_kernel, ns, nwl, blocks, bool(tail)),
            loaded + [dhb, z1, *tail],
            outs,
            scratch=scratch
            + [pltpu.VMEM((ns, STACK, LANES), F32), pltpu.VMEM((ns, rows, LANES), BF)]
            + [pltpu.VMEM(a.shape, a.dtype) for a in loaded]
            + [pltpu.SemaphoreType.DMA((len(loaded),))],
            hbm=len(loaded),
            name="attn_bwd_" + "".join(map(str, shards)),
        )

    a3, small3, dx3 = attn_bwd((3,), dhb)
    got_a3 = swap_tp(a3, 1)
    across_d = added([g2[:D], after(got_g3, a3)[:D]])
    got_dx = swap_tp(across_d, 2)
    up0 = added([after(g0, across_d)[D:], got_g1[D:]])
    up2 = added([g2[D:], got_g3[D:]])
    half = D // 2
    up_got = swap_rows(jnp.concatenate([up0[half:], up2[half:]], axis=0), bits[0])
    a2, small2, dx2 = attn_bwd((2,), after(dhb, across_d, up0, up2))
    across_a = added([a2, got_a3])
    got_ax = swap_tp(across_a, 2)
    a0, a1, up_g, low_g, small = attn_bwd(
        (0, 1),
        after(dhb, across_a),
        (dx2, dx3, x_win, dh, vecs, vec_mlp, small3, small2, dub01, dub2, dub3),
    )
    got_a1 = swap_tp(a1, 1)
    page_own = jnp.concatenate([after(up_y, a2), lower_y], axis=0)
    from_c = swap_tp(page_own, 1)

    up_got = after(up_got, a0)
    up0 = added([up0[:half], up_got[:half]])
    up2 = added([up2[:half], up_got[half:]])
    up_x = swap_tp(up2, 2)
    down = scatter_step([after(g0, up2)[:D], after(got_g1, up2)[:D], got_dx], bits[1], blocks)

    attn = [after(a0, up2, down[0]), got_a1, got_ax]
    small = [small]
    mlp = None
    gather_a = [b for b in reversed(bits) if b < blocks]
    gather_m = gather_a[:-2] + gather_a[:-3:-1]
    steps = len(bits) + len(gather_a)
    for i in range(steps):
        if i < len(bits):
            mark = added(attn)
            attn, small = riding_step([mark], small, bits[i], blocks)
        else:
            mark = added(attn) if i == len(bits) else jnp.concatenate(attn, axis=0)
            attn = [mark, swap_rows(mark, gather_a[i - len(bits)])]
        if i == 0:
            lower_g = shift_rows(after(low_g, mark), 1)
            down = scatter_step([after(down[0], mark), down[1]], bits[0], blocks)
            up = scatter_step([after(up0, mark), up_x], bits[1], blocks)
            from_x = swap_tp(after(page_own, mark), 2)
        elif i + 1 < steps:
            if i == 1:
                mlp = [added([after(down[0], mark), down[1]]), added([after(up[0], mark), up[1]])]
                mlp = scatter_step([interleaved(mlp, blocks // 4)], bits[2], blocks)
            elif i + 1 < len(bits):
                mlp = scatter_step([after(mlp[0], mark), mlp[1]], bits[i + 1], blocks)
            else:
                kept = after(mlp[0], mark)
                first = i + 1 == len(bits)
                total = added([kept, mlp[1]]) if first else jnp.concatenate([kept, mlp[1]], axis=0)
                mlp = [total, swap_rows(total, gather_m[i + 1 - len(bits)])]
        if i == len(bits):
            small = added([after(small[0], mark), small[1]])
            own_g = jnp.concatenate([up_g, lower_g, small], axis=0)
            g_x = swap_tp(own_g, 2)
            g_c = swap_tp(own_g, 1)
            from_cx = swap_tp(after(from_x, mark), 1)
    g_cx = swap_tp(after(g_x, mark), 1)
    block_out = page([after(page_own, mark), from_c, from_x, from_cx], patches.shape, "page_y")
    grad_patches = page([after(own_g, mark), g_c, g_x, g_cx], patches.shape, "page_g")
    *v, qvb_line, up_line, table = call(
        small_kernel,
        [own_g, g_c, g_x, g_cx],
        [((1, D), F32)] * 6 + [((2, LANES), F32), ((D // LANES, LANES), F32), ((HEADS_HERE, TABLE), F32)],
        name="small",
    )
    attn[0] = after(attn[0], block_out, grad_patches, table)
    grad_qkv, grad_proj = finish(attn, blocks, gather_a, "finish_attn")
    grad_down, grad_up = finish([after(mlp[0], grad_qkv), mlp[1]], blocks, gather_m, "finish_mlp")

    v = [line.reshape(D) for line in v]

    return (
        block_out,
        grad_patches,
        v[4],
        v[5],
        grad_qkv,
        qvb_line,
        table.T,
        grad_proj,
        v[3],
        v[0],
        v[1],
        grad_up,
        up_line.reshape(D),
        grad_down,
        v[2],
    )


def solution(mesh):
    placed = (
        P("rows", None, None),
        P("rows", None, None),
        P("rows", None),
        P(),
        P(),
        P(None, None, "tp"),
        P(None, "tp"),
        P(None, "tp"),
        P("tp", None),
        P(),
        P(),
        P(),
        P(None, "tp"),
        P("tp"),
        P("tp", None),
        P(),
    )
    return jax.shard_map(
        per_device,
        mesh=mesh,
        in_specs=placed,
        out_specs=(
            P("rows", None, None),
            P("rows", None, None),
            P(),
            P(),
            P(None, None, "tp"),
            P(None, "tp"),
            P(None, "tp"),
            P("tp", None),
            P(),
            P(),
            P(),
            P(None, "tp"),
            P("tp"),
            P("tp", None),
            P(),
        ),
        check_vma=False,
    )
```
